32 devices in a mesh: rep: 2 (over x), shard: 16 (over z, y, core).
Axes of the slice: x: 2, y: 2, z: 4, core: 2. Of those that a mesh axis runs over, the one named last changes fastest.
Arguments:
- tokens: bfloat16 [32, 1024, 1024], P(('rep', 'shard')), may hold values from -6 to 6
- enc_states: bfloat16 [32, 1024, 1024], P(('rep', 'shard')), may hold values from -6 to 6
- unit_ids: int32 [32, 1024], P(('rep', 'shard')), may hold values from 0 to 7, as said below
- enc_ids: int32 [32, 1024], P(('rep', 'shard')), may hold values from 0 to 7, as said below
- self_q: bfloat16 [1024, 1024], P('shard'), may hold values from -0.25 to 0.25
- self_k: bfloat16 [1024, 1024], P('shard'), may hold values from -0.25 to 0.25
- self_v: bfloat16 [1024, 1024], P('shard'), may hold values from -0.1875 to 0.1875
- self_o: bfloat16 [1024, 1024], P('shard'), may hold values from -0.75 to 0.75
- cross_q: bfloat16 [1024, 1024], P('shard'), may hold values from -0.25 to 0.25
- cross_k: bfloat16 [1024, 1024], P('shard'), may hold values from -0.25 to 0.25
- cross_v: bfloat16 [1024, 1024], P('shard'), may hold values from -0.1875 to 0.1875
- cross_o: bfloat16 [1024, 1024], P('shard'), may hold values from -0.75 to 0.75
- ffn_in: bfloat16 [1024, 4096], P('shard'), may hold values from -0.1875 to 0.1875
- ffn_out: bfloat16 [4096, 1024], P('shard'), may hold values from -0.125 to 0.125
- norm_gains: bfloat16 [4, 1024], P(None, 'shard'), may hold values from 0.25 to 1.75
- norm_biases: bfloat16 [4, 1024], P(None, 'shard'), may hold values from -1.5 to 1.5
- cotangent: bfloat16 [32, 1024, 1024], P(('rep', 'shard')), may hold values from -6 to 6
Outputs:
- layer_out: bfloat16 [32, 1024, 1024], P(('rep', 'shard'))
- grad_tokens: float32 [32, 1024, 1024], P(('rep', 'shard'))
- grad_enc_states: float32 [32, 1024, 1024], P(('rep', 'shard'))
- grad_self_q: float32 [1024, 1024], P('shard')
- grad_self_k: float32 [1024, 1024], P('shard')
- grad_self_v: float32 [1024, 1024], P('shard')
- grad_self_o: float32 [1024, 1024], P('shard')
- grad_cross_q: float32 [1024, 1024], P('shard')
- grad_cross_k: float32 [1024, 1024], P('shard')
- grad_cross_v: float32 [1024, 1024], P('shard')
- grad_cross_o: float32 [1024, 1024], P('shard')
- grad_ffn_in: float32 [1024, 4096], P('shard')
- grad_ffn_out: float32 [4096, 1024], P('shard')
- grad_norm_gains: float32 [4, 1024], P(None, 'shard')
- grad_norm_biases: float32 [4, 1024], P(None, 'shard')
The draws below stay inside these ranges and needn't reach their ends.
Inputs may be any that keep to these rules, and one draw needn't show every extreme that they name: `unit_ids`: within each sequence the document number never falls from one unit to the next, and every number 0 to 7 labels one or more units; document lengths are uneven. `enc_ids`: within each sequence the document number never falls from one encoder state to the next, and every number 0 to 7 labels one or more encoder states, so each unit's document has encoder states in the same sequence.
All inputs are finite; a program needn't handle non-finite values.
Results may differ from the reference program's by a relative error of at most 0.025.
The reference program's roundings to bfloat16 on the way count: a program that leaves them out, or rounds other values in their place, can miss the bound.
Values may be sent and summed in bfloat16 or wider, within the bound.
No kernel may reach another device: no remote copies, remote signals or barrier semaphores. Data moves between devices by JAX's collectives and lax.ppermute only.
A program may use at most 512 MiB of HBM per device.

```python
import math
import jax
import jax.numpy as jnp
from jax import lax

D = 1024
HEADS = 16
HEAD = 64
FF = 4096
LEN = 1024
ENC = 1024
DOCS = 8
SEQUENCES = 32


def document_ids(key, total):
    powers = jax.random.randint(key, (SEQUENCES, DOCS), 0, 7)
    doc_weights = jnp.left_shift(jnp.ones_like(powers), powers)
    spare_units = total - DOCS
    extra_units = doc_weights * spare_units // jnp.sum(doc_weights, axis=1, keepdims=True)
    lengths = 1 + extra_units
    missing = total - jnp.sum(lengths, axis=1)
    lengths = lengths.at[:, DOCS - 1].add(missing)
    doc_ends = jnp.cumsum(lengths, axis=1)
    places = jnp.arange(total, dtype=jnp.int32)
    return jnp.sum((places[None, :, None] >= doc_ends[:, None, :]).astype(jnp.int32), axis=2).astype(jnp.int32)


def draw_unit_ids(key, part):
    return document_ids(jax.random.fold_in(key, 11), LEN)


def draw_enc_ids(key, part):
    return document_ids(jax.random.fold_in(key, 13), ENC)


def steps_of(own_key, extent, cuts, low, high):
    level = 1.0
    for axis_at, shards_of in cuts:
        heights = jax.random.uniform(jax.random.fold_in(jax.random.fold_in(own_key, 6), axis_at), (shards_of,), jnp.float32, low / len(cuts), high / len(cuts))
        level = level * jnp.repeat(jnp.exp(heights), extent[axis_at] // shards_of).reshape((-1,) + (1,) * (len(extent) - 1 - axis_at))
    return level


def scatter_about(own_key, shape, scale, limit, shards=(), kind=jnp.bfloat16):
    result = jax.random.normal(own_key, shape, jnp.float32) * scale
    if len(shards) > 0:
        result = steps_of(own_key, shape, shards, -0.22, 0.18) * result
    return jnp.clip(result, min=-limit, max=limit).astype(kind)


def setup_inputs(seed: int = 0) -> dict:
    splits = jax.random.split(jax.random.key(seed), 18)
    return {
        "tokens": scatter_about(splits[0], (SEQUENCES, LEN, D), 1.0, 6.0, ((0, 32),)),
        "enc_states": scatter_about(splits[1], (SEQUENCES, ENC, D), 1.0, 6.0, ((0, 32),)),
        "unit_ids": draw_unit_ids(jax.random.fold_in(splits[17], 71), 0),
        "enc_ids": draw_enc_ids(jax.random.fold_in(splits[17], 71), 0),
        "self_q": scatter_about(splits[4], (D, D), (D // 2) ** -0.5, 0.25, ((0, 16),)),
        "self_k": scatter_about(splits[5], (D, D), (D // 2) ** -0.5, 0.25, ((0, 16),)),
        "self_v": scatter_about(splits[6], (D, D), D ** -0.5, 0.1875, ((0, 16),)),
        "self_o": scatter_about(splits[7], (D, D), (D // 16) ** -0.5, 0.75, ((0, 16),)),
        "cross_q": scatter_about(splits[8], (D, D), (D // 2) ** -0.5, 0.25, ((0, 16),)),
        "cross_k": scatter_about(splits[9], (D, D), (D // 2) ** -0.5, 0.25, ((0, 16),)),
        "cross_v": scatter_about(splits[10], (D, D), D ** -0.5, 0.1875, ((0, 16),)),
        "cross_o": scatter_about(splits[11], (D, D), (D // 16) ** -0.5, 0.75, ((0, 16),)),
        "ffn_in": scatter_about(splits[12], (D, FF), D ** -0.5, 0.1875, ((0, 16),)),
        "ffn_out": scatter_about(splits[13], (FF, D), (FF // 2) ** -0.5, 0.125, ((0, 16),)),
        "norm_gains": jnp.clip(1.0 + 0.15 * jax.random.normal(splits[14], (4, D), jnp.float32), 0.25, 1.75).astype(jnp.bfloat16),
        "norm_biases": scatter_about(splits[15], (4, D), 0.3, 1.5, ((1, 16),)),
        "cotangent": scatter_about(splits[16], (SEQUENCES, LEN, D), 1.0, 6.0, ((0, 32),)),
    }


@jax.custom_vjp
def low(v):
    return lax.optimization_barrier(v.astype(jnp.bfloat16)).astype(jnp.float32)

@jax.custom_vjp
def low_back(v):
    return v

def low_keep(v):
    return (low(v), None)

def low_pass(kept, grad):
    return (grad,)

def back_keep(v):
    return (v, None)

def back_low(kept, grad):
    return (low(grad),)
low.defvjp(low_keep, low_pass)
low_back.defvjp(back_keep, back_low)
highest = lax.Precision.HIGHEST
eps_norm = 1e-05
big_negative = -1e+30

def matmul(left, right):
    return jnp.dot(left, right, precision=highest)

def layer_norm(values_in, gain_row, bias_row):
    centre = values_in - lax.optimization_barrier(jnp.mean(values_in, axis=-1, keepdims=True))
    spread = lax.optimization_barrier(jnp.mean(centre * centre, axis=-1, keepdims=True))
    return centre * lax.rsqrt(spread + eps_norm) * gain_row + bias_row

def attention(queries, key_rows, value_rows, query_ids, key_ids, causal):
    row_count = queries.shape[0]
    key_count = key_rows.shape[0]
    block_rows = min(512, row_count)
    score_scale = 1.0 / math.sqrt(HEAD)
    heads_k = key_rows.reshape(key_count, HEADS, HEAD)
    heads_v = value_rows.reshape(key_count, HEADS, HEAD)
    key_place = jnp.arange(key_count)

    def one_block(block_index):
        first_row = (block_index * block_rows).astype(jnp.int32)
        query_part = lax.dynamic_slice_in_dim(queries, first_row, block_rows, 0).reshape(block_rows, HEADS, HEAD)
        part_ids = lax.dynamic_slice_in_dim(query_ids, first_row, block_rows, 0)
        raw_scores = low_back(jnp.einsum('qhe,khe->hqk', query_part, heads_k, precision=highest))
        allowed = part_ids[:, None] == key_ids[None, :]
        if causal:
            allowed = allowed & ((first_row + jnp.arange(block_rows))[:, None] >= key_place[None, :])
        scores = jnp.where(allowed[None], raw_scores * score_scale, big_negative)
        soft_probs = low(jax.nn.softmax(scores, axis=-1))
        attended = jnp.einsum('hqk,khe->qhe', soft_probs, heads_v, precision=highest)
        return attended.reshape(block_rows, HEADS * HEAD)
    blocks = lax.map(jax.checkpoint(one_block), jnp.arange(row_count // block_rows).astype(jnp.int32))
    return blocks.reshape(row_count, HEADS * HEAD)

def layer(tokens, enc_rows, weights, gain_rows, biases, unit_row, enc_row):
    self_q, self_k, self_v, self_o, cross_q, cross_k, cross_v, cross_o, ffn_in, ffn_out = weights
    normed = low(layer_norm(tokens, gain_rows[0], biases[0]))
    queries = low(low_back(matmul(normed, self_q)))
    key_rows = low(low_back(matmul(normed, self_k)))
    value_rows = low(low_back(matmul(normed, self_v)))
    attended = low(low_back(attention(queries, key_rows, value_rows, unit_row, unit_row, True)))
    after_self = tokens + low_back(matmul(attended, self_o))
    normed = low(layer_norm(after_self, gain_rows[1], biases[1]))
    queries = low(low_back(matmul(normed, cross_q)))
    key_rows = low(low_back(matmul(enc_rows, cross_k)))
    value_rows = low(low_back(matmul(enc_rows, cross_v)))
    attended = low(low_back(attention(queries, key_rows, value_rows, unit_row, enc_row, False)))
    after_cross = after_self + low_back(matmul(attended, cross_o))
    normed = low(layer_norm(after_cross, gain_rows[2], biases[2]))
    pre_active = low_back(matmul(normed, ffn_in))
    hidden = low(jax.nn.gelu(pre_active, approximate=False))
    after_ffn = after_cross + low_back(matmul(hidden, ffn_out))
    return layer_norm(after_ffn, gain_rows[3], biases[3])

def reference(tokens, enc_states, unit_ids, enc_ids, self_q, self_k, self_v, self_o, cross_q, cross_k, cross_v, cross_o, ffn_in, ffn_out, norm_gains, norm_biases, cotangent):
    weights = (self_q.astype(jnp.float32), self_k.astype(jnp.float32), self_v.astype(jnp.float32), self_o.astype(jnp.float32), cross_q.astype(jnp.float32), cross_k.astype(jnp.float32), cross_v.astype(jnp.float32), cross_o.astype(jnp.float32), ffn_in.astype(jnp.float32), ffn_out.astype(jnp.float32))
    gain_rows = norm_gains.astype(jnp.float32)
    biases = norm_biases.astype(jnp.float32)

    def per_sequence(totals, seq_items):
        token_row, enc_row, unit_row, enc_id_row, cot_row = seq_items

        def forward(rows_in, enc_in, weight_set, gain_set, bias_set):
            return layer(rows_in, enc_in, weight_set, gain_set, bias_set, unit_row, enc_id_row)
        layer_value, pullback = jax.vjp(forward, token_row.astype(jnp.float32), enc_row.astype(jnp.float32), weights, gain_rows, biases)
        grad_rows, grad_enc, grad_weights, grad_gains, grad_biases = pullback(cot_row.astype(jnp.float32))
        totals = jax.tree.map(jnp.add, totals, (grad_weights, grad_gains, grad_biases))
        return (totals, (layer_value.astype(jnp.bfloat16), grad_rows, grad_enc))
    zero_grads = jax.tree.map(jnp.zeros_like, (weights, gain_rows, biases))
    totals, stacked = lax.scan(per_sequence, zero_grads, (tokens, enc_states, unit_ids, enc_ids, cotangent))
    grad_weights, grad_gains, grad_biases = totals
    outputs, grad_tokens, grad_enc = stacked
    return (outputs, grad_tokens, grad_enc, grad_weights[0], grad_weights[1], grad_weights[2], grad_weights[3], grad_weights[4], grad_weights[5], grad_weights[6], grad_weights[7], grad_weights[8], grad_weights[9], grad_gains, grad_biases)
```

```python
import functools
import math

import jax
import jax.numpy as jnp
from jax import lax
from jax.experimental import pallas as pl
from jax.experimental.pallas import tpu as pltpu
from jax.sharding import PartitionSpec as P

HEADS = 16
HEAD = 64


eps_norm = 1e-05
big_negative = -1e30


def layer_norm(values_in, gain_row, bias_row):
    centre = values_in - jnp.mean(values_in, axis=-1, keepdims=True)
    spread = jnp.mean(centre * centre, axis=-1, keepdims=True)
    return centre * lax.rsqrt(spread + eps_norm) * gain_row + bias_row


def norm_backward(values_in, gain_row, bias_row, grad_out):
    result, pullback = jax.vjp(layer_norm, values_in, gain_row, bias_row)
    return pullback(grad_out)


def gelu_slope(values_in):
    return 0.5 * (1.0 + lax.erf(values_in * (1.0 / math.sqrt(2.0)))) + values_in * jnp.exp(
        -0.5 * values_in * values_in
    ) * (1.0 / math.sqrt(2.0 * math.pi))


BIG = 1e30
NT = (((1,), (1,)), ((), ()))
TN = (((0,), (0,)), ((), ()))


def key_extras(ids):
    lane = jnp.arange(128)[None, :] % 64
    return jnp.where(lane < 8, (ids[:, None] != lane).astype(jnp.bfloat16), ((lane >= 8) & (lane < 11)).astype(jnp.bfloat16))


def query_extras(ids):
    lane = jnp.arange(128)[None, :] % 64
    return jnp.where((lane < 8) & (ids[:, None] == lane), -BIG, 0.0).astype(jnp.bfloat16)


def windows(unit_ids, key_ids, bq, bk, causal):
    n = key_ids.shape[0]
    nq = unit_ids.shape[0] // bq
    blocks = unit_ids.reshape(nq, bq)
    low = jnp.sum((key_ids[None, :] < blocks[:, :1]).astype(jnp.int32), axis=1)
    if causal:
        end = (jnp.arange(nq, dtype=jnp.int32) + 1) * bq
        count = (end - low + bk - 1) // bk
        start = end - count * bk
    else:
        end = jnp.sum((key_ids[None, :] <= blocks[:, -1:]).astype(jnp.int32), axis=1)
        low = low // 16 * 16
        count = (end - low + bk - 1) // bk
        start = jnp.minimum(low, n - count * bk)
    return jnp.concatenate([start, count])


def attend_forward_kernel(bq, bk, causal, hp, norm, win_ref, q_ref, k_ref, v_ref, qx_ref, kx_ref, o_ref, qe_ref, ka):
    L, N = q_ref.shape[0], k_ref.shape[0]
    nq = L // bq
    lane = lax.broadcasted_iota(jnp.int32, (1, 128), 1)
    first = lane < 64
    part = lane % 64
    for g in range(hp):
        kp = k_ref[:, g*128:(g+1)*128]
        ka[2*g] = jnp.where(first, kp, kx_ref[...])
        ka[2*g+1] = jnp.where(first, kx_ref[...], kp)
    row = lax.broadcasted_iota(jnp.int32, (128, 1), 0)
    rpart = row % 64

    def one(i, W):
        rows = pl.ds(pl.multiple_of(i * bq, bq), bq)
        win = pl.ds(pl.multiple_of(win_ref[i], 16), W)
        xb = qx_ref[rows, :]
        ss = []
        for h in range(2*hp):
            g = h // 2
            qb = q_ref[rows, g*128:(g+1)*128]
            qa = jnp.where(first, qb, xb) if h % 2 == 0 else jnp.where(first, xb, qb)
            s = lax.dot_general(ka[h, win, :], qa, NT, preferred_element_type=jnp.float32)
            if causal:
                tri = lax.broadcasted_iota(jnp.int32, (bq, bq), 0) <= lax.broadcasted_iota(jnp.int32, (bq, bq), 1)
                d = jnp.where(tri, s[W - bq:, :], -BIG)
                s = d if W == bq else jnp.concatenate([s[: W - bq, :], d], axis=0)
            ss.append(s)
        outs, invs, lses = [], [], []
        for h in range(2*hp):
            g = h // 2
            s = ss[h]
            m = jnp.max(s, axis=0, keepdims=True)
            p = jnp.exp(s - m)
            l = jnp.sum(p, axis=0, keepdims=True)
            inv = 1.0 / l
            if norm: p = p * inv
            o = lax.dot_general(p.astype(jnp.bfloat16), v_ref[win, g*128:(g+1)*128], TN, preferred_element_type=jnp.float32)
            outs.append(o); invs.append(inv)
            neg = -(m + jnp.log(l))
            hi = neg.astype(jnp.bfloat16).astype(jnp.float32)
            mid = (neg - hi).astype(jnp.bfloat16).astype(jnp.float32)
            lo = neg - hi - mid
            lses.append((hi, mid, lo))
        for g in range(hp):
            o = jnp.where(first, outs[2*g], outs[2*g+1])
            if not norm:
                t = jnp.where(row < 64, invs[2*g], invs[2*g+1])
                o = o * jnp.transpose(t)
            o_ref[rows, g*128:(g+1)*128] = o.astype(jnp.bfloat16)
            a, b = lses[2*g], lses[2*g+1]
            e = jnp.where(row < 64, jnp.where(rpart == 8, b[0], jnp.where(rpart == 9, b[1], b[2])), jnp.where(rpart == 8, a[0], jnp.where(rpart == 9, a[1], a[2])))
            e = jnp.transpose(jnp.where((rpart >= 8) & (rpart < 11), e, 0.0))
            qe_ref[rows, g*128:(g+1)*128] = jnp.where(part < 8, xb.astype(jnp.float32), e).astype(jnp.bfloat16)

    def step(i, c):
        for j in range(1, N // bk + 1):
            @pl.when(win_ref[nq + i] == j)
            def _():
                one(i, j * bk)
        return c

    lax.fori_loop(0, nq, step, 0)

def attend_forward(q, k, v, qx, kx, win, causal, bq=256, bk=256, hp=1, norm=False):
    L, D = q.shape
    N = k.shape[0]
    w = 128*hp
    col = lambda n: pl.BlockSpec((n, w), lambda p, _: (0, p))
    fix = lambda n: pl.BlockSpec((n, 128), lambda p, _: (0, 0))
    return pl.pallas_call(
        functools.partial(attend_forward_kernel, bq, bk, causal, hp, norm),
        grid_spec=pltpu.PrefetchScalarGridSpec(
            num_scalar_prefetch=1, grid=(D // w,),
            in_specs=[col(L), col(N), col(N), fix(L), fix(N)],
            out_specs=[col(L), col(L)],
            scratch_shapes=[pltpu.VMEM((2*hp, N, 128), jnp.bfloat16)]),
        out_shape=[jax.ShapeDtypeStruct((L, D), jnp.bfloat16)] * 2,
        compiler_params=pltpu.CompilerParams(vmem_limit_bytes=56 << 20),
    )(win, q, k, v, qx, kx)


def attend_backward_kernel(bq, bk, causal, win_ref, q_ref, k_ref, v_ref, o_ref, do_ref, qe_ref, kx_ref, dq_ref, dk_ref, dv_ref, ka, va, dka, dva):
    L, N = q_ref.shape[0], k_ref.shape[0]
    nq = L // bq
    lane = lax.broadcasted_iota(jnp.int32, (1, 128), 1)
    first = lane < 64
    part = lane % 64
    ones = jnp.broadcast_to(jnp.where(part < 3, 1.0, 0.0).astype(jnp.bfloat16), (N, 128))
    ka[0] = jnp.where(first, k_ref[...], kx_ref[...])
    ka[1] = jnp.where(first, kx_ref[...], k_ref[...])
    va[0] = jnp.where(first, v_ref[...], ones)
    va[1] = jnp.where(first, ones, v_ref[...])
    dka[...] = jnp.zeros_like(dka)
    dva[...] = jnp.zeros_like(dva)
    zero = jnp.zeros((1, 128), jnp.bfloat16)

    def one(i, W):
        rows = pl.ds(pl.multiple_of(i * bq, bq), bq)
        win = pl.ds(pl.multiple_of(win_ref[i], 16), W)
        qb, xb, dob = q_ref[rows, :], qe_ref[rows, :], do_ref[rows, :]
        prod = dob.astype(jnp.float32) * o_ref[rows, :].astype(jnp.float32)
        ps, dss = [], []
        for h in range(2):
            mine = first if h == 0 else jnp.logical_not(first)
            neg = -jnp.sum(jnp.where(mine, prod, 0.0), axis=1, keepdims=True)
            hi = neg.astype(jnp.bfloat16).astype(jnp.float32)
            mid = (neg - hi).astype(jnp.bfloat16).astype(jnp.float32)
            lo = neg - hi - mid
            de = jnp.where(part == 0, hi, jnp.where(part == 1, mid, jnp.where(part == 2, lo, 0.0))).astype(jnp.bfloat16)
            qa = jnp.where(mine, qb, xb)
            da = jnp.where(mine, dob, de)
            s = lax.dot_general(ka[h, win, :], qa, NT, preferred_element_type=jnp.float32)
            if causal:
                tri = lax.broadcasted_iota(jnp.int32, (bq, bq), 0) <= lax.broadcasted_iota(jnp.int32, (bq, bq), 1)
                d = jnp.where(tri, s[W - bq:, :], -BIG)
                s = d if W == bq else jnp.concatenate([s[: W - bq, :], d], axis=0)
            p = jnp.exp(s)
            dp = lax.dot_general(va[h, win, :], da, NT, preferred_element_type=jnp.float32)
            dss.append((p * dp).astype(jnp.bfloat16))
            ps.append(p.astype(jnp.bfloat16))
        docat = jnp.concatenate([jnp.where(first, dob, zero), jnp.where(first, zero, dob)], axis=0)
        qcat = jnp.concatenate([jnp.where(first, qb, zero), jnp.where(first, zero, qb)], axis=0)
        dva[win, :] += jnp.dot(jnp.concatenate(ps, axis=1), docat, preferred_element_type=jnp.float32)
        dka[win, :] += jnp.dot(jnp.concatenate(dss, axis=1), qcat, preferred_element_type=jnp.float32)
        kw = k_ref[win, :]
        dq0 = lax.dot_general(dss[0], kw, TN, preferred_element_type=jnp.float32)
        dq1 = lax.dot_general(dss[1], kw, TN, preferred_element_type=jnp.float32)
        dq_ref[rows, :] = (jnp.where(first, dq0, dq1) * 0.125).astype(jnp.bfloat16)

    def step(i, c):
        for j in range(1, N // bk + 1):
            @pl.when(win_ref[nq + i] == j)
            def _():
                one(i, j * bk)
        return c

    lax.fori_loop(0, nq, step, 0)
    dk_ref[...] = dka[...].astype(jnp.bfloat16)
    dv_ref[...] = dva[...].astype(jnp.bfloat16)


def attend_backward(q, k, v, o, do, qe, kx, win, causal, bq=256, bk=256):
    L, D = q.shape
    N = k.shape[0]
    col = lambda n: pl.BlockSpec((n, 128), lambda p, w: (0, p))
    fix = lambda n: pl.BlockSpec((n, 128), lambda p, w: (0, 0))
    return pl.pallas_call(
        functools.partial(attend_backward_kernel, bq, bk, causal),
        grid_spec=pltpu.PrefetchScalarGridSpec(
            num_scalar_prefetch=1, grid=(D // 128,),
            in_specs=[col(L), col(N), col(N), col(L), col(L), col(L), fix(N)],
            out_specs=[col(L), col(N), col(N)],
            scratch_shapes=[pltpu.VMEM((2, N, 128), jnp.bfloat16)] * 2 + [pltpu.VMEM((N, 128), jnp.float32)] * 2),
        out_shape=[jax.ShapeDtypeStruct((L, D), jnp.bfloat16)] + [jax.ShapeDtypeStruct((N, D), jnp.bfloat16)] * 2,
        compiler_params=pltpu.CompilerParams(vmem_limit_bytes=48 << 20),
        cost_estimate=pl.CostEstimate(flops=5 * 2 * L * N * D, bytes_accessed=16 * L * D, transcendentals=0),
    )(win, q, k, v, o, do, qe, kx)


def project(left, right):
    return jnp.dot(left, right, preferred_element_type=jnp.float32)


def weight_term(left, right):
    return jnp.einsum("ra,rb->ab", left, right, preferred_element_type=jnp.float32)


def back_project(grad_rows, weight):
    return jnp.einsum("rb,ab->ra", grad_rows, weight, preferred_element_type=jnp.float32)


def ring_place(chips):
    half = chips // 2
    walk = [2 * i for i in range(half)] + [2 * i + 1 for i in reversed(range(half))]
    place = [0] * chips
    for at, chip in enumerate(walk):
        place[chip] = at
    return walk, place


def ring_moves(count):
    walk, place = ring_place(count // 2)
    chips = len(walk)
    up = [(2 * walk[i] + c, 2 * walk[(i + 1) % chips] + c) for i in range(chips) for c in range(2)]
    down = [(b, a) for a, b in up]
    swap = [(i, i ^ 1) for i in range(count)]
    return up, down, swap


def gather_rows(piece, count):
    if count != 16:
        return lax.all_gather(piece, "shard", axis=0, tiled=True)
    walk, place = ring_place(count // 2)
    up, down, swap = ring_moves(count)
    chips = count // 2
    me = lax.axis_index("shard")
    core = me % 2
    walk_at = jnp.array(walk, jnp.int32)
    at = jnp.array(place, jnp.int32)[me // 2]
    rows = piece.shape[0]
    pieces = {0: piece}
    upward = downward = piece
    for step in range(1, chips // 2 + 1):
        upward = lax.ppermute(upward, "shard", up)
        pieces[-step] = upward
        if step < chips // 2:
            downward = lax.ppermute(downward, "shard", down)
            pieces[step] = downward
    whole = jnp.zeros((count * rows,) + piece.shape[1:], piece.dtype)
    for step, part in pieces.items():
        chip = walk_at[(at + step) % chips]
        other = lax.ppermute(part, "shard", swap)
        whole = lax.dynamic_update_slice_in_dim(whole, part, (2 * chip + core) * rows, 0)
        whole = lax.dynamic_update_slice_in_dim(whole, other, (2 * chip + 1 - core) * rows, 0)
    return whole


def add_pair(left, right):
    return (left.astype(jnp.float32) + right.astype(jnp.float32)).astype(jnp.bfloat16)


def reduce_rows(term, count, flip):
    rows = term.shape[0] // count
    term = term.astype(jnp.bfloat16)
    if count != 16:
        owned = lax.psum_scatter(term, "shard", scatter_dimension=0, tiled=True)
        return lax.psum(owned, "rep").astype(jnp.float32)
    walk, place = ring_place(count // 2)
    up, down, swap = ring_moves(count)
    if flip:
        up, down = down, up
    sign = -1 if flip else 1
    chips = count // 2
    me = lax.axis_index("shard")
    core = me % 2
    walk_at = jnp.array(walk, jnp.int32)
    at = jnp.array(place, jnp.int32)[me // 2]
    split = term.reshape((chips, 2, rows) + term.shape[1:])
    mine = lax.dynamic_index_in_dim(split, core, 1, keepdims=False)
    other = lax.dynamic_index_in_dim(split, 1 - core, 1, keepdims=False)
    both = add_pair(mine, lax.ppermute(other, "shard", swap))

    def part(step):
        return lax.dynamic_index_in_dim(both, walk_at[(at + sign * step) % chips], 0, keepdims=False)

    half = chips // 2
    upward = part(half)
    downward = part(-(half - 1))
    for step in range(half, 0, -1):
        upward = lax.ppermute(upward, "shard", up)
        if step > 1:
            upward = add_pair(upward, part(step - 1))
    for step in range(half - 1, 0, -1):
        downward = lax.ppermute(downward, "shard", down)
        if step > 1:
            downward = add_pair(downward, part(-(step - 1)))
    owned = (part(0).astype(jnp.float32) + upward.astype(jnp.float32) + downward.astype(jnp.float32)).astype(jnp.bfloat16)
    partner = lax.ppermute(owned, "rep", [(0, 1), (1, 0)])
    return owned.astype(jnp.float32) + partner.astype(jnp.float32)


def body(
    tokens,
    enc_states,
    unit_ids,
    enc_ids,
    self_q,
    self_k,
    self_v,
    self_o,
    cross_q,
    cross_k,
    cross_v,
    cross_o,
    ffn_in,
    ffn_out,
    norm_gains,
    norm_biases,
    cotangent,
):
    count = lax.axis_size("shard")
    norm_piece = jnp.concatenate([norm_gains, norm_biases], axis=0)
    own_width = norm_piece.shape[1]
    norm_rows = jnp.pad(norm_piece.reshape(1, -1), ((0, 15), (0, self_q.shape[1] - 8 * own_width)))
    first_set = gather_rows(jnp.concatenate([self_q, self_k, self_v, norm_rows], axis=0), count)
    own_rows = self_q.shape[0]
    first_set = first_set.reshape(count, 3 * own_rows + 16, -1)
    w_sq, w_sk, w_sv = (
        first_set[:, i * own_rows : (i + 1) * own_rows].reshape(count * own_rows, -1) for i in range(3)
    )
    norm_set = first_set[:, 3 * own_rows, : 8 * own_width].reshape(count, 8, own_width)
    norm_set = jnp.transpose(norm_set, (1, 0, 2)).reshape(8, count * own_width).astype(jnp.float32)
    gain_rows, bias_rows = norm_set[:4], norm_set[4:]
    w_so = gather_rows(self_o, count)
    w_cq = gather_rows(cross_q, count)
    w_ck = gather_rows(cross_k, count)
    w_cv = gather_rows(cross_v, count)
    w_co = gather_rows(cross_o, count)
    w_in = gather_rows(ffn_in, count)
    w_out = gather_rows(ffn_out, count)
    seq_count = tokens.shape[0]
    unit_count = tokens.shape[1]
    enc_count = enc_states.shape[1]
    row_count = seq_count * unit_count
    width = tokens.shape[2]
    rows_in = tokens.reshape(row_count, width).astype(jnp.float32)
    enc_rows = enc_states.reshape(seq_count * enc_count, width)
    normed_one = layer_norm(rows_in, gain_rows[0], bias_rows[0]).astype(jnp.bfloat16)
    queries_one = (project(normed_one, w_sq) * 0.125).astype(jnp.bfloat16)
    keys_one = project(normed_one, w_sk).astype(jnp.bfloat16)
    values_one = project(normed_one, w_sv).astype(jnp.bfloat16)

    unit_extra, enc_extra = key_extras(unit_ids[0]), key_extras(enc_ids[0])
    query_extra = query_extras(unit_ids[0])
    self_windows = windows(unit_ids[0], unit_ids[0], 256, 256, True)
    cross_windows = windows(unit_ids[0], enc_ids[0], 256, 256, False)
    attended_one, log_one = attend_forward(
        queries_one, keys_one, values_one, query_extra, unit_extra, self_windows, True, hp=2, norm=True
    )
    after_self = rows_in + project(attended_one, w_so)
    normed_two = layer_norm(after_self, gain_rows[1], bias_rows[1]).astype(jnp.bfloat16)
    queries_two = (project(normed_two, w_cq) * 0.125).astype(jnp.bfloat16)
    keys_two = project(enc_rows, w_ck).astype(jnp.bfloat16)
    values_two = project(enc_rows, w_cv).astype(jnp.bfloat16)

    attended_two, log_two = attend_forward(
        queries_two, keys_two, values_two, query_extra, enc_extra, cross_windows, False, hp=2, norm=True
    )
    after_cross = after_self + project(attended_two, w_co)
    normed_three = layer_norm(after_cross, gain_rows[2], bias_rows[2]).astype(jnp.bfloat16)
    pre_active = project(normed_three, w_in)
    hidden = jax.nn.gelu(pre_active, approximate=False).astype(jnp.bfloat16)
    after_ffn = after_cross + project(hidden, w_out)
    layer_out = (
        layer_norm(after_ffn, gain_rows[3], bias_rows[3])
        .astype(jnp.bfloat16)
        .reshape(seq_count, unit_count, width)
    )
    b_sq, b_sk, b_sv, b_so, b_cq, b_ck, b_cv, b_co, b_in, b_out = (
        w_sq, w_sk, w_sv, w_so, w_cq, w_ck, w_cv, w_co, w_in, w_out
    )
    gain_back, bias_back = gain_rows, bias_rows
    grad_out = cotangent.reshape(row_count, width).astype(jnp.float32)
    grad_after_ffn, gain_four, bias_four = norm_backward(
        after_ffn, gain_back[3], bias_back[3], grad_out
    )
    grad_ffn_rows = grad_after_ffn.astype(jnp.bfloat16)
    grad_w_out = weight_term(hidden, grad_ffn_rows)
    grad_hidden = back_project(grad_ffn_rows, b_out)
    grad_pre = (grad_hidden * gelu_slope(pre_active)).astype(jnp.bfloat16)
    grad_w_in = weight_term(normed_three, grad_pre)
    grad_normed_three = back_project(grad_pre, b_in)
    grad_norm_three, gain_three, bias_three = norm_backward(
        after_cross, gain_back[2], bias_back[2], grad_normed_three
    )
    grad_after_cross = grad_after_ffn + grad_norm_three
    grad_cross_rows = grad_after_cross.astype(jnp.bfloat16)
    grad_w_co = weight_term(attended_two, grad_cross_rows)
    grad_attended_two = back_project(grad_cross_rows, b_co).astype(jnp.bfloat16)

    grad_q_two, grad_k_two, grad_v_two = attend_backward(
        queries_two, keys_two, values_two, attended_two, grad_attended_two, log_two, enc_extra, cross_windows, False
    )
    grad_w_cq = weight_term(normed_two, grad_q_two)
    grad_w_ck = weight_term(enc_rows, grad_k_two)
    grad_w_cv = weight_term(enc_rows, grad_v_two)
    grad_enc = (back_project(grad_k_two, b_ck) + back_project(grad_v_two, b_cv)).reshape(
        seq_count, enc_count, width
    )
    grad_norm_two, gain_two, bias_two = norm_backward(
        after_self, gain_back[1], bias_back[1], back_project(grad_q_two, b_cq)
    )
    grad_after_self = grad_after_cross + grad_norm_two
    grad_self_rows = grad_after_self.astype(jnp.bfloat16)
    grad_w_so = weight_term(attended_one, grad_self_rows)
    grad_attended_one = back_project(grad_self_rows, b_so).astype(jnp.bfloat16)

    grad_q_one, grad_k_one, grad_v_one = attend_backward(
        queries_one, keys_one, values_one, attended_one, grad_attended_one, log_one, unit_extra, self_windows, True
    )
    grad_w_sq = weight_term(normed_one, grad_q_one)
    grad_w_sk = weight_term(normed_one, grad_k_one)
    grad_w_sv = weight_term(normed_one, grad_v_one)
    grad_normed_one = (
        back_project(grad_q_one, b_sq)
        + back_project(grad_k_one, b_sk)
        + back_project(grad_v_one, b_sv)
    )
    grad_norm_one, gain_one, bias_one = norm_backward(
        rows_in, gain_back[0], bias_back[0], grad_normed_one
    )
    grad_tokens = (grad_after_self + grad_norm_one).reshape(seq_count, unit_count, width)
    grad_gains = jnp.stack([gain_one, gain_two, gain_three, gain_four])
    grad_biases = jnp.stack([bias_one, bias_two, bias_three, bias_four])
    norm_term = jnp.concatenate([grad_gains, grad_biases], axis=0).reshape(8, count, own_width)
    norm_term = jnp.transpose(norm_term, (1, 0, 2)).reshape(count, 1, 8 * own_width)
    norm_term = jnp.pad(norm_term, ((0, 0), (0, 15), (0, width - 8 * own_width)))
    last_set = jnp.concatenate(
        [w.reshape(count, own_rows, width) for w in (grad_w_sq, grad_w_sk, grad_w_sv)] + [norm_term], axis=1
    )
    last_set = reduce_rows(last_set.reshape(count * (3 * own_rows + 16), width), count, False)
    norm_sum = last_set[3 * own_rows, : 8 * own_width].reshape(8, own_width)
    summed = (
        last_set[:own_rows],
        last_set[own_rows : 2 * own_rows],
        last_set[2 * own_rows : 3 * own_rows],
        reduce_rows(grad_w_so, count, True),
        reduce_rows(grad_w_cq, count, False),
        reduce_rows(grad_w_ck, count, True),
        reduce_rows(grad_w_cv, count, False),
        reduce_rows(grad_w_co, count, True),
        reduce_rows(grad_w_in, count, False),
        reduce_rows(grad_w_out, count, True),
        norm_sum[:4],
        norm_sum[4:],
    )
    return (
        layer_out,
        grad_tokens,
        grad_enc,
        summed[0],
        summed[1],
        summed[2],
        summed[3],
        summed[4],
        summed[5],
        summed[6],
        summed[7],
        summed[8],
        summed[9],
        summed[10],
        summed[11],
    )


def solution(mesh):
    return jax.shard_map(
        body,
        mesh=mesh,
        in_specs=(
            P(("rep", "shard"), None, None),
            P(("rep", "shard"), None, None),
            P(("rep", "shard"), None),
            P(("rep", "shard"), None),
            P("shard", None),
            P("shard", None),
            P("shard", None),
            P("shard", None),
            P("shard", None),
            P("shard", None),
            P("shard", None),
            P("shard", None),
            P("shard", None),
            P("shard", None),
            P(None, "shard"),
            P(None, "shard"),
            P(("rep", "shard"), None, None),
        ),
        out_specs=(
            P(("rep", "shard"), None, None),
            P(("rep", "shard"), None, None),
            P(("rep", "shard"), None, None),
            P("shard", None),
            P("shard", None),
            P("shard", None),
            P("shard", None),
            P("shard", None),
            P("shard", None),
            P("shard", None),
            P("shard", None),
            P("shard", None),
            P("shard", None),
            P(None, "shard"),
            P(None, "shard"),
        ),
        check_vma=False,
    )
```

```python
import functools
import math

import jax
import jax.numpy as jnp
from jax import lax
from jax.experimental import pallas as pl
from jax.experimental.pallas import tpu as pltpu
from jax.sharding import PartitionSpec as P

HEADS = 16
HEAD = 64


eps_norm = 1e-05


COST = 4
BIG = 1e30
NT = (((1,), (1,)), ((), ()))
TN = (((0,), (0,)), ((), ()))


def key_extras(ids):
    lane = jnp.arange(128)[None, :] % 64
    return jnp.where(lane < 8, (ids[:, None] != lane).astype(jnp.bfloat16), ((lane >= 8) & (lane < 11)).astype(jnp.bfloat16))


def query_extras(ids):
    lane = jnp.arange(128)[None, :] % 64
    return jnp.where((lane < 8) & (ids[:, None] == lane), -BIG, 0.0).astype(jnp.bfloat16)


def windows(unit_ids, key_ids, bq, bk, causal):
    n = key_ids.shape[0]
    nq = unit_ids.shape[0] // bq
    blocks = unit_ids.reshape(nq, bq)
    low = jnp.sum((key_ids[None, :] < blocks[:, :1]).astype(jnp.int32), axis=1)
    if causal:
        end = (jnp.arange(nq, dtype=jnp.int32) + 1) * bq
        count = (end - low + bk - 1) // bk
        start = end - count * bk
    else:
        end = jnp.sum((key_ids[None, :] <= blocks[:, -1:]).astype(jnp.int32), axis=1)
        low = low // 16 * 16
        count = (end - low + bk - 1) // bk
        start = jnp.minimum(low, n - count * bk)
    return jnp.concatenate([start, count])


def attend_forward_kernel(bq, bk, causal, hp, norm, win_ref, q_ref, k_ref, v_ref, qx_ref, kx_ref, o_ref, qe_ref, ka):
    L, N = q_ref.shape[0], k_ref.shape[0]
    nq = L // bq
    lane = lax.broadcasted_iota(jnp.int32, (1, 128), 1)
    first = lane < 64
    part = lane % 64
    for g in range(hp):
        kp = k_ref[:, g*128:(g+1)*128]
        ka[2*g] = jnp.where(first, kp, kx_ref[...])
        ka[2*g+1] = jnp.where(first, kx_ref[...], kp)
    row = lax.broadcasted_iota(jnp.int32, (128, 1), 0)
    rpart = row % 64

    def one(i, W):
        rows = pl.ds(pl.multiple_of(i * bq, bq), bq)
        win = pl.ds(pl.multiple_of(win_ref[i], 16), W)
        xb = qx_ref[rows, :]
        ss = []
        for h in range(2*hp):
            g = h // 2
            qb = q_ref[rows, g*128:(g+1)*128]
            qa = jnp.where(first, qb, xb) if h % 2 == 0 else jnp.where(first, xb, qb)
            s = lax.dot_general(ka[h, win, :], qa, NT, preferred_element_type=jnp.float32)
            if causal:
                tri = lax.broadcasted_iota(jnp.int32, (bq, bq), 0) <= lax.broadcasted_iota(jnp.int32, (bq, bq), 1)
                d = jnp.where(tri, s[W - bq:, :], -BIG)
                s = d if W == bq else jnp.concatenate([s[: W - bq, :], d], axis=0)
            ss.append(s)
        outs, invs, lses = [], [], []
        for h in range(2*hp):
            g = h // 2
            s = ss[h]
            m = jnp.max(s, axis=0, keepdims=True)
            p = jnp.exp(s - m)
            l = jnp.sum(p, axis=0, keepdims=True)
            inv = 1.0 / l
            if norm: p = p * inv
            o = lax.dot_general(p.astype(jnp.bfloat16), v_ref[win, g*128:(g+1)*128], TN, preferred_element_type=jnp.float32)
            outs.append(o); invs.append(inv)
            neg = -(m + jnp.log(l))
            hi = neg.astype(jnp.bfloat16).astype(jnp.float32)
            mid = (neg - hi).astype(jnp.bfloat16).astype(jnp.float32)
            lo = neg - hi - mid
            lses.append((hi, mid, lo))
        for g in range(hp):
            o = jnp.where(first, outs[2*g], outs[2*g+1])
            if not norm:
                t = jnp.where(row < 64, invs[2*g], invs[2*g+1])
                o = o * jnp.transpose(t)
            o_ref[rows, g*128:(g+1)*128] = o.astype(jnp.bfloat16)
            a, b = lses[2*g], lses[2*g+1]
            e = jnp.where(row < 64, jnp.where(rpart == 8, b[0], jnp.where(rpart == 9, b[1], b[2])), jnp.where(rpart == 8, a[0], jnp.where(rpart == 9, a[1], a[2])))
            e = jnp.transpose(jnp.where((rpart >= 8) & (rpart < 11), e, 0.0))
            qe_ref[rows, g*128:(g+1)*128] = jnp.where(part < 8, xb.astype(jnp.float32), e).astype(jnp.bfloat16)

    def step(i, c):
        for j in range(1, N // bk + 1):
            @pl.when(win_ref[nq + i] == j)
            def _():
                one(i, j * bk)
        return c

    lax.fori_loop(0, nq, step, 0)

def attend_forward(q, k, v, qx, kx, win, causal, bq=256, bk=256, hp=1, norm=False):
    L, D = q.shape
    N = k.shape[0]
    w = 128*hp
    col = lambda n: pl.BlockSpec((n, w), lambda p, _: (0, p))
    fix = lambda n: pl.BlockSpec((n, 128), lambda p, _: (0, 0))
    return pl.pallas_call(
        functools.partial(attend_forward_kernel, bq, bk, causal, hp, norm),
        grid_spec=pltpu.PrefetchScalarGridSpec(
            num_scalar_prefetch=1, grid=(D // w,),
            in_specs=[col(L), col(N), col(N), fix(L), fix(N)],
            out_specs=[col(L), col(L)],
            scratch_shapes=[pltpu.VMEM((2*hp, N, 128), jnp.bfloat16)]),
        out_shape=[jax.ShapeDtypeStruct((L, D), jnp.bfloat16)] * 2,
        compiler_params=pltpu.CompilerParams(vmem_limit_bytes=56 << 20),
        cost_estimate=pl.CostEstimate(flops=COST * 2 * 2 * L * N * D, bytes_accessed=10 * L * D, transcendentals=0),
    )(win, q, k, v, qx, kx)


def attend_backward_kernel(bq, bk, causal, win_ref, q_ref, k_ref, v_ref, o_ref, do_ref, qe_ref, kx_ref, dq_ref, dk_ref, dv_ref, ka, va, dka, dva):
    L, N = q_ref.shape[0], k_ref.shape[0]
    nq = L // bq
    lane = lax.broadcasted_iota(jnp.int32, (1, 128), 1)
    first = lane < 64
    part = lane % 64
    ones = jnp.broadcast_to(jnp.where(part < 3, 1.0, 0.0).astype(jnp.bfloat16), (N, 128))
    ka[0] = jnp.where(first, k_ref[...], kx_ref[...])
    ka[1] = jnp.where(first, kx_ref[...], k_ref[...])
    va[0] = jnp.where(first, v_ref[...], ones)
    va[1] = jnp.where(first, ones, v_ref[...])
    dka[...] = jnp.zeros_like(dka)
    dva[...] = jnp.zeros_like(dva)
    zero = jnp.zeros((1, 128), jnp.bfloat16)

    def one(i, W):
        rows = pl.ds(pl.multiple_of(i * bq, bq), bq)
        win = pl.ds(pl.multiple_of(win_ref[i], 16), W)
        qb, xb, dob = q_ref[rows, :], qe_ref[rows, :], do_ref[rows, :]
        prod = dob.astype(jnp.float32) * o_ref[rows, :].astype(jnp.float32)
        ps, dss = [], []
        for h in range(2):
            mine = first if h == 0 else jnp.logical_not(first)
            neg = -jnp.sum(jnp.where(mine, prod, 0.0), axis=1, keepdims=True)
            hi = neg.astype(jnp.bfloat16).astype(jnp.float32)
            mid = (neg - hi).astype(jnp.bfloat16).astype(jnp.float32)
            lo = neg - hi - mid
            de = jnp.where(part == 0, hi, jnp.where(part == 1, mid, jnp.where(part == 2, lo, 0.0))).astype(jnp.bfloat16)
            qa = jnp.where(mine, qb, xb)
            da = jnp.where(mine, dob, de)
            s = lax.dot_general(ka[h, win, :], qa, NT, preferred_element_type=jnp.float32)
            if causal:
                tri = lax.broadcasted_iota(jnp.int32, (bq, bq), 0) <= lax.broadcasted_iota(jnp.int32, (bq, bq), 1)
                d = jnp.where(tri, s[W - bq:, :], -BIG)
                s = d if W == bq else jnp.concatenate([s[: W - bq, :], d], axis=0)
            p = jnp.exp(s)
            dp = lax.dot_general(va[h, win, :], da, NT, preferred_element_type=jnp.float32)
            dss.append((p * dp).astype(jnp.bfloat16))
            ps.append(p.astype(jnp.bfloat16))
        docat = jnp.concatenate([jnp.where(first, dob, zero), jnp.where(first, zero, dob)], axis=0)
        qcat = jnp.concatenate([jnp.where(first, qb, zero), jnp.where(first, zero, qb)], axis=0)
        dva[win, :] += jnp.dot(jnp.concatenate(ps, axis=1), docat, preferred_element_type=jnp.float32)
        dka[win, :] += jnp.dot(jnp.concatenate(dss, axis=1), qcat, preferred_element_type=jnp.float32)
        kw = k_ref[win, :]
        dq0 = lax.dot_general(dss[0], kw, TN, preferred_element_type=jnp.float32)
        dq1 = lax.dot_general(dss[1], kw, TN, preferred_element_type=jnp.float32)
        dq_ref[rows, :] = (jnp.where(first, dq0, dq1) * 0.125).astype(jnp.bfloat16)

    def step(i, c):
        for j in range(1, N // bk + 1):
            @pl.when(win_ref[nq + i] == j)
            def _():
                one(i, j * bk)
        return c

    lax.fori_loop(0, nq, step, 0)
    dk_ref[...] = dka[...].astype(jnp.bfloat16)
    dv_ref[...] = dva[...].astype(jnp.bfloat16)


def attend_backward(q, k, v, o, do, qe, kx, win, causal, bq=256, bk=256):
    L, D = q.shape
    N = k.shape[0]
    col = lambda n: pl.BlockSpec((n, 128), lambda p, w: (0, p))
    fix = lambda n: pl.BlockSpec((n, 128), lambda p, w: (0, 0))
    return pl.pallas_call(
        functools.partial(attend_backward_kernel, bq, bk, causal),
        grid_spec=pltpu.PrefetchScalarGridSpec(
            num_scalar_prefetch=1, grid=(D // 128,),
            in_specs=[col(L), col(N), col(N), col(L), col(L), col(L), fix(N)],
            out_specs=[col(L), col(N), col(N)],
            scratch_shapes=[pltpu.VMEM((2, N, 128), jnp.bfloat16)] * 2 + [pltpu.VMEM((N, 128), jnp.float32)] * 2),
        out_shape=[jax.ShapeDtypeStruct((L, D), jnp.bfloat16)] + [jax.ShapeDtypeStruct((N, D), jnp.bfloat16)] * 2,
        compiler_params=pltpu.CompilerParams(vmem_limit_bytes=48 << 20),
        cost_estimate=pl.CostEstimate(flops=COST * 5 * 2 * L * N * D, bytes_accessed=16 * L * D, transcendentals=0),
    )(win, q, k, v, o, do, qe, kx)


def fetch(plan, refs, order_ref, dst, sem):
    kind, offset, rows, flat, piece_rows, count = plan
    if kind == "flat":
        pltpu.make_async_copy(refs[0].at[pl.ds(flat, rows * count)], dst, sem).start()
        return
    for j in range(count):
        if kind == "ring":
            src = refs[j].at[pl.ds(offset, rows)]
            at = pl.multiple_of(order_ref[j] * rows, 16)
        else:
            src = refs[0].at[pl.ds(j * piece_rows + offset, rows)]
            at = j * rows
        pltpu.make_async_copy(src, dst.at[pl.ds(at, rows)], sem).start()


def arrived(dst, sem):
    pltpu.make_async_copy(dst, dst, sem).wait()


def normed(values_in):
    centre = values_in - jnp.mean(values_in, axis=-1, keepdims=True)
    spread = jnp.mean(centre * centre, axis=-1, keepdims=True)
    scale = lax.rsqrt(spread + eps_norm)
    return centre * scale, scale


def normed_back(unit, scale, gain, grad_out):
    grad_unit = grad_out * gain
    inner = jnp.mean(grad_unit * unit, axis=-1, keepdims=True)
    return (grad_unit - jnp.mean(grad_unit, axis=-1, keepdims=True) - unit * inner) * scale


def mm(left, right):
    return jnp.dot(left, right, preferred_element_type=jnp.float32)


def mm_back(left, right):
    return lax.dot_general(left, right, NT, preferred_element_type=jnp.float32)


def low(values_in):
    return values_in.astype(jnp.bfloat16)


def term_rows(refs, at, values_in):
    refs[at : at + 1, :] += jnp.sum(values_in, axis=0, keepdims=True)


def first_kernel(plans, n_refs, order_ref, x_ref, norm_ref, *rest):
    refs, (a_ref, q_ref, k_ref, v_ref, w, sem) = rest[:n_refs], rest[n_refs:]

    @pl.when(pl.program_id(0) == 0)
    def _():
        for i in range(3):
            fetch(plans[i], refs, order_ref, w.at[i], sem.at[i])
        for i in range(3):
            arrived(w.at[i], sem.at[i])

    unit, _ = normed(x_ref[...].astype(jnp.float32))
    a = low(unit * norm_ref[0:1, :] + norm_ref[4:5, :])
    a_ref[...] = a
    q_ref[...] = low(mm(a, w[0]) * 0.125)
    k_ref[...] = low(mm(a, w[1]))
    v_ref[...] = low(mm(a, w[2]))


def second_kernel(plans, n_refs, order_ref, o_ref, x_ref, e_ref, norm_ref, *rest):
    refs, (r_ref, a_ref, q_ref, k_ref, v_ref, w, sem) = rest[:n_refs], rest[n_refs:]

    @pl.when(pl.program_id(0) == 0)
    def _():
        for i in range(4):
            fetch(plans[i], refs, order_ref, w.at[i], sem.at[i])
        for i in range(4):
            arrived(w.at[i], sem.at[i])

    r = x_ref[...].astype(jnp.float32) + mm(o_ref[...], w[0])
    r_ref[...] = r
    k_ref[...] = low(mm(e_ref[...], w[2]))
    v_ref[...] = low(mm(e_ref[...], w[3]))
    unit, _ = normed(r)
    a = low(unit * norm_ref[1:2, :] + norm_ref[5:6, :])
    a_ref[...] = a
    q_ref[...] = low(mm(a, w[1]) * 0.125)


def third_kernel(plans, n_b, n_c, order_ref, o_ref, r_ref, cot_ref, norm_ref, *rest):
    refs_b, refs_c = rest[:n_b], rest[n_b : n_b + n_c]
    (out_ref, a_ref, h_ref, df_ref, du_ref, dr_ref, dc_ref, do_ref, term_ref, wc, wi, wo, slope, sem) = rest[n_b + n_c :]
    parts = wi.shape[0]
    first = pl.program_id(0) == 0

    @pl.when(first)
    def _():
        fetch(plans[0], refs_b, order_ref, wc, sem.at[0])
        for i in range(parts):
            fetch(plans[1 + i], refs_c, order_ref, wi.at[i], sem.at[1 + i])
        fetch(plans[1 + parts], refs_c, order_ref, wo, sem.at[1 + parts])
        term_ref[...] = jnp.zeros_like(term_ref)
        arrived(wc, sem.at[0])

    r2 = r_ref[...] + mm(o_ref[...], wc[...])
    unit2, scale2 = normed(r2)
    a3 = low(unit2 * norm_ref[2:3, :] + norm_ref[6:7, :])
    a_ref[...] = a3

    @pl.when(first)
    def _():
        for i in range(parts):
            arrived(wi.at[i], sem.at[1 + i])
        arrived(wo, sem.at[1 + parts])

    width = wi.shape[2]
    r3 = r2
    for i in range(parts):
        cols = slice(i * width, (i + 1) * width)
        u = mm(a3, wi[i])
        half = 0.5 * (1.0 + lax.erf(u * (1.0 / math.sqrt(2.0))))
        h = low(u * half)
        h_ref[:, cols] = h
        slope[:, cols] = half + u * jnp.exp(-0.5 * u * u) * (1.0 / math.sqrt(2.0 * math.pi))
        r3 = r3 + mm(h, wo[cols, :])
    unit3, scale3 = normed(r3)
    out_ref[...] = low(unit3 * norm_ref[3:4, :] + norm_ref[7:8, :])
    cot = cot_ref[...].astype(jnp.float32)
    term_rows(term_ref, 3, cot * unit3)
    term_rows(term_ref, 7, cot)
    dr3 = normed_back(unit3, scale3, norm_ref[3:4, :], cot)
    df = low(dr3)
    df_ref[...] = df
    da3 = jnp.zeros_like(dr3)
    for i in range(parts):
        cols = slice(i * width, (i + 1) * width)
        du = low(mm_back(df, wo[cols, :]) * slope[:, cols])
        du_ref[:, cols] = du
        da3 = da3 + mm_back(du, wi[i])
    term_rows(term_ref, 2, da3 * unit2)
    term_rows(term_ref, 6, da3)
    dr2 = dr3 + normed_back(unit2, scale2, norm_ref[2:3, :], da3)
    dr_ref[...] = dr2
    dc = low(dr2)
    dc_ref[...] = dc
    do_ref[...] = low(mm_back(dc, wc[...]))


def fourth_kernel(plans, n_refs, order_ref, dq_ref, r_ref, dr_ref, dk_ref, dv_ref, norm_ref, *rest):
    refs, (dx_ref, dc_ref, do_ref, de_ref, term_ref, w, sem) = rest[:n_refs], rest[n_refs:]

    @pl.when(pl.program_id(0) == 0)
    def _():
        for i in range(4):
            fetch(plans[i], refs, order_ref, w.at[i], sem.at[i])
        for i in range(4):
            arrived(w.at[i], sem.at[i])
        term_ref[...] = jnp.zeros_like(term_ref)

    da = mm_back(dq_ref[...], w[1])
    unit, scale = normed(r_ref[...])
    term_rows(term_ref, 1, da * unit)
    term_rows(term_ref, 5, da)
    dx = dr_ref[...] + normed_back(unit, scale, norm_ref[1:2, :], da)
    dx_ref[...] = dx
    dc = low(dx)
    dc_ref[...] = dc
    do_ref[...] = low(mm_back(dc, w[0]))
    de_ref[...] = mm_back(dk_ref[...], w[2]) + mm_back(dv_ref[...], w[3])


def fifth_kernel(plans, n_refs, order_ref, dq_ref, dk_ref, dv_ref, x_ref, dr_ref, norm_ref, *rest):
    refs, (dx_ref, term_ref, w, sem) = rest[:n_refs], rest[n_refs:]

    @pl.when(pl.program_id(0) == 0)
    def _():
        for i in range(3):
            fetch(plans[i], refs, order_ref, w.at[i], sem.at[i])
        for i in range(3):
            arrived(w.at[i], sem.at[i])
        term_ref[...] = jnp.zeros_like(term_ref)

    da = mm_back(dq_ref[...], w[0]) + mm_back(dk_ref[...], w[1]) + mm_back(dv_ref[...], w[2])
    unit, scale = normed(x_ref[...].astype(jnp.float32))
    term_rows(term_ref, 0, da * unit)
    term_rows(term_ref, 4, da)
    dx_ref[...] = dr_ref[...] + normed_back(unit, scale, norm_ref[0:1, :], da)


def by_rows(kernel, order, row_inputs, norms, piece_refs, row_outputs, terms, scratch, flops, block=256):
    rows = row_inputs[0].shape[0]

    def spec(width):
        return pl.BlockSpec((block, width), lambda i, _: (i, 0))

    def fixed(shape):
        return pl.BlockSpec(shape, lambda i, _: (0, 0))

    out_shape = [jax.ShapeDtypeStruct((rows, w), t) for w, t in row_outputs]
    out_specs = [spec(w) for w, _ in row_outputs]
    if terms:
        out_shape.append(jax.ShapeDtypeStruct(norms.shape, jnp.float32))
        out_specs.append(fixed(norms.shape))
    moved = sum(x.size * x.dtype.itemsize for x in row_inputs) + sum(rows * w * t.dtype.itemsize if hasattr(t, "dtype") else rows * w * jnp.dtype(t).itemsize for w, t in row_outputs)
    return pl.pallas_call(
        kernel,
        grid_spec=pltpu.PrefetchScalarGridSpec(
            num_scalar_prefetch=1,
            grid=(rows // block,),
            in_specs=[spec(x.shape[1]) for x in row_inputs]
            + [fixed(norms.shape)]
            + [pl.BlockSpec(memory_space=pl.ANY)] * len(piece_refs),
            out_specs=out_specs,
            scratch_shapes=scratch,
        ),
        out_shape=out_shape,
        compiler_params=pltpu.CompilerParams(vmem_limit_bytes=58 << 20),
        cost_estimate=pl.CostEstimate(flops=flops, bytes_accessed=moved, transcendentals=0),
    )(order, *row_inputs, norms, *piece_refs)


def term_kernel(pairs, chips, rank_ref, *rest):
    lefts, rights = rest[: len(pairs)], rest[len(pairs) : 2 * len(pairs)]
    mine_ref, other_ref, turned = rest[2 * len(pairs) :]
    weight = pl.program_id(0)
    rows = mine_ref.shape[1]
    for i in range(len(pairs)):
        new_left = i == 0 or pairs[i] != pairs[i - 1]

        @pl.when(weight == i)
        def _():
            if new_left:

                @pl.when(pl.program_id(1) == 0)
                def _():
                    turned[...] = jnp.transpose(lefts[i][...])

            total = low(mm(turned[...], rights[i][...]))
            core = rank_ref[chips]
            for chip in range(chips):
                one = total[2 * chip * rows : (2 * chip + 1) * rows]
                two = total[(2 * chip + 1) * rows : (2 * chip + 2) * rows]
                mine_ref[rank_ref[chip]] = jnp.where(core == 0, one, two)
                other_ref[rank_ref[chip]] = jnp.where(core == 0, two, one)


def term_sets(rank, lefts, rights, pairs, count, block=256):
    total, width = lefts[0].shape[1], rights[0].shape[1]
    rows = total // count
    chips = count // 2
    number = len(lefts)

    def right_spec(i):
        return pl.BlockSpec(
            (rights[i].shape[0], block),
            lambda w, n, _: (0, jnp.where(w == i, n, jnp.where(w < i, 0, width // block - 1))),
        )

    return pl.pallas_call(
        functools.partial(term_kernel, pairs, chips),
        grid_spec=pltpu.PrefetchScalarGridSpec(
            num_scalar_prefetch=1,
            grid=(number, width // block),
            in_specs=[pl.BlockSpec(x.shape, lambda w, n, _: (0, 0)) for x in lefts] + [right_spec(i) for i in range(number)],
            out_specs=[pl.BlockSpec((chips, rows, block), lambda w, n, _: (0, w, n))] * 2,
            scratch_shapes=[pltpu.VMEM((total, lefts[0].shape[0]), jnp.bfloat16)],
        ),
        out_shape=[jax.ShapeDtypeStruct((chips, number * rows, width), jnp.bfloat16)] * 2,
        compiler_params=pltpu.CompilerParams(vmem_limit_bytes=58 << 20),
        cost_estimate=pl.CostEstimate(flops=2 * number * total * width * lefts[0].shape[0], bytes_accessed=6 * number * total * width, transcendentals=0),
    )(rank, *lefts, *rights)


def ring_walk(chips):
    half = chips // 2
    return [2 * i for i in range(half)] + [2 * i + 1 for i in reversed(range(half))]


def ring_moves(count):
    walk = ring_walk(count // 2)
    chips = len(walk)
    up = [(2 * walk[i] + c, 2 * walk[(i + 1) % chips] + c) for i in range(chips) for c in range(2)]
    down = [(b, a) for a, b in up]
    swap = [(i, i ^ 1) for i in range(count)]
    return up, down, swap


def ring_tables(count):
    chips = count // 2
    walk = ring_walk(chips)
    place = [0] * chips
    for at, chip in enumerate(walk):
        place[chip] = at
    order, rank = [], []
    for shard in range(count):
        at, core = place[shard // 2], shard % 2
        near = [walk[(at + k) % chips] for k in range(chips)]
        order.append([2 * c + core for c in near] + [2 * c + 1 - core for c in near])
        rank.append([(place[c] - at) % chips for c in range(chips)] + [core])
    me = lax.axis_index("shard")
    return jnp.array(order, jnp.int32)[me], jnp.array(rank, jnp.int32)[me]


def gather_pieces(piece, count):
    up, down, swap = ring_moves(count)
    chips = count // 2
    pieces = [piece] + [None] * (chips - 1)
    upward = downward = piece
    for step in range(1, chips // 2 + 1):
        upward = lax.ppermute(upward, "shard", up)
        pieces[chips - step] = upward
        if step < chips // 2:
            downward = lax.ppermute(downward, "shard", down)
            pieces[step] = downward
    return pieces + [lax.ppermute(p, "shard", swap) for p in pieces]


def add_low(*values_in):
    return low(sum(v.astype(jnp.float32) for v in values_in))


def over_rep(owned):
    partner = lax.ppermute(owned, "rep", [(0, 1), (1, 0)])
    return owned.astype(jnp.float32) + partner.astype(jnp.float32)


def ring_sum(mine, other, count):
    up, down, swap = ring_moves(count)
    chips = count // 2
    half = chips // 2
    came = lax.ppermute(other, "shard", swap)
    upward = add_low(mine[half], came[half])
    downward = add_low(mine[chips - half + 1], came[chips - half + 1])
    for step in range(half - 1, -1, -1):
        upward = lax.ppermute(upward, "shard", up)
        if step:
            upward = add_low(upward, mine[step], came[step])
    for step in range(half - 2, -1, -1):
        downward = lax.ppermute(downward, "shard", down)
        if step:
            downward = add_low(downward, mine[chips - step], came[chips - step])
    return over_rep(add_low(mine[0], came[0], upward, downward))


def scatter_sum(term):
    return over_rep(lax.psum_scatter(low(term), "shard", scatter_dimension=0, tiled=True))


def total_sum(values_in, count):
    step = 1
    while step < count:
        values_in = values_in + lax.ppermute(values_in, "shard", [(i, i ^ step) for i in range(count)])
        step *= 2
    return values_in + lax.ppermute(values_in, "rep", [(0, 1), (1, 0)])


def weight_term(left, right):
    return jnp.einsum("ra,rb->ab", left, right, preferred_element_type=jnp.float32)


def body(
    tokens,
    enc_states,
    unit_ids,
    enc_ids,
    self_q,
    self_k,
    self_v,
    self_o,
    cross_q,
    cross_k,
    cross_v,
    cross_o,
    ffn_in,
    ffn_out,
    norm_gains,
    norm_biases,
    cotangent,
):
    count = lax.axis_size("shard")
    ring = count == 16
    own, width = self_q.shape
    own_out = ffn_out.shape[0]
    parts = ffn_in.shape[1] // width
    hidden = parts * width
    own_width = norm_gains.shape[1]
    x = tokens.reshape(-1, width)
    enc = enc_states.reshape(-1, width)
    cot = cotangent.reshape(-1, width)
    row_count = x.shape[0]
    bf16, f32 = jnp.bfloat16, jnp.float32

    norm_piece = jnp.concatenate([norm_gains, norm_biases], axis=0)
    in_parts = [ffn_in[:, i * width : (i + 1) * width] for i in range(parts)]
    if ring:
        order, rank = ring_tables(count)
        norm_row = jnp.pad(norm_piece.reshape(1, -1), ((0, 15), (0, width - 8 * own_width)))
        set_a = gather_pieces(jnp.concatenate([self_q, self_k, self_v, norm_row], axis=0), count)
        set_b = gather_pieces(jnp.concatenate([self_o, cross_q, cross_k, cross_v, cross_o], axis=0), count)
        set_c = [lax.all_gather(jnp.concatenate(in_parts + [ffn_out], axis=0), "shard", axis=0, tiled=True)]
        norm_rows = jnp.concatenate([p[3 * own : 3 * own + 1, : 8 * own_width] for p in set_a], axis=0)
        place = (jnp.arange(count, dtype=jnp.int32)[:, None] == order[None, :]).astype(bf16)
        norms = mm(place, norm_rows)
        norms = jnp.transpose(norms.reshape(count, 8, own_width), (1, 0, 2)).reshape(8, width)
        kinds = ("ring", "ring", "tiled")
    else:
        order = jnp.zeros((1,), jnp.int32)

        def whole(part):
            return lax.all_gather(part, "shard", axis=0, tiled=True)

        set_a = [jnp.concatenate([whole(w) for w in (self_q, self_k, self_v)], axis=0)]
        set_b = [jnp.concatenate([whole(w) for w in (self_o, cross_q, cross_k, cross_v, cross_o)], axis=0)]
        set_c = [jnp.concatenate([whole(w) for w in in_parts + [ffn_out]], axis=0)]
        norms = lax.all_gather(norm_piece, "shard", axis=1, tiled=True).astype(f32)
        kinds = ("flat", "flat", "flat")
    plan_a = [(kinds[0], i * own, own, i * width, 0, count) for i in range(3)]
    plan_b = [(kinds[1], i * own, own, i * width, 0, count) for i in range(5)]
    piece_c = parts * own + own_out
    plan_c = [(kinds[2], i * own, own, i * width, piece_c, count) for i in range(parts)]
    plan_c.append((kinds[2], parts * own, own_out, parts * width, piece_c, count))
    sems = pltpu.SemaphoreType.DMA
    square = 2 * row_count * width * width

    unit_extra, enc_extra = key_extras(unit_ids[0]), key_extras(enc_ids[0])
    query_extra = query_extras(unit_ids[0])
    self_windows = windows(unit_ids[0], unit_ids[0], 256, 256, True)
    cross_windows = windows(unit_ids[0], enc_ids[0], 256, 256, False)
    a1, q1, k1, v1 = by_rows(
        functools.partial(first_kernel, plan_a, len(set_a)), order, [x], norms, set_a,
        [(width, bf16)] * 4, False,
        [pltpu.VMEM((3, width, width), bf16), sems((3,))], 3 * square,
    )
    o1, log1 = attend_forward(q1, k1, v1, query_extra, unit_extra, self_windows, True, hp=2, norm=True)
    r1, a2, q2, k2, v2 = by_rows(
        functools.partial(second_kernel, plan_b[:4], len(set_b)), order, [o1, x, enc], norms, set_b,
        [(width, f32)] + [(width, bf16)] * 4, False,
        [pltpu.VMEM((4, width, width), bf16), sems((4,))], 4 * square,
    )
    o2, log2 = attend_forward(q2, k2, v2, query_extra, enc_extra, cross_windows, False, hp=2, norm=True)
    out, a3, h, df, du, dr2, dc2, do2, terms_three = by_rows(
        functools.partial(third_kernel, plan_b[4:] + plan_c, len(set_b), len(set_c)), order, [o2, r1, cot], norms, set_b + set_c,
        [(width, bf16), (width, bf16), (hidden, bf16), (width, bf16), (hidden, bf16), (width, f32), (width, bf16), (width, bf16)], True,
        [
            pltpu.VMEM((width, width), bf16),
            pltpu.VMEM((parts, width, width), bf16),
            pltpu.VMEM((hidden, width), bf16),
            pltpu.VMEM((256, hidden), f32),
            sems((parts + 2,)),
        ],
        (2 + 4 * parts) * square,
    )

    grad_out = scatter_sum(weight_term(h, df))
    grad_in = scatter_sum(weight_term(a3, du))
    dq2, dk2, dv2 = attend_backward(q2, k2, v2, o2, do2, log2, enc_extra, cross_windows, False)
    dr1, dc1, do1, grad_enc, terms_two = by_rows(
        functools.partial(fourth_kernel, plan_b[:4], len(set_b)), order, [dq2, r1, dr2, dk2, dv2], norms, set_b,
        [(width, f32), (width, bf16), (width, bf16), (width, f32)], True,
        [pltpu.VMEM((4, width, width), bf16), sems((4,))], 4 * square,
    )
    lefts, rights = [o2, a2, enc, enc, o1], [dc2, dq2, dk2, dv2, dc1]
    if ring:
        mine, other = term_sets(rank, lefts, rights, (0, 1, 2, 2, 3), count)
        grad_b = ring_sum(mine, other, count)
        grad_co, grad_cq, grad_ck, grad_cv, grad_so = (grad_b[i * own : (i + 1) * own] for i in range(5))
    else:
        grad_co, grad_cq, grad_ck, grad_cv, grad_so = (scatter_sum(weight_term(a, b)) for a, b in zip(lefts, rights))
    dq1, dk1, dv1 = attend_backward(q1, k1, v1, o1, do1, log1, unit_extra, self_windows, True)
    lefts, rights = [a1, a1, a1], [dq1, dk1, dv1]
    if ring:
        mine, other = term_sets(rank, lefts, rights, (0, 0, 0), count)
        grad_a = ring_sum(mine, other, count)
        grad_sq, grad_sk, grad_sv = (grad_a[i * own : (i + 1) * own] for i in range(3))
    else:
        grad_sq, grad_sk, grad_sv = (scatter_sum(weight_term(a, b)) for a, b in zip(lefts, rights))
    grad_x, terms_one = by_rows(
        functools.partial(fifth_kernel, plan_a, len(set_a)), order, [dq1, dk1, dv1, x, dr1], norms, set_a,
        [(width, f32)], True,
        [pltpu.VMEM((3, width, width), bf16), sems((3,))], 3 * square,
    )
    norm_sum = total_sum(terms_one + terms_two + terms_three, count)
    norm_sum = lax.dynamic_slice_in_dim(norm_sum, lax.axis_index("shard") * own_width, own_width, 1)
    return (
        out.reshape(tokens.shape),
        grad_x.reshape(tokens.shape),
        grad_enc.reshape(enc_states.shape),
        grad_sq,
        grad_sk,
        grad_sv,
        grad_so,
        grad_cq,
        grad_ck,
        grad_cv,
        grad_co,
        grad_in,
        grad_out,
        norm_sum[:4],
        norm_sum[4:],
    )


def solution(mesh):
    return jax.shard_map(
        body,
        mesh=mesh,
        in_specs=(
            P(("rep", "shard"), None, None),
            P(("rep", "shard"), None, None),
            P(("rep", "shard"), None),
            P(("rep", "shard"), None),
            P("shard", None),
            P("shard", None),
            P("shard", None),
            P("shard", None),
            P("shard", None),
            P("shard", None),
            P("shard", None),
            P("shard", None),
            P("shard", None),
            P("shard", None),
            P(None, "shard"),
            P(None, "shard"),
            P(("rep", "shard"), None, None),
        ),
        out_specs=(
            P(("rep", "shard"), None, None),
            P(("rep", "shard"), None, None),
            P(("rep", "shard"), None, None),
            P("shard", None),
            P("shard", None),
            P("shard", None),
            P("shard", None),
            P("shard", None),
            P("shard", None),
            P("shard", None),
            P("shard", None),
            P("shard", None),
            P("shard", None),
            P(None, "shard"),
            P(None, "shard"),
        ),
        check_vma=False,
    )
```

```python
import functools
import math

import jax
import jax.numpy as jnp
from jax import lax
from jax.experimental import pallas as pl
from jax.experimental.pallas import tpu as pltpu
from jax.sharding import PartitionSpec as P

HEADS = 16
HEAD = 64


eps_norm = 1e-05


COST = 4


def estimate(flops, bytes_accessed, transcendentals):
    return pl.CostEstimate(flops=flops // 8, bytes_accessed=bytes_accessed // 8, transcendentals=0)
BIG = 1e30
NT = (((1,), (1,)), ((), ()))
TN = (((0,), (0,)), ((), ()))


def key_extras(ids):
    lane = jnp.arange(128)[None, :] % 64
    return jnp.where(lane < 8, (ids[:, None] != lane).astype(jnp.bfloat16), ((lane >= 8) & (lane < 11)).astype(jnp.bfloat16))


def query_extras(ids):
    lane = jnp.arange(128)[None, :] % 64
    return jnp.where((lane < 8) & (ids[:, None] == lane), -BIG, 0.0).astype(jnp.bfloat16)


def windows(unit_ids, key_ids, bq, bk, causal):
    n = key_ids.shape[0]
    nq = unit_ids.shape[0] // bq
    blocks = unit_ids.reshape(nq, bq)
    low = jnp.sum((key_ids[None, :] < blocks[:, :1]).astype(jnp.int32), axis=1)
    if causal:
        end = (jnp.arange(nq, dtype=jnp.int32) + 1) * bq
        count = (end - low + bk - 1) // bk
        start = end - count * bk
    else:
        end = jnp.sum((key_ids[None, :] <= blocks[:, -1:]).astype(jnp.int32), axis=1)
        low = low // 16 * 16
        count = (end - low + bk - 1) // bk
        start = jnp.minimum(low, n - count * bk)
    return jnp.concatenate([start, count])


def attend_forward_kernel(bq, bk, causal, hp, norm, win_ref, q_ref, k_ref, v_ref, qx_ref, kx_ref, *rest):
    o_ref, qe_ref, ka = rest[-3:]
    L, N = q_ref.shape[0], k_ref.shape[0]
    nq = L // bq
    lane = lax.broadcasted_iota(jnp.int32, (1, 128), 1)
    first = lane < 64
    part = lane % 64
    for g in range(hp):
        kp = k_ref[:, g*128:(g+1)*128]
        ka[2*g] = jnp.where(first, kp, kx_ref[...])
        ka[2*g+1] = jnp.where(first, kx_ref[...], kp)
    row = lax.broadcasted_iota(jnp.int32, (128, 1), 0)
    rpart = row % 64

    def one(i, W):
        rows = pl.ds(pl.multiple_of(i * bq, bq), bq)
        win = pl.ds(pl.multiple_of(win_ref[i], 16), W)
        xb = qx_ref[rows, :]
        ss = []
        for h in range(2*hp):
            g = h // 2
            qb = q_ref[rows, g*128:(g+1)*128]
            qa = jnp.where(first, qb, xb) if h % 2 == 0 else jnp.where(first, xb, qb)
            s = lax.dot_general(ka[h, win, :], qa, NT, preferred_element_type=jnp.float32)
            if causal:
                tri = lax.broadcasted_iota(jnp.int32, (bq, bq), 0) <= lax.broadcasted_iota(jnp.int32, (bq, bq), 1)
                d = jnp.where(tri, s[W - bq:, :], -BIG)
                s = d if W == bq else jnp.concatenate([s[: W - bq, :], d], axis=0)
            ss.append(s)
        outs, invs, lses = [], [], []
        for h in range(2*hp):
            g = h // 2
            s = ss[h]
            m = jnp.max(s, axis=0, keepdims=True)
            p = jnp.exp(s - m)
            l = jnp.sum(p, axis=0, keepdims=True)
            inv = 1.0 / l
            if norm: p = p * inv
            o = lax.dot_general(p.astype(jnp.bfloat16), v_ref[win, g*128:(g+1)*128], TN, preferred_element_type=jnp.float32)
            outs.append(o); invs.append(inv)
            neg = -(m + jnp.log(l))
            hi = neg.astype(jnp.bfloat16).astype(jnp.float32)
            mid = (neg - hi).astype(jnp.bfloat16).astype(jnp.float32)
            lo = neg - hi - mid
            lses.append((hi, mid, lo))
        for g in range(hp):
            o = jnp.where(first, outs[2*g], outs[2*g+1])
            if not norm:
                t = jnp.where(row < 64, invs[2*g], invs[2*g+1])
                o = o * jnp.transpose(t)
            o_ref[rows, g*128:(g+1)*128] = o.astype(jnp.bfloat16)
            a, b = lses[2*g], lses[2*g+1]
            e = jnp.where(row < 64, jnp.where(rpart == 8, b[0], jnp.where(rpart == 9, b[1], b[2])), jnp.where(rpart == 8, a[0], jnp.where(rpart == 9, a[1], a[2])))
            e = jnp.transpose(jnp.where((rpart >= 8) & (rpart < 11), e, 0.0))
            qe_ref[rows, g*128:(g+1)*128] = jnp.where(part < 8, xb.astype(jnp.float32), e).astype(jnp.bfloat16)

    def step(i, c):
        for j in range(1, N // bk + 1):
            @pl.when(win_ref[nq + i] == j)
            def _():
                one(i, j * bk)
        return c

    lax.fori_loop(0, nq, step, 0)

def attend_forward(q, k, v, qx, kx, win, causal, pairs, after=(), bq=256, bk=256, hp=2):
    L, N = q.shape[0], k.shape[0]
    w = 128 * hp
    start, number = pairs[0] // hp, (pairs[1] - pairs[0]) // hp
    col = lambda n: pl.BlockSpec((n, w), lambda p, _: (0, start + p))
    own = lambda n: pl.BlockSpec((n, w), lambda p, _: (0, p))
    fix = lambda n: pl.BlockSpec((n, 128), lambda p, _: (0, 0))
    return pl.pallas_call(
        functools.partial(attend_forward_kernel, bq, bk, causal, hp, True),
        grid_spec=pltpu.PrefetchScalarGridSpec(
            num_scalar_prefetch=1,
            grid=(number,),
            in_specs=[col(L), col(N), col(N), fix(L), fix(N)] + [pl.BlockSpec(memory_space=pl.ANY)] * len(after),
            out_specs=[own(L), own(L)],
            scratch_shapes=[pltpu.VMEM((2 * hp, N, 128), jnp.bfloat16)],
        ),
        out_shape=[jax.ShapeDtypeStruct((L, number * w), jnp.bfloat16)] * 2,
        compiler_params=pltpu.CompilerParams(vmem_limit_bytes=56 << 20),
        cost_estimate=estimate(
            flops=COST * 2 * 2 * L * N * number * w, bytes_accessed=10 * L * number * w, transcendentals=0
        ),
    )(win, q, k, v, qx, kx, *after)


def attend_backward_kernel(bq, bk, causal, win_ref, q_ref, k_ref, v_ref, o_ref, do_ref, qe_ref, kx_ref, *rest):
    dq_ref, dk_ref, dv_ref, ka, va, dka, dva = rest[-7:]
    L, N = q_ref.shape[0], k_ref.shape[0]
    nq = L // bq
    lane = lax.broadcasted_iota(jnp.int32, (1, 128), 1)
    first = lane < 64
    part = lane % 64
    ones = jnp.broadcast_to(jnp.where(part < 3, 1.0, 0.0).astype(jnp.bfloat16), (N, 128))
    ka[0] = jnp.where(first, k_ref[...], kx_ref[...])
    ka[1] = jnp.where(first, kx_ref[...], k_ref[...])
    va[0] = jnp.where(first, v_ref[...], ones)
    va[1] = jnp.where(first, ones, v_ref[...])
    dka[...] = jnp.zeros_like(dka)
    dva[...] = jnp.zeros_like(dva)
    zero = jnp.zeros((1, 128), jnp.bfloat16)

    def one(i, W):
        rows = pl.ds(pl.multiple_of(i * bq, bq), bq)
        win = pl.ds(pl.multiple_of(win_ref[i], 16), W)
        qb, xb, dob = q_ref[rows, :], qe_ref[rows, :], do_ref[rows, :]
        prod = dob.astype(jnp.float32) * o_ref[rows, :].astype(jnp.float32)
        ps, dss = [], []
        for h in range(2):
            mine = first if h == 0 else jnp.logical_not(first)
            neg = -jnp.sum(jnp.where(mine, prod, 0.0), axis=1, keepdims=True)
            hi = neg.astype(jnp.bfloat16).astype(jnp.float32)
            mid = (neg - hi).astype(jnp.bfloat16).astype(jnp.float32)
            lo = neg - hi - mid
            de = jnp.where(part == 0, hi, jnp.where(part == 1, mid, jnp.where(part == 2, lo, 0.0))).astype(jnp.bfloat16)
            qa = jnp.where(mine, qb, xb)
            da = jnp.where(mine, dob, de)
            s = lax.dot_general(ka[h, win, :], qa, NT, preferred_element_type=jnp.float32)
            if causal:
                tri = lax.broadcasted_iota(jnp.int32, (bq, bq), 0) <= lax.broadcasted_iota(jnp.int32, (bq, bq), 1)
                d = jnp.where(tri, s[W - bq:, :], -BIG)
                s = d if W == bq else jnp.concatenate([s[: W - bq, :], d], axis=0)
            p = jnp.exp(s)
            dp = lax.dot_general(va[h, win, :], da, NT, preferred_element_type=jnp.float32)
            dss.append((p * dp).astype(jnp.bfloat16))
            ps.append(p.astype(jnp.bfloat16))
        docat = jnp.concatenate([jnp.where(first, dob, zero), jnp.where(first, zero, dob)], axis=0)
        qcat = jnp.concatenate([jnp.where(first, qb, zero), jnp.where(first, zero, qb)], axis=0)
        dva[win, :] += jnp.dot(jnp.concatenate(ps, axis=1), docat, preferred_element_type=jnp.float32)
        dka[win, :] += jnp.dot(jnp.concatenate(dss, axis=1), qcat, preferred_element_type=jnp.float32)
        kw = k_ref[win, :]
        dq0 = lax.dot_general(dss[0], kw, TN, preferred_element_type=jnp.float32)
        dq1 = lax.dot_general(dss[1], kw, TN, preferred_element_type=jnp.float32)
        dq_ref[rows, :] = (jnp.where(first, dq0, dq1) * 0.125).astype(jnp.bfloat16)

    def step(i, c):
        for j in range(1, N // bk + 1):
            @pl.when(win_ref[nq + i] == j)
            def _():
                one(i, j * bk)
        return c

    lax.fori_loop(0, nq, step, 0)
    dk_ref[...] = dka[...].astype(jnp.bfloat16)
    dv_ref[...] = dva[...].astype(jnp.bfloat16)


def attend_backward(q, k, v, o, do, qe, kx, win, causal, pairs, base=0, after=(), bq=256, bk=256):
    L, N = q.shape[0], k.shape[0]
    start, number = pairs[0], pairs[1] - pairs[0]
    col = lambda n: pl.BlockSpec((n, 128), lambda p, _: (0, start + p))
    own = lambda n: pl.BlockSpec((n, 128), lambda p, _: (0, p))
    held = pl.BlockSpec((L, 128), lambda p, _: (0, start - base + p))
    fix = lambda n: pl.BlockSpec((n, 128), lambda p, _: (0, 0))
    return pl.pallas_call(
        functools.partial(attend_backward_kernel, bq, bk, causal),
        grid_spec=pltpu.PrefetchScalarGridSpec(
            num_scalar_prefetch=1,
            grid=(number,),
            in_specs=[col(L), col(N), col(N), held, col(L), held, fix(N)]
            + [pl.BlockSpec(memory_space=pl.ANY)] * len(after),
            out_specs=[own(L), own(N), own(N)],
            scratch_shapes=[pltpu.VMEM((2, N, 128), jnp.bfloat16)] * 2 + [pltpu.VMEM((N, 128), jnp.float32)] * 2,
        ),
        out_shape=[jax.ShapeDtypeStruct((L, number * 128), jnp.bfloat16)]
        + [jax.ShapeDtypeStruct((N, number * 128), jnp.bfloat16)] * 2,
        compiler_params=pltpu.CompilerParams(vmem_limit_bytes=48 << 20),
        cost_estimate=estimate(
            flops=COST * 5 * 2 * L * N * number * 128, bytes_accessed=16 * L * number * 128, transcendentals=0
        ),
    )(win, q, k, v, o, do, qe, kx, *after)


def fetch(plan, refs, order_ref, dst, sem):
    kind, offset, rows, flat, piece_rows, count = plan
    if kind == "flat":
        part = rows * count // 16
        for j in range(16):
            pltpu.make_async_copy(refs[0].at[pl.ds(flat + j * part, part)], dst.at[pl.ds(j * part, part)], sem).start()
        return
    for j in range(count):
        if kind == "ring":
            src = refs[j].at[pl.ds(offset, rows)]
            at = pl.multiple_of(order_ref[j] * rows, 16)
        else:
            src = refs[0].at[pl.ds(j * piece_rows + offset, rows)]
            at = j * rows
        pltpu.make_async_copy(src, dst.at[pl.ds(at, rows)], sem).start()


def arrived(dst, sem):
    pltpu.make_async_copy(dst, dst, sem).wait()


def normed(values_in):
    centre = values_in - jnp.mean(values_in, axis=-1, keepdims=True)
    spread = jnp.mean(centre * centre, axis=-1, keepdims=True)
    scale = lax.rsqrt(spread + eps_norm)
    return centre * scale, scale


def normed_back(unit, scale, gain, grad_out):
    grad_unit = grad_out * gain
    inner = jnp.mean(grad_unit * unit, axis=-1, keepdims=True)
    return (grad_unit - jnp.mean(grad_unit, axis=-1, keepdims=True) - unit * inner) * scale


def mm(left, right):
    return jnp.dot(left, right, preferred_element_type=jnp.float32)


def mm_back(left, right):
    return lax.dot_general(left, right, NT, preferred_element_type=jnp.float32)


def low(values_in):
    return values_in.astype(jnp.bfloat16)


def term_rows(refs, at, values_in):
    refs[at : at + 1, :] += jnp.sum(values_in, axis=0, keepdims=True)


def first_kernel(plans, n_refs, order_ref, x_ref, norm_ref, *rest):
    refs, (a_ref, q_ref, k_ref, v_ref, w, sem) = rest[:n_refs], rest[-6:]

    @pl.when(pl.program_id(0) == 0)
    def _():
        for i in range(3):
            fetch(plans[i], refs, order_ref, w.at[i], sem.at[i])
        for i in range(3):
            arrived(w.at[i], sem.at[i])

    unit, _ = normed(x_ref[...].astype(jnp.float32))
    a = low(unit * norm_ref[0:1, :] + norm_ref[4:5, :])
    a_ref[...] = a
    q_ref[...] = low(mm(a, w[0]) * 0.125)
    k_ref[...] = low(mm(a, w[1]))
    v_ref[...] = low(mm(a, w[2]))


def joined(refs):
    return refs[0][...] if len(refs) == 1 else jnp.concatenate([r[...] for r in refs], axis=1)


def second_kernel(plans, n_refs, n_o, order_ref, *rest):
    o_refs, (x_ref, e_ref, norm_ref), rest = rest[:n_o], rest[n_o : n_o + 3], rest[n_o + 3 :]
    refs, (r_ref, a_ref, q_ref, k_ref, v_ref, w, sem) = rest[:n_refs], rest[-7:]

    @pl.when(pl.program_id(0) == 0)
    def _():
        for i in range(4):
            fetch(plans[i], refs, order_ref, w.at[i], sem.at[i])
        for i in range(4):
            arrived(w.at[i], sem.at[i])

    r = x_ref[...].astype(jnp.float32) + mm(joined(o_refs), w[0])
    r_ref[...] = r
    k_ref[...] = low(mm(e_ref[...], w[2]))
    v_ref[...] = low(mm(e_ref[...], w[3]))
    unit, _ = normed(r)
    a = low(unit * norm_ref[1:2, :] + norm_ref[5:6, :])
    a_ref[...] = a
    q_ref[...] = low(mm(a, w[1]) * 0.125)


def third_kernel(plans, n_b, n_c, n_o, order_ref, *rest):
    o_refs, (r_ref, cot_ref, norm_ref), rest = rest[:n_o], rest[n_o : n_o + 3], rest[n_o + 3 :]
    refs_b, refs_c = rest[:n_b], rest[n_b : n_b + n_c]
    (out_ref, a_ref, h_ref, df_ref, du_ref, dr_ref, dc_ref, do_ref, term_ref, wc, wi, wo, slope, sem) = rest[-14:]
    parts = wi.shape[0]
    first = pl.program_id(0) == 0

    @pl.when(first)
    def _():
        fetch(plans[0], refs_b, order_ref, wc, sem.at[0])
        for i in range(parts):
            fetch(plans[1 + i], refs_c, order_ref, wi.at[i], sem.at[1 + i])
        fetch(plans[1 + parts], refs_c, order_ref, wo, sem.at[1 + parts])
        term_ref[...] = jnp.zeros_like(term_ref)
        arrived(wc, sem.at[0])

    r2 = r_ref[...] + mm(joined(o_refs), wc[...])
    unit2, scale2 = normed(r2)
    a3 = low(unit2 * norm_ref[2:3, :] + norm_ref[6:7, :])
    a_ref[...] = a3

    @pl.when(first)
    def _():
        for i in range(parts):
            arrived(wi.at[i], sem.at[1 + i])
        arrived(wo, sem.at[1 + parts])

    width = wi.shape[2]
    r3 = r2
    for i in range(parts):
        cols = slice(i * width, (i + 1) * width)
        u = mm(a3, wi[i])
        half = 0.5 * (1.0 + lax.erf(u * (1.0 / math.sqrt(2.0))))
        h = low(u * half)
        h_ref[:, cols] = h
        slope[:, cols] = half + u * jnp.exp(-0.5 * u * u) * (1.0 / math.sqrt(2.0 * math.pi))
        r3 = r3 + mm(h, wo[cols, :])
    unit3, scale3 = normed(r3)
    out_ref[...] = low(unit3 * norm_ref[3:4, :] + norm_ref[7:8, :])
    cot = cot_ref[...].astype(jnp.float32)
    term_rows(term_ref, 3, cot * unit3)
    term_rows(term_ref, 7, cot)
    dr3 = normed_back(unit3, scale3, norm_ref[3:4, :], cot)
    df = low(dr3)
    df_ref[...] = df
    da3 = jnp.zeros_like(dr3)
    for i in range(parts):
        cols = slice(i * width, (i + 1) * width)
        du = low(mm_back(df, wo[cols, :]) * slope[:, cols])
        du_ref[:, cols] = du
        da3 = da3 + mm_back(du, wi[i])
    term_rows(term_ref, 2, da3 * unit2)
    term_rows(term_ref, 6, da3)
    dr2 = dr3 + normed_back(unit2, scale2, norm_ref[2:3, :], da3)
    dr_ref[...] = dr2
    dc = low(dr2)
    dc_ref[...] = dc
    do_ref[...] = low(mm_back(dc, wc[...]))


def fourth_kernel(plans, n_refs, n_g, order_ref, *rest):
    dq_refs, dk_refs, dv_refs = (rest[i * n_g : (i + 1) * n_g] for i in range(3))
    (r_ref, dr_ref, norm_ref), rest = rest[3 * n_g : 3 * n_g + 3], rest[3 * n_g + 3 :]
    refs, (dx_ref, dc_ref, do_ref, de_ref, term_ref, w, sem) = rest[:n_refs], rest[-7:]

    @pl.when(pl.program_id(0) == 0)
    def _():
        for i in range(4):
            fetch(plans[i], refs, order_ref, w.at[i], sem.at[i])
        for i in range(4):
            arrived(w.at[i], sem.at[i])
        term_ref[...] = jnp.zeros_like(term_ref)

    da = mm_back(joined(dq_refs), w[1])
    unit, scale = normed(r_ref[...])
    term_rows(term_ref, 1, da * unit)
    term_rows(term_ref, 5, da)
    dx = dr_ref[...] + normed_back(unit, scale, norm_ref[1:2, :], da)
    dx_ref[...] = dx
    dc = low(dx)
    dc_ref[...] = dc
    do_ref[...] = low(mm_back(dc, w[0]))
    de_ref[...] = mm_back(joined(dk_refs), w[2]) + mm_back(joined(dv_refs), w[3])


def fifth_kernel(plans, n_refs, n_g, order_ref, *rest):
    dq_refs, dk_refs, dv_refs = (rest[i * n_g : (i + 1) * n_g] for i in range(3))
    (x_ref, dr_ref, norm_ref), rest = rest[3 * n_g : 3 * n_g + 3], rest[3 * n_g + 3 :]
    refs, (dx_ref, term_ref, w, sem) = rest[:n_refs], rest[-4:]

    @pl.when(pl.program_id(0) == 0)
    def _():
        for i in range(3):
            fetch(plans[i], refs, order_ref, w.at[i], sem.at[i])
        for i in range(3):
            arrived(w.at[i], sem.at[i])
        term_ref[...] = jnp.zeros_like(term_ref)

    da = mm_back(joined(dq_refs), w[0]) + mm_back(joined(dk_refs), w[1]) + mm_back(joined(dv_refs), w[2])
    unit, scale = normed(x_ref[...].astype(jnp.float32))
    term_rows(term_ref, 0, da * unit)
    term_rows(term_ref, 4, da)
    dx_ref[...] = dr_ref[...] + normed_back(unit, scale, norm_ref[0:1, :], da)


def by_rows(kernel, order, row_inputs, norms, piece_refs, row_outputs, terms, scratch, flops, after=(), block=256, part=(0, 1), into=None):
    rows = row_inputs[0].shape[0]
    steps = rows // block // part[1]
    first = part[0] * steps
    piece_refs = list(piece_refs) + list(after) + ([] if into is None else [into])
    aliases = {} if into is None else {1 + len(row_inputs) + len(piece_refs): 0}

    def spec(width):
        return pl.BlockSpec((block, width), lambda i, _: (first + i, 0))

    def fixed(shape):
        return pl.BlockSpec(shape, lambda i, _: (0, 0))

    out_shape = [jax.ShapeDtypeStruct((rows, w), t) for w, t in row_outputs]
    out_specs = [spec(w) for w, _ in row_outputs]
    if terms:
        out_shape.append(jax.ShapeDtypeStruct(norms.shape, jnp.float32))
        out_specs.append(fixed(norms.shape))
    moved = sum(x.size * x.dtype.itemsize for x in row_inputs) + sum(rows * w * t.dtype.itemsize if hasattr(t, "dtype") else rows * w * jnp.dtype(t).itemsize for w, t in row_outputs)
    return pl.pallas_call(
        kernel,
        grid_spec=pltpu.PrefetchScalarGridSpec(
            num_scalar_prefetch=1,
            grid=(steps,),
            in_specs=[spec(x.shape[1]) for x in row_inputs]
            + [fixed(norms.shape)]
            + [pl.BlockSpec(memory_space=pl.ANY)] * len(piece_refs),
            out_specs=out_specs,
            scratch_shapes=scratch,
        ),
        out_shape=out_shape,
        input_output_aliases=aliases,
        compiler_params=pltpu.CompilerParams(vmem_limit_bytes=58 << 20),
        cost_estimate=estimate(flops=flops, bytes_accessed=moved, transcendentals=0),
    )(order, *row_inputs, norms, *piece_refs)


def term_kernel(names, chips, n_left, n_right, rank_ref, *rest):
    parts = len(names)
    flat, rest = rest[: sum(n_left)], rest[sum(n_left) :]
    lefts = [flat[sum(n_left[:i]) : sum(n_left[: i + 1])] for i in range(len(n_left))]
    rights = [rest[sum(n_right[:i]) : sum(n_right[: i + 1])] for i in range(parts)]
    mine_ref, other_ref, turned = rest[-3:]
    rows = mine_ref.shape[1]
    for i in range(parts):

        @pl.when(pl.program_id(0) == i)
        def _():
            if i == 0 or names[i] != names[i - 1]:
                turned[...] = jnp.transpose(joined(lefts[names[i]]))
            total = low(mm(turned[...], joined(rights[i])))
            core = rank_ref[chips]
            for chip in range(chips):
                one = total[2 * chip * rows : (2 * chip + 1) * rows]
                two = total[(2 * chip + 1) * rows : (2 * chip + 2) * rows]
                mine_ref[rank_ref[chip]] = jnp.where(core == 0, one, two)
                other_ref[rank_ref[chip]] = jnp.where(core == 0, two, one)


def term_sets(rank, lefts, parts, count, after=()):
    total, depth = sum(x.shape[1] for x in lefts[0]), lefts[0][0].shape[0]
    flat = [x for left in lefts for x in left]
    rows = total // count
    chips = count // 2
    number = len(parts)
    rights, specs = [], []
    for _, given in parts:
        for x, c in given:
            rights.append(x)
            specs.append(pl.BlockSpec((depth, 512 // len(given)), lambda n, _, c=c: (0, c)))
    return pl.pallas_call(
        functools.partial(term_kernel, [p[0] for p in parts], chips, [len(left) for left in lefts], [len(p[1]) for p in parts]),
        grid_spec=pltpu.PrefetchScalarGridSpec(
            num_scalar_prefetch=1,
            grid=(number,),
            in_specs=[pl.BlockSpec(x.shape, lambda n, _: (0, 0)) for x in flat]
            + specs
            + [pl.BlockSpec(memory_space=pl.ANY)] * len(after),
            out_specs=[pl.BlockSpec((chips, rows, 512), lambda n, _: (0, n, 0))] * 2,
            scratch_shapes=[pltpu.VMEM((total, depth), jnp.bfloat16)],
        ),
        out_shape=[jax.ShapeDtypeStruct((chips, number * rows, 512), jnp.bfloat16)] * 2,
        compiler_params=pltpu.CompilerParams(vmem_limit_bytes=58 << 20),
        cost_estimate=estimate(
            flops=2 * number * total * 512 * depth, bytes_accessed=6 * number * total * 512, transcendentals=0
        ),
    )(rank, *flat, *rights, *after)


def ffn_term_kernel(parts, a_ref, du_ref, h_ref, df_ref, *rest):
    out_ref = rest[-1]
    step = pl.program_id(1)
    width = a_ref.shape[1]
    rows_in = width // out_ref.shape[0]
    rows_out = parts * rows_in
    owners = width // rows_out

    def deal(total, rows, first, at):
        for i in range(width // rows):
            out_ref[first + i, pl.ds(at, rows)] = total[i * rows : (i + 1) * rows]

    for i in range(parts):

        @pl.when(step == i)
        def _():
            total = low(lax.dot_general(a_ref[...], du_ref[...], TN, preferred_element_type=jnp.float32))
            deal(total, rows_in, 0, i * rows_in)

        @pl.when(step == parts + i)
        def _():
            total = low(lax.dot_general(h_ref[...], df_ref[...], TN, preferred_element_type=jnp.float32))
            deal(total, rows_out, i * owners, parts * rows_in)


def ffn_terms(a, du, h, df, count, block=512):
    depth, width = a.shape
    parts = du.shape[1] // width
    rows = (parts * width + h.shape[1]) // count
    per = width // block
    return pl.pallas_call(
        functools.partial(ffn_term_kernel, parts),
        grid=(per, 2 * parts),
        in_specs=[
            pl.BlockSpec((depth, width), lambda n, s: (0, 0)),
            pl.BlockSpec((depth, block), lambda n, s: (0, jnp.minimum(s, parts - 1) * per + n)),
            pl.BlockSpec((depth, width), lambda n, s: (0, jnp.maximum(s - parts, 0))),
            pl.BlockSpec((depth, block), lambda n, s: (0, n)),
        ],
        out_specs=pl.BlockSpec((count, rows, block), lambda n, s: (0, 0, n)),
        out_shape=jax.ShapeDtypeStruct((count, rows, width), jnp.bfloat16),
        compiler_params=pltpu.CompilerParams(vmem_limit_bytes=58 << 20),
        cost_estimate=estimate(
            flops=4 * parts * depth * width * width, bytes_accessed=12 * parts * width * width, transcendentals=0
        ),
    )(a, du, h, df)


def halve_kernel(split, rep_ref, mine_ref, came_ref, *rest):
    keep_ref, soon_ref, late_ref = rest[-3:]
    total = low(mine_ref[...].astype(jnp.float32) + came_ref[...].astype(jnp.float32))
    half = total.shape[1] // 2
    one, two = total[:, :half], total[:, half:]
    keep_ref[...] = jnp.where(rep_ref[0] == 0, one, two)
    send = jnp.where(rep_ref[0] == 0, two, one)

    @pl.when(pl.program_id(0) < split)
    def _():
        soon_ref[...] = send

    @pl.when(pl.program_id(0) >= split)
    def _():
        late_ref[...] = send


def halve(rep, mine, came, split, after=()):
    chips, rows, width = mine.shape
    pairs = chips // 2
    spec = pl.BlockSpec((2, rows, width), lambda i, _: (i, 0, 0))
    block = (2, rows // 2, width)
    half = rows // 2
    return pl.pallas_call(
        functools.partial(halve_kernel, split),
        grid_spec=pltpu.PrefetchScalarGridSpec(
            num_scalar_prefetch=1,
            grid=(pairs,),
            in_specs=[spec, spec] + [pl.BlockSpec(memory_space=pl.ANY)] * len(after),
            out_specs=[
                pl.BlockSpec(block, lambda i, _: (i, 0, 0)),
                pl.BlockSpec(block, lambda i, _: (jnp.minimum(i, split - 1), 0, 0)),
                pl.BlockSpec(block, lambda i, _: (jnp.maximum(i - split, 0), 0, 0)),
            ],
        ),
        out_shape=[
            jax.ShapeDtypeStruct((chips, half, width), jnp.bfloat16),
            jax.ShapeDtypeStruct((2 * split, half, width), jnp.bfloat16),
            jax.ShapeDtypeStruct((chips - 2 * split, half, width), jnp.bfloat16),
        ],
        compiler_params=pltpu.CompilerParams(vmem_limit_bytes=32 << 20),
        cost_estimate=estimate(flops=2 * mine.size, bytes_accessed=6 * mine.size, transcendentals=0),
    )(rep, mine, came, *after)


def pair_kernel(split, one_ref, soon_ref, late_ref, *rest):
    two = jnp.where(pl.program_id(0) < split, soon_ref[...], late_ref[...])
    rest[-1][...] = low(one_ref[...].astype(jnp.float32) + two.astype(jnp.float32))


def pair_sum(one, soon, late, after=()):
    chips, rows, width = one.shape
    split = soon.shape[0] // 2
    block = (2, rows, width)
    spec = pl.BlockSpec(block, lambda i: (i, 0, 0))
    return pl.pallas_call(
        functools.partial(pair_kernel, split),
        grid=(chips // 2,),
        in_specs=[
            spec,
            pl.BlockSpec(block, lambda i: (jnp.minimum(i, split - 1), 0, 0)),
            pl.BlockSpec(block, lambda i: (jnp.maximum(i - split, 0), 0, 0)),
        ]
        + [pl.BlockSpec(memory_space=pl.ANY)] * len(after),
        out_specs=spec,
        out_shape=jax.ShapeDtypeStruct(one.shape, jnp.bfloat16),
        compiler_params=pltpu.CompilerParams(vmem_limit_bytes=32 << 20),
        cost_estimate=estimate(flops=one.size, bytes_accessed=6 * one.size, transcendentals=0),
    )(one, soon, late, *after)


def hop_kernel(first, second, *rest):
    if first:
        mine_up, came_up, mine_down, came_down = rest[:4]
        up = mine_up[0].astype(jnp.float32) + came_up[0].astype(jnp.float32)
        down = mine_down[0].astype(jnp.float32) + came_down[0].astype(jnp.float32)
        rest[-2][...] = low(up)
        rest[-1][...] = low(down)
        return
    up_ref, mine_up, came_up = rest[:3]
    up = up_ref[...].astype(jnp.float32) + mine_up[0].astype(jnp.float32) + came_up[0].astype(jnp.float32)
    if not second:
        rest[-1][...] = low(up)
        return
    down_ref, mine_down, came_down = rest[3:6]
    down = down_ref[...].astype(jnp.float32) + mine_down[0].astype(jnp.float32) + came_down[0].astype(jnp.float32)
    rest[-2][...] = low(up)
    rest[-1][...] = low(down)


def hop(mine, came, up, down, up_at, down_at, after=()):
    rows, width = mine.shape[1:]
    blocks = 2 if rows % 32 == 0 else 1
    part = rows // blocks

    def pick(at):
        return pl.BlockSpec((1, part, width), lambda i: (at, i, 0))

    flat = pl.BlockSpec((part, width), lambda i: (i, 0))
    args, specs = [], []
    if up is not None:
        args.append(up)
        specs.append(flat)
    args += [mine, came]
    specs += [pick(up_at)] * 2
    if down_at is not None:
        if down is not None:
            args.append(down)
            specs.append(flat)
        args += [mine, came]
        specs += [pick(down_at)] * 2
    number = 1 if down_at is None else 2
    return pl.pallas_call(
        functools.partial(hop_kernel, up is None, down_at is not None),
        grid=(blocks,),
        in_specs=specs + [pl.BlockSpec(memory_space=pl.ANY)] * len(after),
        out_specs=[flat] * number,
        out_shape=[jax.ShapeDtypeStruct((rows, width), jnp.bfloat16)] * number,
        cost_estimate=estimate(flops=4 * rows * width, bytes_accessed=16 * rows * width, transcendentals=0),
    )(*args, *after)


def ring_walk(chips):
    half = chips // 2
    return [2 * i for i in range(half)] + [2 * i + 1 for i in reversed(range(half))]


def ring_moves(count):
    walk = ring_walk(count // 2)
    chips = len(walk)
    up = [(2 * walk[i] + c, 2 * walk[(i + 1) % chips] + c) for i in range(chips) for c in range(2)]
    down = [(b, a) for a, b in up]
    swap = [(i, i ^ 1) for i in range(count)]
    return up, down, swap


def ring_tables(count):
    chips = count // 2
    walk = ring_walk(chips)
    place = [0] * chips
    for at, chip in enumerate(walk):
        place[chip] = at
    order, rank = [], []
    for shard in range(count):
        at, core = place[shard // 2], shard % 2
        near = [walk[(at + k) % chips] for k in range(chips)]
        order.append([2 * c + core for c in near] + [2 * c + 1 - core for c in near])
        rank.append([(place[c] - at) % chips for c in range(chips)] + [core])
    me = lax.axis_index("shard")
    return jnp.array(order, jnp.int32)[me], jnp.array(rank, jnp.int32)[me]


def gather_pieces(piece, count):
    up, down, swap = ring_moves(count)
    chips = count // 2
    pieces = [piece] + [None] * (chips - 1)
    upward = downward = piece
    for step in range(1, chips // 2 + 1):
        upward = lax.ppermute(upward, "shard", up)
        pieces[chips - step] = upward
        if step < chips // 2:
            downward = lax.ppermute(downward, "shard", down)
            pieces[step] = downward
    return pieces + [lax.ppermute(p, "shard", swap) for p in pieces]


class RingGather:
    def __init__(self, piece, count):
        self.up, self.down, self.swap = ring_moves(count)
        self.chips = count // 2
        self.pieces = [piece] + [None] * (self.chips - 1)
        self.step = 0

    def hop(self, after):
        def held(part):
            return part + after[:1, :1] * 0

        last, half = self.step, self.chips // 2
        self.step += 1
        up = lax.ppermute(held(self.pieces[-last % self.chips]), "shard", self.up)
        self.pieces[self.chips - self.step] = up
        if self.step == half:
            return [up]
        down = lax.ppermute(held(self.pieces[last]), "shard", self.down)
        self.pieces[self.step] = down
        return [up, down]

    def finish(self):
        return self.pieces + [lax.ppermute(p, "shard", self.swap) for p in self.pieces]


def add_low(*values_in):
    return low(sum(v.astype(jnp.float32) for v in values_in))


def over_rep(owned):
    partner = lax.ppermute(owned, "rep", [(0, 1), (1, 0)])
    return owned.astype(jnp.float32) + partner.astype(jnp.float32)


class RingSum:
    def __init__(self, mine, other, count, flip=False):
        self.up, self.down, swap = ring_moves(count)
        self.chips = count // 2
        self.sign = 1
        if flip:
            self.up, self.down, self.sign = self.down, self.up, -1
        self.mine = mine
        self.came = lax.ppermute(other, "shard", swap)
        self.step = self.chips // 2
        self.upward = self.downward = None

    def at(self, distance):
        return (self.sign * distance) % self.chips

    def hop(self, after=()):
        half = self.chips // 2
        down_at = 1 - self.step if self.step > 1 else None
        sums = hop(
            self.mine, self.came, self.upward, self.downward if down_at is not None else None,
            self.at(self.step), None if down_at is None else self.at(down_at), after,
        )
        self.upward = lax.ppermute(sums[0], "shard", self.up)
        if down_at is not None:
            self.downward = lax.ppermute(sums[1], "shard", self.down)
        self.step -= 1
        return [sums[0]]

    def finish(self):
        owned = add_low(self.mine[0], self.came[0], self.upward, self.downward)
        return over_rep(owned)


class HalfSum:
    def __init__(self, rep, mine, other, count):
        self.rep, self.count, self.mine = rep, count, mine
        self.came = lax.ppermute(other, "shard", ring_moves(count)[2])

    def over_rep(self, split, after=()):
        swap = [(0, 1), (1, 0)]
        self.keep, soon, late = halve(self.rep, self.mine, self.came, split, after)
        self.soon, self.late = lax.ppermute(soon, "rep", swap), lax.ppermute(late, "rep", swap)
        return [self.keep]

    def over_chips(self, after=()):
        both = pair_sum(self.keep, self.soon, self.late, after).reshape(-1, self.keep.shape[2])
        groups = [list(range(core, self.count, 2)) for core in range(2)]
        self.owned = lax.psum_scatter(both, "shard", scatter_dimension=0, axis_index_groups=groups, tiled=True)
        return [both]

    def finish(self):
        partner = lax.ppermute(self.owned, "rep", [(0, 1), (1, 0)])
        first = self.rep[0] == 0
        return jnp.concatenate(
            [jnp.where(first, self.owned, partner), jnp.where(first, partner, self.owned)], axis=0
        ).astype(jnp.float32)


def scatter_sum(term):
    return over_rep(lax.psum_scatter(low(term), "shard", scatter_dimension=0, tiled=True))


class TotalSum:
    def __init__(self, values_in, count):
        self.value, self.count, self.step = values_in, count, 1

    def phase(self):
        if self.step < self.count:
            radix = min(4, self.count // self.step)
            came = [
                lax.ppermute(self.value, "shard", [(i, i ^ (k * self.step)) for i in range(self.count)])
                for k in range(1, radix)
            ]
            self.step *= radix
        else:
            came = [lax.ppermute(self.value, "rep", [(0, 1), (1, 0)])]
        self.value = self.value + sum(came[1:], came[0])
        return [self.value]


def weight_term(left, right):
    return jnp.einsum("ra,rb->ab", left, right, preferred_element_type=jnp.float32)


def body(
    tokens,
    enc_states,
    unit_ids,
    enc_ids,
    self_q,
    self_k,
    self_v,
    self_o,
    cross_q,
    cross_k,
    cross_v,
    cross_o,
    ffn_in,
    ffn_out,
    norm_gains,
    norm_biases,
    cotangent,
):
    count = lax.axis_size("shard")
    ring = count == 16
    own, width = self_q.shape
    own_out = ffn_out.shape[0]
    parts = ffn_in.shape[1] // width
    hidden = parts * width
    own_width = norm_gains.shape[1]
    x = tokens.reshape(-1, width)
    enc = enc_states.reshape(-1, width)
    cot = cotangent.reshape(-1, width)
    row_count = x.shape[0]
    bf16, f32 = jnp.bfloat16, jnp.float32

    norm_piece = jnp.concatenate([norm_gains, norm_biases], axis=0)
    in_parts = [ffn_in[:, i * width : (i + 1) * width] for i in range(parts)]
    if ring:
        order, rank = ring_tables(count)
        norm_row = jnp.pad(norm_piece.reshape(1, -1), ((0, 15), (0, width - 8 * own_width)))
        set_a = gather_pieces(jnp.concatenate([self_q, self_k, self_v, norm_row], axis=0), count)
        ring_b = RingGather(jnp.concatenate([self_o, cross_q, cross_k, cross_v, cross_o], axis=0), count)
        ring_b.hop(set_a[count // 4])
        rep = lax.axis_index("rep").astype(jnp.int32).reshape(1)
        half_c = jnp.where(rep[0] == 0, jnp.concatenate(in_parts, axis=0), ffn_out)
        set_c = [lax.all_gather(half_c, ("rep", "shard"), axis=0, tiled=True)]
        norm_rows = jnp.concatenate([p[3 * own : 3 * own + 1, : 8 * own_width] for p in set_a], axis=0)
        place = (jnp.arange(count, dtype=jnp.int32)[:, None] == order[None, :]).astype(bf16)
        norms = mm(place, norm_rows)
        norms = jnp.transpose(norms.reshape(count, 8, own_width), (1, 0, 2)).reshape(8, width)
        kinds = ("ring", "ring", "tiled")
    else:
        order = jnp.zeros((1,), jnp.int32)

        def whole(part):
            return lax.all_gather(part, "shard", axis=0, tiled=True)

        set_a = [jnp.concatenate([whole(w) for w in (self_q, self_k, self_v)], axis=0)]
        set_b = [jnp.concatenate([whole(w) for w in (self_o, cross_q, cross_k, cross_v, cross_o)], axis=0)]
        set_c = [jnp.concatenate([whole(w) for w in in_parts + [ffn_out]], axis=0)]
        norms = lax.all_gather(norm_piece, "shard", axis=1, tiled=True).astype(f32)
        kinds = ("flat", "flat", "flat")
    plan_a = [(kinds[0], i * own, own, i * width, 0, count) for i in range(3)]
    plan_b = [(kinds[1], i * own, own, i * width, 0, count) for i in range(5)]
    plan_c = [(kinds[2], i * own, own, i * width, parts * own, count) for i in range(parts)]
    plan_c.append(("flat", 0, own_out, parts * width, 0, count))
    sems = pltpu.SemaphoreType.DMA
    square = 2 * row_count * width * width

    unit_extra, enc_extra = key_extras(unit_ids[0]), key_extras(enc_ids[0])
    query_extra = query_extras(unit_ids[0])
    self_windows = windows(unit_ids[0], unit_ids[0], 256, 256, True)
    cross_windows = windows(unit_ids[0], enc_ids[0], 256, 256, False)
    a1, q1, k1, v1 = by_rows(
        functools.partial(first_kernel, plan_a, len(set_a)), order, [x], norms, set_a,
        [(width, bf16)] * 4, False,
        [pltpu.VMEM((3, width, width), bf16), sems((3,))], 3 * square,
    )
    pairs = width // 128
    self_args = (q1, k1, v1, query_extra, unit_extra, self_windows, True)
    if ring:
        o1_low, log1_low = attend_forward(*self_args, (0, pairs // 2))
        ring_b.hop(o1_low)
        o1_high, log1_high = attend_forward(*self_args, (pairs // 2, pairs), [o1_low])
        ring_b.hop(o1_high)
        ring_b.hop(o1_high)
        set_b = ring_b.finish()
    else:
        o1_low, log1_low = attend_forward(*self_args, (0, pairs // 2))
        o1_high, log1_high = attend_forward(*self_args, (pairs // 2, pairs))
    o1 = [o1_low, o1_high]
    r1, a2, q2, k2, v2 = by_rows(
        functools.partial(second_kernel, plan_b[:4], len(set_b), 2), order, o1 + [x, enc], norms, set_b,
        [(width, f32)] + [(width, bf16)] * 4, False,
        [pltpu.VMEM((4, width, width), bf16), sems((4,))], 4 * square,
    )
    o2, log2 = attend_forward(q2, k2, v2, query_extra, enc_extra, cross_windows, False, (0, pairs))
    out, a3, h, df, du, dr2, dc2, do2, terms_three = by_rows(
        functools.partial(third_kernel, plan_b[4:] + plan_c, len(set_b), len(set_c), 1), order, [o2, r1, cot], norms, set_b + set_c,
        [(width, bf16), (width, bf16), (hidden, bf16), (width, bf16), (hidden, bf16), (width, f32), (width, bf16), (width, bf16)], True,
        [
            pltpu.VMEM((width, width), bf16),
            pltpu.VMEM((parts, width, width), bf16),
            pltpu.VMEM((hidden, width), bf16),
            pltpu.VMEM((256, hidden), f32),
            sems((parts + 2,)),
        ],
        (2 + 4 * parts) * square,
    )

    cross_args = (q2, k2, v2, o2, do2, log2, enc_extra, cross_windows, False)
    if ring:
        plain = jnp.concatenate([jnp.arange(count // 2, dtype=jnp.int32), rank[-1:]])
        ffn_set = ffn_terms(a3, du, h, df, count)
        ffn_set = lax.psum_scatter(ffn_set.reshape(-1, width), "shard", scatter_dimension=0, tiled=True)
    else:
        grad_in, grad_out = scatter_sum(weight_term(a3, du)), scatter_sum(weight_term(h, df))
    dq2, dk2, dv2 = attend_backward(*cross_args, (0, pairs))
    fourth = functools.partial(
        by_rows, functools.partial(fourth_kernel, plan_b[:4], len(set_b), 1), order, [dq2, dk2, dv2, r1, dr2], norms, set_b,
        [(width, f32), (width, bf16), (width, bf16), (width, f32)], True,
        [pltpu.VMEM((4, width, width), bf16), sems((4,))], 4 * square,
    )

    half = pairs // 2

    def self_backward(i, after):
        return attend_backward(
            q1, k1, v1, o1[i], do1, (log1_low, log1_high)[i], unit_extra, self_windows, True,
            (i * half, (i + 1) * half), i * half, after,
        )

    def fifth(groups, after, part=(0, 1), into=None):
        dq1, dk1, dv1 = ([g[i] for g in groups] for i in range(3))
        return by_rows(
            functools.partial(fifth_kernel, plan_a, len(set_a), len(groups)), order, dq1 + dk1 + dv1 + [x, dr1], norms, set_a,
            [(width, f32)], True,
            [pltpu.VMEM((3, width, width), bf16), sems((3,))], 3 * square // part[1], after, part=part, into=into,
        )

    if ring:
        sums_b = HalfSum(
            rep,
            *term_sets(
                plain, [(o2,), (a2,), (enc,)],
                [(i, [(g, c)]) for i, g in ((0, dc2), (1, dq2), (2, dk2), (2, dv2)) for c in range(2)], count,
            ),
            count,
        )
        dr1, dc1, do1, grad_enc, terms_two = fourth([sums_b.mine])
        groups = [self_backward(0, sums_b.over_rep(2, [dc1]))]
        groups.append(self_backward(1, [groups[0][0], sums_b.soon]))
        sums_a = RingSum(
            *term_sets(
                rank, [tuple(o1), (a1,)],
                [(0, [(dc1, c)]) for c in range(2)] + [(1, [(g[i], 0)]) for i in range(3) for g in groups], count, [sums_b.late],
            ),
            count, True,
        )
        grad_x, terms_one = fifth(groups, [sums_a.mine])
        norm_sum = TotalSum(terms_one + terms_two + terms_three, count)
        last = sums_b.over_chips(sums_a.hop([grad_x]) + [ffn_set])
        for _ in range(count // 4 - 1):
            last = sums_a.hop(last + norm_sum.phase())
        ffn_set = over_rep(ffn_set)
        grad_in = jnp.concatenate([ffn_set[i * own : (i + 1) * own] for i in range(parts)], axis=1)
        grad_out = ffn_set[parts * own :]
        grad_a, grad_b = sums_a.finish(), sums_b.finish()

        def columns(array, places):
            return jnp.concatenate([array[i * own : (i + 1) * own] for i in places], axis=1)

        grad_co, grad_cq, grad_ck, grad_cv = (columns(grad_b, (2 * w, 2 * w + 1)) for w in range(4))
        grad_so, grad_sq, grad_sk, grad_sv = (columns(grad_a, (2 * w, 2 * w + 1)) for w in range(4))
    else:
        dr1, dc1, do1, grad_enc, terms_two = fourth()
        groups = [self_backward(i, ()) for i in range(2)]
        dq1, dk1, dv1 = (jnp.concatenate([g[i] for g in groups], axis=1) for i in range(3))
        grad_x, terms_one = fifth(groups, ())
        norm_sum = TotalSum(terms_one + terms_two + terms_three, count)
        while norm_sum.step < count:
            norm_sum.phase()
        norm_sum.phase()
        grad_co, grad_cq, grad_ck, grad_cv, grad_so, grad_sq, grad_sk, grad_sv = (
            scatter_sum(weight_term(a, b))
            for a, b in (
                (o2, dc2), (a2, dq2), (enc, dk2), (enc, dv2), (jnp.concatenate(o1, axis=1), dc1), (a1, dq1), (a1, dk1), (a1, dv1)
            )
        )
    norm_sum = norm_sum.value
    norm_sum = lax.dynamic_slice_in_dim(norm_sum, lax.axis_index("shard") * own_width, own_width, 1)
    return (
        out.reshape(tokens.shape),
        grad_x.reshape(tokens.shape),
        grad_enc.reshape(enc_states.shape),
        grad_sq,
        grad_sk,
        grad_sv,
        grad_so,
        grad_cq,
        grad_ck,
        grad_cv,
        grad_co,
        grad_in,
        grad_out,
        norm_sum[:4],
        norm_sum[4:],
    )


def solution(mesh):
    return jax.shard_map(
        body,
        mesh=mesh,
        in_specs=(
            P(("rep", "shard"), None, None),
            P(("rep", "shard"), None, None),
            P(("rep", "shard"), None),
            P(("rep", "shard"), None),
            P("shard", None),
            P("shard", None),
            P("shard", None),
            P("shard", None),
            P("shard", None),
            P("shard", None),
            P("shard", None),
            P("shard", None),
            P("shard", None),
            P("shard", None),
            P(None, "shard"),
            P(None, "shard"),
            P(("rep", "shard"), None, None),
        ),
        out_specs=(
            P(("rep", "shard"), None, None),
            P(("rep", "shard"), None, None),
            P(("rep", "shard"), None, None),
            P("shard", None),
            P("shard", None),
            P("shard", None),
            P("shard", None),
            P("shard", None),
            P("shard", None),
            P("shard", None),
            P("shard", None),
            P("shard", None),
            P("shard", None),
            P(None, "shard"),
            P(None, "shard"),
        ),
        check_vma=False,
    )
```

```python
import functools
import math

import jax
import jax.numpy as jnp
from jax import lax
from jax.experimental import pallas as pl
from jax.experimental.pallas import tpu as pltpu
from jax.sharding import PartitionSpec as P

HEADS = 16
HEAD = 64


eps_norm = 1e-05


COST = 4


def estimate(flops, bytes_accessed, transcendentals):
    return pl.CostEstimate(flops=flops // 8, bytes_accessed=bytes_accessed // 8, transcendentals=0)
BIG = 1e30
NT = (((1,), (1,)), ((), ()))
TN = (((0,), (0,)), ((), ()))


def key_extras(ids):
    lane = jnp.arange(128)[None, :] % 64
    return jnp.where(lane < 8, (ids[:, None] != lane).astype(jnp.bfloat16), ((lane >= 8) & (lane < 11)).astype(jnp.bfloat16))


def query_extras(ids):
    lane = jnp.arange(128)[None, :] % 64
    return jnp.where((lane < 8) & (ids[:, None] == lane), -BIG, 0.0).astype(jnp.bfloat16)


def windows(unit_ids, key_ids, bq, bk, causal):
    n = key_ids.shape[0]
    nq = unit_ids.shape[0] // bq
    blocks = unit_ids.reshape(nq, bq)
    low = jnp.sum((key_ids[None, :] < blocks[:, :1]).astype(jnp.int32), axis=1)
    if causal:
        end = (jnp.arange(nq, dtype=jnp.int32) + 1) * bq
        count = (end - low + bk - 1) // bk
        start = end - count * bk
    else:
        end = jnp.sum((key_ids[None, :] <= blocks[:, -1:]).astype(jnp.int32), axis=1)
        low = low // 16 * 16
        count = (end - low + bk - 1) // bk
        start = jnp.minimum(low, n - count * bk)
    return jnp.concatenate([start, count])


def attend_forward_kernel(bq, bk, causal, hp, norm, win_ref, q_ref, k_ref, v_ref, qx_ref, kx_ref, *rest):
    o_ref, qe_ref, ka = rest[-3:]
    L, N = q_ref.shape[0], k_ref.shape[0]
    nq = L // bq
    lane = lax.broadcasted_iota(jnp.int32, (1, 128), 1)
    first = lane < 64
    part = lane % 64
    for g in range(hp):
        kp = k_ref[:, g*128:(g+1)*128]
        ka[2*g] = jnp.where(first, kp, kx_ref[...])
        ka[2*g+1] = jnp.where(first, kx_ref[...], kp)
    row = lax.broadcasted_iota(jnp.int32, (128, 1), 0)
    rpart = row % 64
    zero = jnp.zeros((1, 128), jnp.bfloat16)

    def one(i, W):
        rows = pl.ds(pl.multiple_of(i * bq, bq), bq)
        win = pl.ds(pl.multiple_of(win_ref[i], 16), W)
        xb = qx_ref[rows, :]
        ss = []
        for h in range(2*hp):
            g = h // 2
            qb = q_ref[rows, g*128:(g+1)*128]
            qa = jnp.where(first, qb, xb) if h % 2 == 0 else jnp.where(first, xb, qb)
            s = lax.dot_general(ka[h, win, :], qa, NT, preferred_element_type=jnp.float32)
            if causal:
                tri = lax.broadcasted_iota(jnp.int32, (bq, bq), 0) <= lax.broadcasted_iota(jnp.int32, (bq, bq), 1)
                d = jnp.where(tri, s[W - bq:, :], -BIG)
                s = d if W == bq else jnp.concatenate([s[: W - bq, :], d], axis=0)
            ss.append(s)
        outs, invs, lses = [], [], []
        for h in range(2*hp):
            g = h // 2
            s = ss[h]
            m = jnp.max(s, axis=0, keepdims=True)
            p = jnp.exp(s - m)
            l = jnp.sum(p, axis=0, keepdims=True)
            inv = 1.0 / l
            if norm: p = p * inv
            vw = v_ref[win, g*128:(g+1)*128]
            vw = jnp.where(first, vw, zero) if h % 2 == 0 else jnp.where(first, zero, vw)
            outs.append(lax.dot_general(vw, p.astype(jnp.bfloat16), TN, preferred_element_type=jnp.float32)); invs.append(inv)
            neg = -(m + jnp.log(l))
            hi = neg.astype(jnp.bfloat16).astype(jnp.float32)
            mid = (neg - hi).astype(jnp.bfloat16).astype(jnp.float32)
            lo = neg - hi - mid
            lses.append((hi, mid, lo))
        for g in range(hp):
            o = outs[2*g] + outs[2*g+1]
            if not norm:
                o = o * jnp.where(row < 64, invs[2*g], invs[2*g+1])
            o = jnp.transpose(o)
            o_ref[rows, g*128:(g+1)*128] = o.astype(jnp.bfloat16)
            a, b = lses[2*g], lses[2*g+1]
            e = jnp.where(row < 64, jnp.where(rpart == 8, b[0], jnp.where(rpart == 9, b[1], b[2])), jnp.where(rpart == 8, a[0], jnp.where(rpart == 9, a[1], a[2])))
            e = jnp.transpose(jnp.where((rpart >= 8) & (rpart < 11), e, 0.0))
            qe_ref[rows, g*128:(g+1)*128] = jnp.where(part < 8, xb.astype(jnp.float32), e).astype(jnp.bfloat16)

    def step(i, c):
        for j in range(1, N // bk + 1):
            @pl.when(win_ref[nq + i] == j)
            def _():
                one(i, j * bk)
        return c

    lax.fori_loop(0, nq, step, 0)

def attend_forward(q, k, v, qx, kx, win, causal, pairs, after=(), bq=256, bk=256, hp=4):
    L, N = q.shape[0], k.shape[0]
    w = 128 * hp
    start, number = pairs[0] // hp, (pairs[1] - pairs[0]) // hp
    col = lambda n: pl.BlockSpec((n, w), lambda p, _: (0, start + p))
    own = lambda n: pl.BlockSpec((n, w), lambda p, _: (0, p))
    fix = lambda n: pl.BlockSpec((n, 128), lambda p, _: (0, 0))
    return pl.pallas_call(
        functools.partial(attend_forward_kernel, bq, bk, causal, hp, True),
        grid_spec=pltpu.PrefetchScalarGridSpec(
            num_scalar_prefetch=1,
            grid=(number,),
            in_specs=[col(L), col(N), col(N), fix(L), fix(N)] + [pl.BlockSpec(memory_space=pl.ANY)] * len(after),
            out_specs=[own(L), own(L)],
            scratch_shapes=[pltpu.VMEM((2 * hp, N, 128), jnp.bfloat16)],
        ),
        out_shape=[jax.ShapeDtypeStruct((L, number * w), jnp.bfloat16)] * 2,
        compiler_params=pltpu.CompilerParams(vmem_limit_bytes=56 << 20),
        cost_estimate=estimate(
            flops=COST * 2 * 2 * L * N * number * w, bytes_accessed=10 * L * number * w, transcendentals=0
        ),
    )(win, q, k, v, qx, kx, *after)


def attend_backward_kernel(bq, bk, causal, hp, win_ref, q_ref, k_ref, v_ref, o_ref, do_ref, qe_ref, kx_ref, *rest):
    dq_ref, dk_ref, dv_ref, ka, va, dka, dva = rest[-7:]
    L, N = q_ref.shape[0], k_ref.shape[0]
    nq = L // bq
    lane = lax.broadcasted_iota(jnp.int32, (1, 128), 1)
    first = lane < 64
    part = lane % 64
    ones = jnp.broadcast_to(jnp.where(part < 3, 1.0, 0.0).astype(jnp.bfloat16), (N, 128))
    for g in range(hp):
        c = slice(g*128,(g+1)*128)
        ka[2*g] = jnp.where(first, k_ref[:, c], kx_ref[...])
        ka[2*g+1] = jnp.where(first, kx_ref[...], k_ref[:, c])
        va[2*g] = jnp.where(first, v_ref[:, c], ones)
        va[2*g+1] = jnp.where(first, ones, v_ref[:, c])
    dka[...] = jnp.zeros_like(dka)
    dva[...] = jnp.zeros_like(dva)
    zero = jnp.zeros((1, 128), jnp.bfloat16)

    def one(i, W):
        rows = pl.ds(pl.multiple_of(i * bq, bq), bq)
        win = pl.ds(pl.multiple_of(win_ref[i], 16), W)
        S = []
        for g in range(hp):
            c = slice(g*128,(g+1)*128)
            qb, xb, dob = q_ref[rows, c], qe_ref[rows, c], do_ref[rows, c]
            prod = dob.astype(jnp.float32) * o_ref[rows, c].astype(jnp.float32)
            for h in range(2):
                mine = first if h == 0 else jnp.logical_not(first)
                neg = -jnp.sum(jnp.where(mine, prod, 0.0), axis=1, keepdims=True)
                hi = neg.astype(jnp.bfloat16).astype(jnp.float32)
                mid = (neg - hi).astype(jnp.bfloat16).astype(jnp.float32)
                lo = neg - hi - mid
                de = jnp.where(part == 0, hi, jnp.where(part == 1, mid, jnp.where(part == 2, lo, 0.0))).astype(jnp.bfloat16)
                qa = jnp.where(mine, qb, xb)
                da = jnp.where(mine, dob, de)
                s = lax.dot_general(ka[2*g+h, win, :], qa, NT, preferred_element_type=jnp.float32)
                dp = lax.dot_general(va[2*g+h, win, :], da, NT, preferred_element_type=jnp.float32)
                S.append((s, dp))
        for g in range(hp):
            c = slice(g*128,(g+1)*128)
            qb, dob = q_ref[rows, c], do_ref[rows, c]
            ps, dss = [], []
            for h in range(2):
                s, dp = S[2*g+h]
                if causal:
                    tri = lax.broadcasted_iota(jnp.int32, (bq, bq), 0) <= lax.broadcasted_iota(jnp.int32, (bq, bq), 1)
                    d = jnp.where(tri, s[W - bq:, :], -BIG)
                    s = d if W == bq else jnp.concatenate([s[: W - bq, :], d], axis=0)
                p = jnp.exp(s)
                dss.append((p * dp).astype(jnp.bfloat16))
                ps.append(p.astype(jnp.bfloat16))
            docat = jnp.concatenate([jnp.where(first, dob, zero), jnp.where(first, zero, dob)], axis=0)
            qcat = jnp.concatenate([jnp.where(first, qb, zero), jnp.where(first, zero, qb)], axis=0)
            dva[win, c] += jnp.dot(jnp.concatenate(ps, axis=1), docat, preferred_element_type=jnp.float32)
            dka[win, c] += jnp.dot(jnp.concatenate(dss, axis=1), qcat, preferred_element_type=jnp.float32)
            kw = k_ref[win, c]
            k0, k1 = jnp.where(first, kw, zero), jnp.where(first, zero, kw)
            turned = lax.dot_general(k0, dss[0], TN, preferred_element_type=jnp.float32)
            turned = turned + lax.dot_general(k1, dss[1], TN, preferred_element_type=jnp.float32)
            dq = jnp.transpose(turned)
            dq_ref[rows, c] = (dq * 0.125).astype(jnp.bfloat16)

    def step(i, c):
        for j in range(1, N // bk + 1):
            @pl.when(win_ref[nq + i] == j)
            def _():
                one(i, j * bk)
        return c

    lax.fori_loop(0, nq, step, 0)
    dk_ref[...] = dka[...].astype(jnp.bfloat16)
    dv_ref[...] = dva[...].astype(jnp.bfloat16)

def attend_backward(q, k, v, o, do, qe, kx, win, causal, pairs, base=0, after=(), bq=256, bk=256, hp=2):
    L, N = q.shape[0], k.shape[0]
    w = 128 * hp
    start, number, base = pairs[0] // hp, (pairs[1] - pairs[0]) // hp, base // hp
    col = lambda n: pl.BlockSpec((n, w), lambda p, _: (0, start + p))
    own = lambda n: pl.BlockSpec((n, w), lambda p, _: (0, p))
    held = pl.BlockSpec((L, w), lambda p, _: (0, start - base + p))
    fix = lambda n: pl.BlockSpec((n, 128), lambda p, _: (0, 0))
    return pl.pallas_call(
        functools.partial(attend_backward_kernel, bq, bk, causal, hp),
        grid_spec=pltpu.PrefetchScalarGridSpec(
            num_scalar_prefetch=1,
            grid=(number,),
            in_specs=[col(L), col(N), col(N), held, col(L), held, fix(N)]
            + [pl.BlockSpec(memory_space=pl.ANY)] * len(after),
            out_specs=[own(L), own(N), own(N)],
            scratch_shapes=[pltpu.VMEM((2 * hp, N, 128), jnp.bfloat16)] * 2 + [pltpu.VMEM((N, w), jnp.float32)] * 2,
        ),
        out_shape=[jax.ShapeDtypeStruct((L, number * w), jnp.bfloat16)]
        + [jax.ShapeDtypeStruct((N, number * w), jnp.bfloat16)] * 2,
        compiler_params=pltpu.CompilerParams(vmem_limit_bytes=58 << 20),
        cost_estimate=estimate(
            flops=COST * 5 * 2 * L * N * number * w, bytes_accessed=16 * L * number * w, transcendentals=0
        ),
    )(win, q, k, v, o, do, qe, kx, *after)


def fetch(plan, refs, order_ref, dst, sem):
    kind, offset, rows, flat, piece_rows, count = plan
    if kind == "flat":
        part = rows * count // 16
        for j in range(16):
            pltpu.make_async_copy(refs[0].at[pl.ds(flat + j * part, part)], dst.at[pl.ds(j * part, part)], sem).start()
        return
    for j in range(count):
        if kind == "ring":
            src = refs[j].at[pl.ds(offset, rows)]
            at = pl.multiple_of(order_ref[j] * rows, 16)
        else:
            src = refs[0].at[pl.ds(j * piece_rows + offset, rows)]
            at = j * rows
        pltpu.make_async_copy(src, dst.at[pl.ds(at, rows)], sem).start()


def arrived(dst, sem):
    pltpu.make_async_copy(dst, dst, sem).wait()


def normed(values_in):
    centre = values_in - jnp.mean(values_in, axis=-1, keepdims=True)
    spread = jnp.mean(centre * centre, axis=-1, keepdims=True)
    scale = lax.rsqrt(spread + eps_norm)
    return centre * scale, scale


def normed_back(unit, scale, gain, grad_out):
    grad_unit = grad_out * gain
    inner = jnp.mean(grad_unit * unit, axis=-1, keepdims=True)
    return (grad_unit - jnp.mean(grad_unit, axis=-1, keepdims=True) - unit * inner) * scale


def mm(left, right):
    return jnp.dot(left, right, preferred_element_type=jnp.float32)


def mm_back(left, right):
    return lax.dot_general(left, right, NT, preferred_element_type=jnp.float32)


def low(values_in):
    return values_in.astype(jnp.bfloat16)


def term_rows(refs, at, values_in):
    refs[at : at + 1, :] += jnp.sum(values_in, axis=0, keepdims=True)


def first_kernel(plans, n_refs, order_ref, x_ref, norm_ref, *rest):
    refs, (a_ref, q_ref, k_ref, v_ref, w, sem) = rest[:n_refs], rest[-6:]

    @pl.when(pl.program_id(0) == 0)
    def _():
        for i in range(3):
            fetch(plans[i], refs, order_ref, w.at[i], sem.at[i])
        for i in range(3):
            arrived(w.at[i], sem.at[i])

    unit, _ = normed(x_ref[...].astype(jnp.float32))
    a = low(unit * norm_ref[0:1, :] + norm_ref[4:5, :])
    a_ref[...] = a
    q_ref[...] = low(mm(a, w[0]) * 0.125)
    k_ref[...] = low(mm(a, w[1]))
    v_ref[...] = low(mm(a, w[2]))


def joined(refs):
    return refs[0][...] if len(refs) == 1 else jnp.concatenate([r[...] for r in refs], axis=1)


def second_kernel(plans, n_refs, n_o, order_ref, *rest):
    o_refs, (x_ref, e_ref, norm_ref), rest = rest[:n_o], rest[n_o : n_o + 3], rest[n_o + 3 :]
    refs, (r_ref, a_ref, q_ref, k_ref, v_ref, w, sem) = rest[:n_refs], rest[-7:]

    @pl.when(pl.program_id(0) == 0)
    def _():
        for i in range(4):
            fetch(plans[i], refs, order_ref, w.at[i], sem.at[i])
        for i in range(4):
            arrived(w.at[i], sem.at[i])

    r = x_ref[...].astype(jnp.float32) + mm(joined(o_refs), w[0])
    r_ref[...] = r
    k_ref[...] = low(mm(e_ref[...], w[2]))
    v_ref[...] = low(mm(e_ref[...], w[3]))
    unit, _ = normed(r)
    a = low(unit * norm_ref[1:2, :] + norm_ref[5:6, :])
    a_ref[...] = a
    q_ref[...] = low(mm(a, w[1]) * 0.125)


def third_kernel(plans, n_b, n_c, n_o, order_ref, *rest):
    o_refs, (r_ref, cot_ref, norm_ref), rest = rest[:n_o], rest[n_o : n_o + 3], rest[n_o + 3 :]
    refs_b, refs_c = rest[:n_b], rest[n_b : n_b + n_c]
    (out_ref, a_ref, h_ref, df_ref, du_ref, dr_ref, dc_ref, do_ref, term_ref, wc, wi, wo, slope, sem) = rest[-14:]
    parts = wi.shape[0]
    first = pl.program_id(0) == 0

    @pl.when(first)
    def _():
        fetch(plans[0], refs_b, order_ref, wc, sem.at[0])
        for i in range(parts):
            fetch(plans[1 + i], refs_c, order_ref, wi.at[i], sem.at[1 + i])
        fetch(plans[1 + parts], refs_c, order_ref, wo, sem.at[1 + parts])
        term_ref[...] = jnp.zeros_like(term_ref)
        arrived(wc, sem.at[0])

    r2 = r_ref[...] + mm(joined(o_refs), wc[...])
    unit2, scale2 = normed(r2)
    a3 = low(unit2 * norm_ref[2:3, :] + norm_ref[6:7, :])
    a_ref[...] = a3

    @pl.when(first)
    def _():
        for i in range(parts):
            arrived(wi.at[i], sem.at[1 + i])
        arrived(wo, sem.at[1 + parts])

    width = wi.shape[2]
    r3 = r2
    for i in range(parts):
        cols = slice(i * width, (i + 1) * width)
        u = mm(a3, wi[i])
        half = 0.5 * (1.0 + lax.erf(u * (1.0 / math.sqrt(2.0))))
        h = low(u * half)
        h_ref[:, cols] = h
        slope[:, cols] = half + u * jnp.exp(-0.5 * u * u) * (1.0 / math.sqrt(2.0 * math.pi))
        r3 = r3 + mm(h, wo[cols, :])
    unit3, scale3 = normed(r3)
    out_ref[...] = low(unit3 * norm_ref[3:4, :] + norm_ref[7:8, :])
    cot = cot_ref[...].astype(jnp.float32)
    term_rows(term_ref, 3, cot * unit3)
    term_rows(term_ref, 7, cot)
    dr3 = normed_back(unit3, scale3, norm_ref[3:4, :], cot)
    df = low(dr3)
    df_ref[...] = df
    da3 = jnp.zeros_like(dr3)
    for i in range(parts):
        cols = slice(i * width, (i + 1) * width)
        du = low(mm_back(df, wo[cols, :]) * slope[:, cols])
        du_ref[:, cols] = du
        da3 = da3 + mm_back(du, wi[i])
    term_rows(term_ref, 2, da3 * unit2)
    term_rows(term_ref, 6, da3)
    dr2 = dr3 + normed_back(unit2, scale2, norm_ref[2:3, :], da3)
    dr_ref[...] = dr2
    dc = low(dr2)
    dc_ref[...] = dc
    do_ref[...] = low(mm_back(dc, wc[...]))


def fourth_kernel(plans, n_refs, order_ref, dq_ref, r_ref, dr_ref, norm_ref, *rest):
    refs, (dx_ref, dc_ref, do_ref, term_ref, w, sem) = rest[:n_refs], rest[-6:]

    @pl.when(pl.program_id(0) == 0)
    def _():
        for i in range(2):
            fetch(plans[i], refs, order_ref, w.at[i], sem.at[i])
        for i in range(2):
            arrived(w.at[i], sem.at[i])
        term_ref[...] = jnp.zeros_like(term_ref)

    da = mm_back(dq_ref[...], w[1])
    unit, scale = normed(r_ref[...])
    term_rows(term_ref, 1, da * unit)
    term_rows(term_ref, 5, da)
    dx = dr_ref[...] + normed_back(unit, scale, norm_ref[1:2, :], da)
    dx_ref[...] = dx
    dc = low(dx)
    dc_ref[...] = dc
    do_ref[...] = low(mm_back(dc, w[0]))


def enc_kernel(plans, n_refs, order_ref, dk_ref, dv_ref, norm_ref, *rest):
    refs, (de_ref, w, sem) = rest[:n_refs], rest[-3:]

    @pl.when(pl.program_id(0) == 0)
    def _():
        for i in range(2):
            fetch(plans[i], refs, order_ref, w.at[i], sem.at[i])
        for i in range(2):
            arrived(w.at[i], sem.at[i])

    de_ref[...] = mm_back(dk_ref[...], w[0]) + mm_back(dv_ref[...], w[1])


def fifth_kernel(plans, n_refs, n_g, order_ref, *rest):
    dq_refs, dk_refs, dv_refs = (rest[i * n_g : (i + 1) * n_g] for i in range(3))
    (x_ref, dr_ref, norm_ref), rest = rest[3 * n_g : 3 * n_g + 3], rest[3 * n_g + 3 :]
    refs, (dx_ref, term_ref, w, sem) = rest[:n_refs], rest[-4:]

    @pl.when(pl.program_id(0) == 0)
    def _():
        for i in range(3):
            fetch(plans[i], refs, order_ref, w.at[i], sem.at[i])
        for i in range(3):
            arrived(w.at[i], sem.at[i])
        term_ref[...] = jnp.zeros_like(term_ref)

    da = mm_back(joined(dq_refs), w[0]) + mm_back(joined(dk_refs), w[1]) + mm_back(joined(dv_refs), w[2])
    unit, scale = normed(x_ref[...].astype(jnp.float32))
    term_rows(term_ref, 0, da * unit)
    term_rows(term_ref, 4, da)
    dx_ref[...] = dr_ref[...] + normed_back(unit, scale, norm_ref[0:1, :], da)


def by_rows(kernel, order, row_inputs, norms, piece_refs, row_outputs, terms, scratch, flops, after=(), block=256, part=(0, 1), into=None):
    rows = row_inputs[0].shape[0]
    steps = rows // block // part[1]
    first = part[0] * steps
    piece_refs = list(piece_refs) + list(after) + ([] if into is None else [into])
    aliases = {} if into is None else {1 + len(row_inputs) + len(piece_refs): 0}

    def spec(width):
        return pl.BlockSpec((block, width), lambda i, _: (first + i, 0))

    def fixed(shape):
        return pl.BlockSpec(shape, lambda i, _: (0, 0))

    out_shape = [jax.ShapeDtypeStruct((rows, w), t) for w, t in row_outputs]
    out_specs = [spec(w) for w, _ in row_outputs]
    if terms:
        out_shape.append(jax.ShapeDtypeStruct(norms.shape, jnp.float32))
        out_specs.append(fixed(norms.shape))
    moved = sum(x.size * x.dtype.itemsize for x in row_inputs) + sum(rows * w * t.dtype.itemsize if hasattr(t, "dtype") else rows * w * jnp.dtype(t).itemsize for w, t in row_outputs)
    return pl.pallas_call(
        kernel,
        grid_spec=pltpu.PrefetchScalarGridSpec(
            num_scalar_prefetch=1,
            grid=(steps,),
            in_specs=[spec(x.shape[1]) for x in row_inputs]
            + [fixed(norms.shape)]
            + [pl.BlockSpec(memory_space=pl.ANY)] * len(piece_refs),
            out_specs=out_specs,
            scratch_shapes=scratch,
        ),
        out_shape=out_shape,
        input_output_aliases=aliases,
        compiler_params=pltpu.CompilerParams(vmem_limit_bytes=58 << 20),
        cost_estimate=estimate(flops=flops, bytes_accessed=moved, transcendentals=0),
    )(order, *row_inputs, norms, *piece_refs)


def term_kernel(names, chips, n_left, n_right, n_extra, rank_ref, *rest):
    parts = len(names)
    extra, rest = rest[:n_extra], rest[n_extra:]
    flat, rest = rest[: sum(n_left)], rest[sum(n_left) :]
    lefts = [flat[sum(n_left[:i]) : sum(n_left[: i + 1])] for i in range(len(n_left))]
    rights = [rest[sum(n_right[:i]) : sum(n_right[: i + 1])] for i in range(parts)]
    mine_ref, other_ref, turned = rest[-3:]
    rows = turned.shape[0] // (2 * chips)

    def deal(chip, at, number, one, two):
        core = rank_ref[chips]
        mine_ref[rank_ref[chip], at : at + number] = jnp.where(core == 0, one, two)
        other_ref[rank_ref[chip], at : at + number] = jnp.where(core == 0, two, one)

    for i in range(parts):

        @pl.when(pl.program_id(0) == i)
        def _():
            if i == 0 or names[i] != names[i - 1]:
                turned[...] = jnp.transpose(joined(lefts[names[i]]))
            total = low(mm(turned[...], joined(rights[i])))
            for chip in range(chips):
                one = total[2 * chip * rows : (2 * chip + 1) * rows]
                two = total[(2 * chip + 1) * rows : (2 * chip + 2) * rows]
                deal(chip, i * rows if extra else 0, rows, one, two)
            if extra and i == 0:
                terms = extra[0][...] + extra[1][...] + extra[2][...]
                empty = jnp.zeros((8, 512 - rows), jnp.float32)
                for chip in range(chips):
                    one, two = (
                        low(jnp.concatenate([jnp.concatenate([terms[:, s * rows : (s + 1) * rows], empty], axis=1), jnp.zeros((24, 512), jnp.float32)], axis=0))
                        for s in (2 * chip, 2 * chip + 1)
                    )
                    deal(chip, parts * rows, 32, one, two)


def term_sets(rank, lefts, parts, count, after=(), extra=()):
    total, depth = sum(x.shape[1] for x in lefts[0]), lefts[0][0].shape[0]
    flat = [x for left in lefts for x in left]
    rows = total // count
    chips = count // 2
    number = len(parts)
    all_rows = number * rows + (32 if extra else 0)
    rights, specs = [], []
    for _, given in parts:
        for x, c in given:
            rights.append(x)
            specs.append(pl.BlockSpec((depth, 512 // len(given)), lambda n, _, c=c: (0, c)))
    return pl.pallas_call(
        functools.partial(term_kernel, [p[0] for p in parts], chips, [len(left) for left in lefts], [len(p[1]) for p in parts], len(extra)),
        grid_spec=pltpu.PrefetchScalarGridSpec(
            num_scalar_prefetch=1,
            grid=(number,),
            in_specs=[pl.BlockSpec(x.shape, lambda n, _: (0, 0)) for x in [*extra, *flat]]
            + specs
            + [pl.BlockSpec(memory_space=pl.ANY)] * len(after),
            out_specs=[pl.BlockSpec((chips, all_rows, 512), lambda n, _: (0, 0, 0)) if extra else pl.BlockSpec((chips, rows, 512), lambda n, _: (0, n, 0))] * 2,
            scratch_shapes=[pltpu.VMEM((total, depth), jnp.bfloat16)],
        ),
        out_shape=[jax.ShapeDtypeStruct((chips, all_rows, 512), jnp.bfloat16)] * 2,
        compiler_params=pltpu.CompilerParams(vmem_limit_bytes=58 << 20),
        cost_estimate=estimate(
            flops=2 * number * total * 512 * depth, bytes_accessed=6 * number * total * 512, transcendentals=0
        ),
    )(rank, *extra, *flat, *rights, *after)


def ffn_term_kernel(parts, a_ref, du_ref, h_ref, df_ref, *rest):
    out_ref = rest[-1]
    step = pl.program_id(1)
    width = a_ref.shape[1]
    rows_in = width // out_ref.shape[0]
    rows_out = parts * rows_in
    owners = width // rows_out

    def deal(total, rows, first, at):
        for i in range(width // rows):
            out_ref[first + i, pl.ds(at, rows)] = total[i * rows : (i + 1) * rows]

    for i in range(parts):

        @pl.when(step == i)
        def _():
            total = low(lax.dot_general(a_ref[...], du_ref[...], TN, preferred_element_type=jnp.float32))
            deal(total, rows_in, 0, i * rows_in)

        @pl.when(step == parts + i)
        def _():
            total = low(lax.dot_general(h_ref[...], df_ref[...], TN, preferred_element_type=jnp.float32))
            deal(total, rows_out, i * owners, parts * rows_in)


def ffn_terms(a, du, h, df, count, block=512):
    depth, width = a.shape
    parts = du.shape[1] // width
    rows = (parts * width + h.shape[1]) // count
    per = width // block
    return pl.pallas_call(
        functools.partial(ffn_term_kernel, parts),
        grid=(per, 2 * parts),
        in_specs=[
            pl.BlockSpec((depth, width), lambda n, s: (0, 0)),
            pl.BlockSpec((depth, block), lambda n, s: (0, jnp.minimum(s, parts - 1) * per + n)),
            pl.BlockSpec((depth, width), lambda n, s: (0, jnp.maximum(s - parts, 0))),
            pl.BlockSpec((depth, block), lambda n, s: (0, n)),
        ],
        out_specs=pl.BlockSpec((count, rows, block), lambda n, s: (0, 0, n)),
        out_shape=jax.ShapeDtypeStruct((count, rows, width), jnp.bfloat16),
        compiler_params=pltpu.CompilerParams(vmem_limit_bytes=58 << 20),
        cost_estimate=estimate(
            flops=4 * parts * depth * width * width, bytes_accessed=12 * parts * width * width, transcendentals=0
        ),
    )(a, du, h, df)


def halve_kernel(rep_ref, mine_ref, came_ref, *rest):
    keep_ref, send_ref = rest[-2:]
    total = low(mine_ref[...].astype(jnp.float32) + came_ref[...].astype(jnp.float32))
    half = total.shape[1] // 2
    one, two = total[:, :half], total[:, half:]
    keep_ref[...] = jnp.where(rep_ref[0] == 0, one, two)
    send_ref[...] = jnp.where(rep_ref[0] == 0, two, one)


def halve(rep, mine, came, after=()):
    chips, rows, width = mine.shape
    spec = pl.BlockSpec((2, rows, width), lambda i, _: (i, 0, 0))
    out = pl.BlockSpec((2, rows // 2, width), lambda i, _: (i, 0, 0))
    return pl.pallas_call(
        halve_kernel,
        grid_spec=pltpu.PrefetchScalarGridSpec(
            num_scalar_prefetch=1,
            grid=(chips // 2,),
            in_specs=[spec, spec] + [pl.BlockSpec(memory_space=pl.ANY)] * len(after),
            out_specs=[out, out],
        ),
        out_shape=[jax.ShapeDtypeStruct((chips, rows // 2, width), jnp.bfloat16)] * 2,
        compiler_params=pltpu.CompilerParams(vmem_limit_bytes=32 << 20),
        cost_estimate=estimate(flops=2 * mine.size, bytes_accessed=6 * mine.size, transcendentals=0),
    )(rep, mine, came, *after)


def hop_kernel(first, second, carried, *rest):
    rest = rest[: len(rest) - carried]
    if first:
        mine_up, came_up, mine_down, came_down = rest[:4]
        up = mine_up[0].astype(jnp.float32) + came_up[0].astype(jnp.float32)
        down = mine_down[0].astype(jnp.float32) + came_down[0].astype(jnp.float32)
        rest[-2][...] = low(up)
        rest[-1][...] = low(down)
        return
    up_ref, mine_up, came_up = rest[:3]
    up = up_ref[...].astype(jnp.float32) + mine_up[0].astype(jnp.float32) + came_up[0].astype(jnp.float32)
    if not second:
        rest[-1][...] = low(up)
        return
    down_ref, mine_down, came_down = rest[3:6]
    down = down_ref[...].astype(jnp.float32) + mine_down[0].astype(jnp.float32) + came_down[0].astype(jnp.float32)
    rest[-2][...] = low(up)
    rest[-1][...] = low(down)


def hop(mine, came, up, down, up_at, down_at, after=(), carry=()):
    rows, width = mine.shape[1:]
    blocks = 2 if rows % 32 == 0 else 1
    part = rows // blocks

    def pick(at):
        return pl.BlockSpec((1, part, width), lambda i: (at, i, 0))

    flat = pl.BlockSpec((part, width), lambda i: (i, 0))
    args, specs = [], []
    if up is not None:
        args.append(up)
        specs.append(flat)
    args += [mine, came]
    specs += [pick(up_at)] * 2
    if down_at is not None:
        if down is not None:
            args.append(down)
            specs.append(flat)
        args += [mine, came]
        specs += [pick(down_at)] * 2
    number = 1 if down_at is None else 2
    return pl.pallas_call(
        functools.partial(hop_kernel, up is None, down_at is not None, len(carry)),
        grid=(blocks,),
        in_specs=specs + [pl.BlockSpec(memory_space=pl.ANY)] * (len(after) + len(carry)),
        out_specs=[flat] * number + [pl.BlockSpec(memory_space=pl.ANY)] * len(carry),
        out_shape=[jax.ShapeDtypeStruct((rows, width), jnp.bfloat16)] * number
        + [jax.ShapeDtypeStruct(x.shape, x.dtype) for x in carry],
        input_output_aliases={len(args) + len(after) + i: number + i for i in range(len(carry))},
        cost_estimate=estimate(flops=4 * rows * width, bytes_accessed=16 * rows * width, transcendentals=0),
    )(*args, *after, *carry)


def ring_walk(chips):
    half = chips // 2
    return [2 * i for i in range(half)] + [2 * i + 1 for i in reversed(range(half))]


def ring_moves(count):
    walk = ring_walk(count // 2)
    chips = len(walk)
    up = [(2 * walk[i] + c, 2 * walk[(i + 1) % chips] + c) for i in range(chips) for c in range(2)]
    down = [(b, a) for a, b in up]
    swap = [(i, i ^ 1) for i in range(count)]
    return up, down, swap


def ring_tables(count):
    chips = count // 2
    walk = ring_walk(chips)
    place = [0] * chips
    for at, chip in enumerate(walk):
        place[chip] = at
    order, rank = [], []
    for shard in range(count):
        at, core = place[shard // 2], shard % 2
        near = [walk[(at + k) % chips] for k in range(chips)]
        order.append([2 * c + core for c in near] + [2 * c + 1 - core for c in near])
        rank.append([(place[c] - at) % chips for c in range(chips)] + [core])
    me = lax.axis_index("shard")
    return jnp.array(order, jnp.int32)[me], jnp.array(rank, jnp.int32)[me]


def gather_pieces(piece, count):
    up, down, swap = ring_moves(count)
    chips = count // 2
    pieces = [piece] + [None] * (chips - 1)
    upward = downward = piece
    for step in range(1, chips // 2 + 1):
        upward = lax.ppermute(upward, "shard", up)
        pieces[chips - step] = upward
        if step < chips // 2:
            downward = lax.ppermute(downward, "shard", down)
            pieces[step] = downward
    return pieces + [lax.ppermute(p, "shard", swap) for p in pieces]


class RingGather:
    def __init__(self, piece, count):
        self.up, self.down, self.swap = ring_moves(count)
        self.chips = count // 2
        self.pieces = [piece] + [None] * (self.chips - 1)
        self.step = 0

    def hop(self, *after):
        last, half = self.step, self.chips // 2
        upward, downward = self.pieces[-last % self.chips], self.pieces[last]
        held = sum(low(a[:1, :1]) for a in after) * 0
        self.step += 1
        self.pieces[self.chips - self.step] = lax.ppermute(upward + held, "shard", self.up)
        if self.step < half:
            self.pieces[self.step] = lax.ppermute(downward + held, "shard", self.down)

    def finish(self):
        return self.pieces + [lax.ppermute(p, "shard", self.swap) for p in self.pieces]


def add_low(*values_in):
    return low(sum(v.astype(jnp.float32) for v in values_in))


def over_rep(owned):
    partner = lax.ppermute(owned, "rep", [(0, 1), (1, 0)])
    return owned.astype(jnp.float32) + partner.astype(jnp.float32)


class RingSum:
    def __init__(self, mine, came, count, flip=False):
        self.up, self.down, _ = ring_moves(count)
        self.chips = count // 2
        self.sign = 1
        if flip:
            self.up, self.down, self.sign = self.down, self.up, -1
        self.mine, self.came = mine, came
        self.step = self.chips // 2
        self.upward = self.downward = None

    def at(self, distance):
        return (self.sign * distance) % self.chips

    def hop(self, after=(), carry=()):
        half = self.chips // 2
        down_at = 1 - self.step if self.step > 1 else None
        sums = hop(
            self.mine, self.came, self.upward, self.downward if down_at is not None else None,
            self.at(self.step), None if down_at is None else self.at(down_at), after, carry,
        )
        self.carried = sums[len(sums) - len(carry) :]
        self.upward = lax.ppermute(sums[0], "shard", self.up)
        if down_at is not None:
            self.downward = lax.ppermute(sums[1], "shard", self.down)
        self.step -= 1
        return [sums[0]]

    def finish(self):
        return add_low(self.mine[0], self.came[0], self.upward, self.downward)


def over_cores(other, count):
    return lax.ppermute(other, "shard", ring_moves(count)[2])


def swap_reps(part):
    return lax.ppermute(part, "rep", [(0, 1), (1, 0)])


def both_halves(rep, owned):
    partner = swap_reps(owned)
    first = rep[0] == 0
    return jnp.concatenate([jnp.where(first, owned, partner), jnp.where(first, partner, owned)], axis=0).astype(jnp.float32)


def scatter_sum(term):
    return over_rep(lax.psum_scatter(low(term), "shard", scatter_dimension=0, tiled=True))


def weight_term(left, right):
    return jnp.einsum("ra,rb->ab", left, right, preferred_element_type=jnp.float32)


def body(
    tokens,
    enc_states,
    unit_ids,
    enc_ids,
    self_q,
    self_k,
    self_v,
    self_o,
    cross_q,
    cross_k,
    cross_v,
    cross_o,
    ffn_in,
    ffn_out,
    norm_gains,
    norm_biases,
    cotangent,
):
    count = lax.axis_size("shard")
    ring = count == 16
    own, width = self_q.shape
    own_out = ffn_out.shape[0]
    parts = ffn_in.shape[1] // width
    hidden = parts * width
    own_width = norm_gains.shape[1]
    x = tokens.reshape(-1, width)
    enc = enc_states.reshape(-1, width)
    cot = cotangent.reshape(-1, width)
    row_count = x.shape[0]
    bf16, f32 = jnp.bfloat16, jnp.float32

    norm_piece = jnp.concatenate([norm_gains, norm_biases], axis=0)
    in_parts = [ffn_in[:, i * width : (i + 1) * width] for i in range(parts)]
    unit_extra, enc_extra = key_extras(unit_ids[0]), key_extras(enc_ids[0])
    query_extra = query_extras(unit_ids[0])
    self_windows = windows(unit_ids[0], unit_ids[0], 256, 256, True)
    cross_windows = windows(unit_ids[0], enc_ids[0], 256, 256, False)
    if ring:
        order, rank = ring_tables(count)
        norm_row = jnp.pad(norm_piece.reshape(1, -1), ((0, 15), (0, width - 8 * own_width)))
        rep = lax.axis_index("rep").astype(jnp.int32).reshape(1)
        piece_b = jnp.concatenate([self_o, cross_q, cross_k, cross_v, cross_o], axis=0)
        half_c = jnp.where(rep[0] == 0, jnp.concatenate(in_parts, axis=0), ffn_out)
        set_a = gather_pieces(jnp.concatenate([self_q, self_k, self_v, norm_row], axis=0), count)
        ring_b = RingGather(piece_b, count)
        ring_b.hop(set_a[count // 4])
        set_c = [lax.all_gather(half_c, ("rep", "shard"), axis=0, tiled=True)]
        norm_rows = jnp.concatenate([p[3 * own : 3 * own + 1, : 8 * own_width] for p in set_a], axis=0)
        place = (jnp.arange(count, dtype=jnp.int32)[:, None] == order[None, :]).astype(bf16)
        norms = mm(place, norm_rows)
        norms = jnp.transpose(norms.reshape(count, 8, own_width), (1, 0, 2)).reshape(8, width)
        kinds = ("ring", "ring", "tiled")
    else:
        order = jnp.zeros((1,), jnp.int32)

        def whole(part):
            return lax.all_gather(part, "shard", axis=0, tiled=True)

        set_a = [jnp.concatenate([whole(w) for w in (self_q, self_k, self_v)], axis=0)]
        set_b = [jnp.concatenate([whole(w) for w in (self_o, cross_q, cross_k, cross_v, cross_o)], axis=0)]
        set_c = [jnp.concatenate([whole(w) for w in in_parts + [ffn_out]], axis=0)]
        norms = lax.all_gather(norm_piece, "shard", axis=1, tiled=True).astype(f32)
        kinds = ("flat", "flat", "flat")
    plan_a = [(kinds[0], i * own, own, i * width, 0, count) for i in range(3)]
    plan_b = [(kinds[1], i * own, own, i * width, 0, count) for i in range(5)]
    plan_c = [(kinds[2], i * own, own, i * width, parts * own, count) for i in range(parts)]
    plan_c.append(("flat", 0, own_out, parts * width, 0, count))
    sems = pltpu.SemaphoreType.DMA
    square = 2 * row_count * width * width

    a1, q1, k1, v1 = by_rows(
        functools.partial(first_kernel, plan_a, len(set_a)), order, [x], norms, set_a,
        [(width, bf16)] * 4, False,
        [pltpu.VMEM((3, width, width), bf16), sems((3,))], 3 * square,
    )
    pairs = width // 128
    self_args = (q1, k1, v1, query_extra, unit_extra, self_windows, True)
    if ring:
        o1_low, log1_low = attend_forward(*self_args, (0, pairs // 2))
        ring_b.hop(o1_low)
        o1_high, log1_high = attend_forward(*self_args, (pairs // 2, pairs), [o1_low])
        ring_b.hop(o1_high)
        ring_b.hop()
        set_b = ring_b.finish()
    else:
        o1_low, log1_low = attend_forward(*self_args, (0, pairs // 2))
        o1_high, log1_high = attend_forward(*self_args, (pairs // 2, pairs))
    o1 = [o1_low, o1_high]
    r1, a2, q2, k2, v2 = by_rows(
        functools.partial(second_kernel, plan_b[:4], len(set_b), 2), order, o1 + [x, enc], norms, set_b,
        [(width, f32)] + [(width, bf16)] * 4, False,
        [pltpu.VMEM((4, width, width), bf16), sems((4,))], 4 * square,
    )
    o2, log2 = attend_forward(q2, k2, v2, query_extra, enc_extra, cross_windows, False, (0, pairs))
    out, a3, h, df, du, dr2, dc2, do2, terms_three = by_rows(
        functools.partial(third_kernel, plan_b[4:] + plan_c, len(set_b), len(set_c), 1), order, [o2, r1, cot], norms, set_b + set_c,
        [(width, bf16), (width, bf16), (hidden, bf16), (width, bf16), (hidden, bf16), (width, f32), (width, bf16), (width, bf16)], True,
        [
            pltpu.VMEM((width, width), bf16),
            pltpu.VMEM((parts, width, width), bf16),
            pltpu.VMEM((hidden, width), bf16),
            pltpu.VMEM((256, hidden), f32),
            sems((parts + 2,)),
        ],
        (2 + 4 * parts) * square,
    )

    cross_args = (q2, k2, v2, o2, do2, log2, enc_extra, cross_windows, False)
    if ring:
        ffn_set = ffn_terms(a3, du, h, df, count)
        ffn_set = lax.psum_scatter(ffn_set.reshape(-1, width), "shard", scatter_dimension=0, tiled=True)
    else:
        grad_in, grad_out = scatter_sum(weight_term(a3, du)), scatter_sum(weight_term(h, df))
    dq2, dk2, dv2 = attend_backward(*cross_args, (0, pairs))
    dr1, dc1, do1, terms_two = by_rows(
        functools.partial(fourth_kernel, plan_b[:2], len(set_b)), order, [dq2, r1, dr2], norms, set_b,
        [(width, f32), (width, bf16), (width, bf16)], True,
        [pltpu.VMEM((2, width, width), bf16), sems((2,))], 2 * square,
    )

    def enc_backward(after):
        return by_rows(
            functools.partial(enc_kernel, plan_b[2:4], len(set_b)), order, [dk2, dv2], norms, set_b,
            [(width, f32)], False,
            [pltpu.VMEM((2, width, width), bf16), sems((2,))], 2 * square, after,
        )[0]

    half = pairs // 2

    def self_backward(i, after):
        return attend_backward(
            q1, k1, v1, o1[i], do1, (log1_low, log1_high)[i], unit_extra, self_windows, True,
            (i * half, (i + 1) * half), i * half, after,
        )

    def fifth(groups, after, part=(0, 1), into=None):
        dq1, dk1, dv1 = ([g[i] for g in groups] for i in range(3))
        return by_rows(
            functools.partial(fifth_kernel, plan_a, len(set_a), len(groups)), order, dq1 + dk1 + dv1 + [x, dr1], norms, set_a,
            [(width, f32)], True,
            [pltpu.VMEM((3, width, width), bf16), sems((3,))], 3 * square // part[1], after, part=part, into=into,
        )

    if ring:
        groups = [self_backward(0, [])]
        groups.append(self_backward(1, [groups[0][0]]))
        mine, other = term_sets(
            rank, [tuple(o1), (a1,)],
            [(0, [(dc1, c)]) for c in range(2)] + [(1, [(g[i], 0)]) for i in range(3) for g in groups], count,
        )
        sums_a = RingSum(mine, over_cores(other, count), count, True)
        grad_x, terms_one = fifth(groups, [mine])
        last = sums_a.hop([grad_x])
        mine, other = term_sets(
            rank, [(o2,), (a2,), (enc,)],
            [(i, [(g, c)]) for i, g in ((0, dc2), (1, dq2), (2, dk2), (2, dv2)) for c in range(2)], count, last,
            [terms_one, terms_two, terms_three],
        )
        last = sums_a.hop([mine], [other])
        came = over_cores(sums_a.carried[0], count)
        grad_enc = enc_backward(last)
        keep, send = halve(rep, mine, came, [grad_enc])
        sums_b = RingSum(keep, swap_reps(send), count)
        last = sums_a.hop(sums_a.hop([keep]))
        ffn_set = over_rep(ffn_set + last[0][:1, :1] * 0)
        last = sums_b.hop(sums_b.hop(sums_b.hop(last)))
        sums_b.hop(last + [ffn_set])
        grad_a, grad_b = over_rep(sums_a.finish()), both_halves(rep, sums_b.finish())
        grad_in = jnp.concatenate([ffn_set[i * own : (i + 1) * own] for i in range(parts)], axis=1)
        grad_out = ffn_set[parts * own :]

        norm_sum = grad_b[8 * own : 8 * own + 8, :own_width]

        def columns(array, places):
            return jnp.concatenate([array[i * own : (i + 1) * own] for i in places], axis=1)

        grad_co, grad_cq, grad_ck, grad_cv = (columns(grad_b, (2 * w, 2 * w + 1)) for w in range(4))
        grad_so, grad_sq, grad_sk, grad_sv = (columns(grad_a, (2 * w, 2 * w + 1)) for w in range(4))
    else:
        grad_enc = enc_backward(())
        groups = [self_backward(i, ()) for i in range(2)]
        dq1, dk1, dv1 = (jnp.concatenate([g[i] for g in groups], axis=1) for i in range(3))
        grad_x, terms_one = fifth(groups, ())
        norm_sum = lax.psum(terms_one + terms_two + terms_three, ("rep", "shard"))
        norm_sum = lax.dynamic_slice_in_dim(norm_sum, lax.axis_index("shard") * own_width, own_width, 1)
        grad_co, grad_cq, grad_ck, grad_cv, grad_so, grad_sq, grad_sk, grad_sv = (
            scatter_sum(weight_term(a, b))
            for a, b in (
                (o2, dc2), (a2, dq2), (enc, dk2), (enc, dv2), (jnp.concatenate(o1, axis=1), dc1), (a1, dq1), (a1, dk1), (a1, dv1)
            )
        )
    return (
        out.reshape(tokens.shape),
        grad_x.reshape(tokens.shape),
        grad_enc.reshape(enc_states.shape),
        grad_sq,
        grad_sk,
        grad_sv,
        grad_so,
        grad_cq,
        grad_ck,
        grad_cv,
        grad_co,
        grad_in,
        grad_out,
        norm_sum[:4],
        norm_sum[4:],
    )


def solution(mesh):
    return jax.shard_map(
        body,
        mesh=mesh,
        in_specs=(
            P(("rep", "shard"), None, None),
            P(("rep", "shard"), None, None),
            P(("rep", "shard"), None),
            P(("rep", "shard"), None),
            P("shard", None),
            P("shard", None),
            P("shard", None),
            P("shard", None),
            P("shard", None),
            P("shard", None),
            P("shard", None),
            P("shard", None),
            P("shard", None),
            P("shard", None),
            P(None, "shard"),
            P(None, "shard"),
            P(("rep", "shard"), None, None),
        ),
        out_specs=(
            P(("rep", "shard"), None, None),
            P(("rep", "shard"), None, None),
            P(("rep", "shard"), None, None),
            P("shard", None),
            P("shard", None),
            P("shard", None),
            P("shard", None),
            P("shard", None),
            P("shard", None),
            P("shard", None),
            P("shard", None),
            P("shard", None),
            P("shard", None),
            P(None, "shard"),
            P(None, "shard"),
        ),
        check_vma=False,
    )
```

```python
import functools
import math

import jax
import jax.numpy as jnp
from jax import lax
from jax.experimental import pallas as pl
from jax.experimental.pallas import tpu as pltpu
from jax.sharding import PartitionSpec as P

HEADS = 16
HEAD = 64


eps_norm = 1e-05


COST = 4


def estimate(flops, bytes_accessed, transcendentals):
    return pl.CostEstimate(flops=flops // 8, bytes_accessed=bytes_accessed // 8, transcendentals=0)
BIG = 1e30
NT = (((1,), (1,)), ((), ()))
TN = (((0,), (0,)), ((), ()))


def key_extras(ids):
    lane = jnp.arange(128)[None, :] % 64
    return jnp.where(lane < 8, (ids[:, None] != lane).astype(jnp.bfloat16), ((lane >= 8) & (lane < 11)).astype(jnp.bfloat16))


def query_extras(ids):
    lane = jnp.arange(128)[None, :] % 64
    return jnp.where((lane < 8) & (ids[:, None] == lane), -BIG, 0.0).astype(jnp.bfloat16)


def windows(unit_ids, key_ids, bq, bk, causal):
    n = key_ids.shape[0]
    nq = unit_ids.shape[0] // bq
    blocks = unit_ids.reshape(nq, bq)
    low = jnp.sum((key_ids[None, :] < blocks[:, :1]).astype(jnp.int32), axis=1)
    if causal:
        end = (jnp.arange(nq, dtype=jnp.int32) + 1) * bq
        count = (end - low + bk - 1) // bk
        start = end - count * bk
    else:
        end = jnp.sum((key_ids[None, :] <= blocks[:, -1:]).astype(jnp.int32), axis=1)
        low = low // 16 * 16
        count = (end - low + bk - 1) // bk
        start = jnp.minimum(low, n - count * bk)
    return jnp.concatenate([start, count])


def attend_forward_kernel(bq, bk, causal, hp, norm, win_ref, q_ref, k_ref, v_ref, qx_ref, kx_ref, *rest):
    o_ref, qe_ref, ka = rest[-3:]
    L, N = q_ref.shape[0], k_ref.shape[0]
    nq = L // bq
    lane = lax.broadcasted_iota(jnp.int32, (1, 128), 1)
    first = lane < 64
    part = lane % 64
    for g in range(hp):
        kp = k_ref[:, g*128:(g+1)*128]
        ka[2*g] = jnp.where(first, kp, kx_ref[...])
        ka[2*g+1] = jnp.where(first, kx_ref[...], kp)
    row = lax.broadcasted_iota(jnp.int32, (128, 1), 0)
    rpart = row % 64
    zero = jnp.zeros((1, 128), jnp.bfloat16)

    def one(i, W):
        rows = pl.ds(pl.multiple_of(i * bq, bq), bq)
        win = pl.ds(pl.multiple_of(win_ref[i], 16), W)
        xb = qx_ref[rows, :]
        ss = []
        for h in range(2*hp):
            g = h // 2
            qb = q_ref[rows, g*128:(g+1)*128]
            qa = jnp.where(first, qb, xb) if h % 2 == 0 else jnp.where(first, xb, qb)
            s = lax.dot_general(ka[h, win, :], qa, NT, preferred_element_type=jnp.float32)
            if causal:
                tri = lax.broadcasted_iota(jnp.int32, (bq, bq), 0) <= lax.broadcasted_iota(jnp.int32, (bq, bq), 1)
                d = jnp.where(tri, s[W - bq:, :], -BIG)
                s = d if W == bq else jnp.concatenate([s[: W - bq, :], d], axis=0)
            ss.append(s)
        outs, invs, lses = [], [], []
        for h in range(2*hp):
            g = h // 2
            s = ss[h]
            m = jnp.max(s, axis=0, keepdims=True)
            p = jnp.exp(s - m)
            l = jnp.sum(p, axis=0, keepdims=True)
            inv = 1.0 / l
            if norm: p = p * inv
            vw = v_ref[win, g*128:(g+1)*128]
            vw = jnp.where(first, vw, zero) if h % 2 == 0 else jnp.where(first, zero, vw)
            outs.append(lax.dot_general(vw, p.astype(jnp.bfloat16), TN, preferred_element_type=jnp.float32)); invs.append(inv)
            neg = -(m + jnp.log(l))
            hi = neg.astype(jnp.bfloat16).astype(jnp.float32)
            mid = (neg - hi).astype(jnp.bfloat16).astype(jnp.float32)
            lo = neg - hi - mid
            lses.append((hi, mid, lo))
        for g in range(hp):
            o = outs[2*g] + outs[2*g+1]
            if not norm:
                o = o * jnp.where(row < 64, invs[2*g], invs[2*g+1])
            o = jnp.transpose(o)
            o_ref[rows, g*128:(g+1)*128] = o.astype(jnp.bfloat16)
            a, b = lses[2*g], lses[2*g+1]
            e = jnp.where(row < 64, jnp.where(rpart == 8, b[0], jnp.where(rpart == 9, b[1], b[2])), jnp.where(rpart == 8, a[0], jnp.where(rpart == 9, a[1], a[2])))
            e = jnp.transpose(jnp.where((rpart >= 8) & (rpart < 11), e, 0.0))
            qe_ref[rows, g*128:(g+1)*128] = jnp.where(part < 8, xb.astype(jnp.float32), e).astype(jnp.bfloat16)

    def step(i, c):
        for j in range(1, N // bk + 1):
            @pl.when(win_ref[nq + i] == j)
            def _():
                one(i, j * bk)
        return c

    lax.fori_loop(0, nq, step, 0)

def attend_forward(q, k, v, qx, kx, win, causal, pairs, after=(), bq=256, bk=256, hp=4):
    L, N = q.shape[0], k.shape[0]
    w = 128 * hp
    start, number = pairs[0] // hp, (pairs[1] - pairs[0]) // hp
    col = lambda n: pl.BlockSpec((n, w), lambda p, _: (0, start + p))
    own = lambda n: pl.BlockSpec((n, w), lambda p, _: (0, p))
    fix = lambda n: pl.BlockSpec((n, 128), lambda p, _: (0, 0))
    return pl.pallas_call(
        functools.partial(attend_forward_kernel, bq, bk, causal, hp, True),
        grid_spec=pltpu.PrefetchScalarGridSpec(
            num_scalar_prefetch=1,
            grid=(number,),
            in_specs=[col(L), col(N), col(N), fix(L), fix(N)] + [pl.BlockSpec(memory_space=pl.ANY)] * len(after),
            out_specs=[own(L), own(L)],
            scratch_shapes=[pltpu.VMEM((2 * hp, N, 128), jnp.bfloat16)],
        ),
        out_shape=[jax.ShapeDtypeStruct((L, number * w), jnp.bfloat16)] * 2,
        compiler_params=pltpu.CompilerParams(vmem_limit_bytes=56 << 20),
        cost_estimate=estimate(
            flops=COST * 2 * 2 * L * N * number * w, bytes_accessed=10 * L * number * w, transcendentals=0
        ),
    )(win, q, k, v, qx, kx, *after)


def attend_backward_kernel(bq, bk, causal, hp, win_ref, q_ref, k_ref, v_ref, o_ref, do_ref, qe_ref, kx_ref, *rest):
    dq_ref, dk_ref, dv_ref, ka, va, dka, dva = rest[-7:]
    L, N = q_ref.shape[0], k_ref.shape[0]
    nq = L // bq
    lane = lax.broadcasted_iota(jnp.int32, (1, 128), 1)
    first = lane < 64
    part = lane % 64
    ones = jnp.broadcast_to(jnp.where(part < 3, 1.0, 0.0).astype(jnp.bfloat16), (N, 128))
    for g in range(hp):
        c = slice(g*128,(g+1)*128)
        ka[2*g] = jnp.where(first, k_ref[:, c], kx_ref[...])
        ka[2*g+1] = jnp.where(first, kx_ref[...], k_ref[:, c])
        va[2*g] = jnp.where(first, v_ref[:, c], ones)
        va[2*g+1] = jnp.where(first, ones, v_ref[:, c])
    dka[...] = jnp.zeros_like(dka)
    dva[...] = jnp.zeros_like(dva)
    zero = jnp.zeros((1, 128), jnp.bfloat16)

    def one(i, W):
        rows = pl.ds(pl.multiple_of(i * bq, bq), bq)
        win = pl.ds(pl.multiple_of(win_ref[i], 16), W)
        S = []
        for g in range(hp):
            c = slice(g*128,(g+1)*128)
            qb, xb, dob = q_ref[rows, c], qe_ref[rows, c], do_ref[rows, c]
            prod = dob.astype(jnp.float32) * o_ref[rows, c].astype(jnp.float32)
            for h in range(2):
                mine = first if h == 0 else jnp.logical_not(first)
                neg = -jnp.sum(jnp.where(mine, prod, 0.0), axis=1, keepdims=True)
                hi = neg.astype(jnp.bfloat16).astype(jnp.float32)
                mid = (neg - hi).astype(jnp.bfloat16).astype(jnp.float32)
                lo = neg - hi - mid
                de = jnp.where(part == 0, hi, jnp.where(part == 1, mid, jnp.where(part == 2, lo, 0.0))).astype(jnp.bfloat16)
                qa = jnp.where(mine, qb, xb)
                da = jnp.where(mine, dob, de)
                s = lax.dot_general(ka[2*g+h, win, :], qa, NT, preferred_element_type=jnp.float32)
                dp = lax.dot_general(va[2*g+h, win, :], da, NT, preferred_element_type=jnp.float32)
                S.append((s, dp))
        for g in range(hp):
            c = slice(g*128,(g+1)*128)
            qb, dob = q_ref[rows, c], do_ref[rows, c]
            ps, dss = [], []
            for h in range(2):
                s, dp = S[2*g+h]
                if causal:
                    tri = lax.broadcasted_iota(jnp.int32, (bq, bq), 0) <= lax.broadcasted_iota(jnp.int32, (bq, bq), 1)
                    d = jnp.where(tri, s[W - bq:, :], -BIG)
                    s = d if W == bq else jnp.concatenate([s[: W - bq, :], d], axis=0)
                p = jnp.exp(s)
                dss.append((p * dp).astype(jnp.bfloat16))
                ps.append(p.astype(jnp.bfloat16))
            docat = jnp.concatenate([jnp.where(first, dob, zero), jnp.where(first, zero, dob)], axis=0)
            qcat = jnp.concatenate([jnp.where(first, qb, zero), jnp.where(first, zero, qb)], axis=0)
            dva[win, c] += jnp.dot(jnp.concatenate(ps, axis=1), docat, preferred_element_type=jnp.float32)
            dka[win, c] += jnp.dot(jnp.concatenate(dss, axis=1), qcat, preferred_element_type=jnp.float32)
            kw = k_ref[win, c]
            k0, k1 = jnp.where(first, kw, zero), jnp.where(first, zero, kw)
            turned = lax.dot_general(k0, dss[0], TN, preferred_element_type=jnp.float32)
            turned = turned + lax.dot_general(k1, dss[1], TN, preferred_element_type=jnp.float32)
            dq = jnp.transpose(turned)
            dq_ref[rows, c] = (dq * 0.125).astype(jnp.bfloat16)

    def step(i, c):
        for j in range(1, N // bk + 1):
            @pl.when(win_ref[nq + i] == j)
            def _():
                one(i, j * bk)
        return c

    lax.fori_loop(0, nq, step, 0)
    dk_ref[...] = dka[...].astype(jnp.bfloat16)
    dv_ref[...] = dva[...].astype(jnp.bfloat16)

def attend_backward(q, k, v, o, do, qe, kx, win, causal, pairs, base=0, after=(), bq=256, bk=256, hp=2):
    L, N = q.shape[0], k.shape[0]
    w = 128 * hp
    start, number, base = pairs[0] // hp, (pairs[1] - pairs[0]) // hp, base // hp
    col = lambda n: pl.BlockSpec((n, w), lambda p, _: (0, start + p))
    own = lambda n: pl.BlockSpec((n, w), lambda p, _: (0, p))
    held = pl.BlockSpec((L, w), lambda p, _: (0, start - base + p))
    fix = lambda n: pl.BlockSpec((n, 128), lambda p, _: (0, 0))
    return pl.pallas_call(
        functools.partial(attend_backward_kernel, bq, bk, causal, hp),
        grid_spec=pltpu.PrefetchScalarGridSpec(
            num_scalar_prefetch=1,
            grid=(number,),
            in_specs=[col(L), col(N), col(N), held, col(L), held, fix(N)]
            + [pl.BlockSpec(memory_space=pl.ANY)] * len(after),
            out_specs=[own(L), own(N), own(N)],
            scratch_shapes=[pltpu.VMEM((2 * hp, N, 128), jnp.bfloat16)] * 2 + [pltpu.VMEM((N, w), jnp.float32)] * 2,
        ),
        out_shape=[jax.ShapeDtypeStruct((L, number * w), jnp.bfloat16)]
        + [jax.ShapeDtypeStruct((N, number * w), jnp.bfloat16)] * 2,
        compiler_params=pltpu.CompilerParams(vmem_limit_bytes=58 << 20),
        cost_estimate=estimate(
            flops=COST * 5 * 2 * L * N * number * w, bytes_accessed=16 * L * number * w, transcendentals=0
        ),
    )(win, q, k, v, o, do, qe, kx, *after)


def fetch(plan, refs, order_ref, dst, sem):
    kind, offset, rows, flat, piece_rows, count = plan
    if kind == "flat":
        part = rows * count // 16
        for j in range(16):
            pltpu.make_async_copy(refs[0].at[pl.ds(flat + j * part, part)], dst.at[pl.ds(j * part, part)], sem).start()
        return
    for j in range(count):
        if kind == "ring":
            src = refs[j].at[pl.ds(offset, rows)]
            at = pl.multiple_of(order_ref[j] * rows, 16)
        else:
            src = refs[0].at[pl.ds(j * piece_rows + offset, rows)]
            at = j * rows
        pltpu.make_async_copy(src, dst.at[pl.ds(at, rows)], sem).start()


def arrived(dst, sem):
    pltpu.make_async_copy(dst, dst, sem).wait()


def normed(values_in):
    centre = values_in - jnp.mean(values_in, axis=-1, keepdims=True)
    spread = jnp.mean(centre * centre, axis=-1, keepdims=True)
    scale = lax.rsqrt(spread + eps_norm)
    return centre * scale, scale


def normed_back(unit, scale, gain, grad_out):
    grad_unit = grad_out * gain
    inner = jnp.mean(grad_unit * unit, axis=-1, keepdims=True)
    return (grad_unit - jnp.mean(grad_unit, axis=-1, keepdims=True) - unit * inner) * scale


def mm(left, right):
    return jnp.dot(left, right, preferred_element_type=jnp.float32)


def mm_back(left, right):
    return lax.dot_general(left, right, NT, preferred_element_type=jnp.float32)


def low(values_in):
    return values_in.astype(jnp.bfloat16)


def term_rows(refs, at, values_in):
    refs[at : at + 1, :] += jnp.sum(values_in, axis=0, keepdims=True)


def first_kernel(plans, n_refs, order_ref, x_ref, norm_ref, *rest):
    refs, (a_ref, q_ref, k_ref, v_ref, w, sem) = rest[:n_refs], rest[-6:]

    @pl.when(pl.program_id(0) == 0)
    def _():
        for i in range(3):
            fetch(plans[i], refs, order_ref, w.at[i], sem.at[i])
        for i in range(3):
            arrived(w.at[i], sem.at[i])

    unit, _ = normed(x_ref[...].astype(jnp.float32))
    a = low(unit * norm_ref[0:1, :] + norm_ref[4:5, :])
    a_ref[...] = a
    q_ref[...] = low(mm(a, w[0]) * 0.125)
    k_ref[...] = low(mm(a, w[1]))
    v_ref[...] = low(mm(a, w[2]))


def joined(refs):
    return refs[0][...] if len(refs) == 1 else jnp.concatenate([r[...] for r in refs], axis=1)


def second_kernel(plans, n_refs, n_o, order_ref, *rest):
    o_refs, (x_ref, e_ref, norm_ref), rest = rest[:n_o], rest[n_o : n_o + 3], rest[n_o + 3 :]
    refs, (r_ref, a_ref, q_ref, k_ref, v_ref, w, sem) = rest[:n_refs], rest[-7:]

    @pl.when(pl.program_id(0) == 0)
    def _():
        for i in range(4):
            fetch(plans[i], refs, order_ref, w.at[i], sem.at[i])
        for i in range(4):
            arrived(w.at[i], sem.at[i])

    r = x_ref[...].astype(jnp.float32) + mm(joined(o_refs), w[0])
    r_ref[...] = r
    k_ref[...] = low(mm(e_ref[...], w[2]))
    v_ref[...] = low(mm(e_ref[...], w[3]))
    unit, _ = normed(r)
    a = low(unit * norm_ref[1:2, :] + norm_ref[5:6, :])
    a_ref[...] = a
    q_ref[...] = low(mm(a, w[1]) * 0.125)


def third_kernel(plans, n_b, n_c, n_o, order_ref, *rest):
    o_refs, (r_ref, cot_ref, norm_ref), rest = rest[:n_o], rest[n_o : n_o + 3], rest[n_o + 3 :]
    refs_b, refs_c = rest[:n_b], rest[n_b : n_b + n_c]
    (out_ref, a_ref, h_ref, df_ref, du_ref, dr_ref, dc_ref, do_ref, term_ref, wc, wi, wo, slope, sem) = rest[-14:]
    parts = wi.shape[0]
    first = pl.program_id(0) == 0

    @pl.when(first)
    def _():
        fetch(plans[0], refs_b, order_ref, wc, sem.at[0])
        for i in range(parts):
            fetch(plans[1 + i], refs_c, order_ref, wi.at[i], sem.at[1 + i])
        fetch(plans[1 + parts], refs_c, order_ref, wo, sem.at[1 + parts])
        term_ref[...] = jnp.zeros_like(term_ref)
        arrived(wc, sem.at[0])

    r2 = r_ref[...] + mm(joined(o_refs), wc[...])
    unit2, scale2 = normed(r2)
    a3 = low(unit2 * norm_ref[2:3, :] + norm_ref[6:7, :])
    a_ref[...] = a3

    @pl.when(first)
    def _():
        for i in range(parts):
            arrived(wi.at[i], sem.at[1 + i])
        arrived(wo, sem.at[1 + parts])

    width = wi.shape[2]
    r3 = r2
    for i in range(parts):
        cols = slice(i * width, (i + 1) * width)
        u = mm(a3, wi[i])
        half = 0.5 * (1.0 + lax.erf(u * (1.0 / math.sqrt(2.0))))
        h = low(u * half)
        h_ref[:, cols] = h
        slope[:, cols] = half + u * jnp.exp(-0.5 * u * u) * (1.0 / math.sqrt(2.0 * math.pi))
        r3 = r3 + mm(h, wo[cols, :])
    unit3, scale3 = normed(r3)
    out_ref[...] = low(unit3 * norm_ref[3:4, :] + norm_ref[7:8, :])
    cot = cot_ref[...].astype(jnp.float32)
    term_rows(term_ref, 3, cot * unit3)
    term_rows(term_ref, 7, cot)
    dr3 = normed_back(unit3, scale3, norm_ref[3:4, :], cot)
    df = low(dr3)
    df_ref[...] = df
    da3 = jnp.zeros_like(dr3)
    for i in range(parts):
        cols = slice(i * width, (i + 1) * width)
        du = low(mm_back(df, wo[cols, :]) * slope[:, cols])
        du_ref[:, cols] = du
        da3 = da3 + mm_back(du, wi[i])
    term_rows(term_ref, 2, da3 * unit2)
    term_rows(term_ref, 6, da3)
    dr2 = dr3 + normed_back(unit2, scale2, norm_ref[2:3, :], da3)
    dr_ref[...] = dr2
    dc = low(dr2)
    dc_ref[...] = dc
    do_ref[...] = low(mm_back(dc, wc[...]))


def fourth_kernel(plans, n_refs, order_ref, dq_ref, r_ref, dr_ref, norm_ref, *rest):
    refs, (dx_ref, dc_ref, do_ref, term_ref, w, sem) = rest[:n_refs], rest[-6:]

    @pl.when(pl.program_id(0) == 0)
    def _():
        for i in range(2):
            fetch(plans[i], refs, order_ref, w.at[i], sem.at[i])
        for i in range(2):
            arrived(w.at[i], sem.at[i])
        term_ref[...] = jnp.zeros_like(term_ref)

    da = mm_back(dq_ref[...], w[1])
    unit, scale = normed(r_ref[...])
    term_rows(term_ref, 1, da * unit)
    term_rows(term_ref, 5, da)
    dx = dr_ref[...] + normed_back(unit, scale, norm_ref[1:2, :], da)
    dx_ref[...] = dx
    dc = low(dx)
    dc_ref[...] = dc
    do_ref[...] = low(mm_back(dc, w[0]))


def enc_kernel(plans, n_refs, order_ref, dk_ref, dv_ref, norm_ref, *rest):
    refs, (de_ref, w, sem) = rest[:n_refs], rest[-3:]

    @pl.when(pl.program_id(0) == 0)
    def _():
        for i in range(2):
            fetch(plans[i], refs, order_ref, w.at[i], sem.at[i])
        for i in range(2):
            arrived(w.at[i], sem.at[i])

    de_ref[...] = mm_back(dk_ref[...], w[0]) + mm_back(dv_ref[...], w[1])


def fifth_kernel(plans, n_refs, n_g, order_ref, *rest):
    dq_refs, dk_refs, dv_refs = (rest[i * n_g : (i + 1) * n_g] for i in range(3))
    (x_ref, dr_ref, norm_ref), rest = rest[3 * n_g : 3 * n_g + 3], rest[3 * n_g + 3 :]
    refs, (dx_ref, term_ref, w, sem) = rest[:n_refs], rest[-4:]

    @pl.when(pl.program_id(0) == 0)
    def _():
        for i in range(3):
            fetch(plans[i], refs, order_ref, w.at[i], sem.at[i])
        for i in range(3):
            arrived(w.at[i], sem.at[i])
        term_ref[...] = jnp.zeros_like(term_ref)

    da = mm_back(joined(dq_refs), w[0]) + mm_back(joined(dk_refs), w[1]) + mm_back(joined(dv_refs), w[2])
    unit, scale = normed(x_ref[...].astype(jnp.float32))
    term_rows(term_ref, 0, da * unit)
    term_rows(term_ref, 4, da)
    dx_ref[...] = dr_ref[...] + normed_back(unit, scale, norm_ref[0:1, :], da)


def by_rows(kernel, order, row_inputs, norms, piece_refs, row_outputs, terms, scratch, flops, after=(), block=256, part=(0, 1), into=None):
    rows = row_inputs[0].shape[0]
    steps = rows // block // part[1]
    first = part[0] * steps
    piece_refs = list(piece_refs) + list(after) + ([] if into is None else [into])
    aliases = {} if into is None else {1 + len(row_inputs) + len(piece_refs): 0}

    def spec(width):
        return pl.BlockSpec((block, width), lambda i, _: (first + i, 0))

    def fixed(shape):
        return pl.BlockSpec(shape, lambda i, _: (0, 0))

    out_shape = [jax.ShapeDtypeStruct((rows, w), t) for w, t in row_outputs]
    out_specs = [spec(w) for w, _ in row_outputs]
    if terms:
        out_shape.append(jax.ShapeDtypeStruct(norms.shape, jnp.float32))
        out_specs.append(fixed(norms.shape))
    moved = sum(x.size * x.dtype.itemsize for x in row_inputs) + sum(rows * w * t.dtype.itemsize if hasattr(t, "dtype") else rows * w * jnp.dtype(t).itemsize for w, t in row_outputs)
    return pl.pallas_call(
        kernel,
        grid_spec=pltpu.PrefetchScalarGridSpec(
            num_scalar_prefetch=1,
            grid=(steps,),
            in_specs=[spec(x.shape[1]) for x in row_inputs]
            + [fixed(norms.shape)]
            + [pl.BlockSpec(memory_space=pl.ANY)] * len(piece_refs),
            out_specs=out_specs,
            scratch_shapes=scratch,
        ),
        out_shape=out_shape,
        input_output_aliases=aliases,
        compiler_params=pltpu.CompilerParams(vmem_limit_bytes=58 << 20),
        cost_estimate=estimate(flops=flops, bytes_accessed=moved, transcendentals=0),
    )(order, *row_inputs, norms, *piece_refs)


def term_kernel(names, chips, n_left, n_right, n_extra, rank_ref, *rest):
    parts = len(names)
    extra, rest = rest[:n_extra], rest[n_extra:]
    flat, rest = rest[: sum(n_left)], rest[sum(n_left) :]
    lefts = [flat[sum(n_left[:i]) : sum(n_left[: i + 1])] for i in range(len(n_left))]
    rights = [rest[sum(n_right[:i]) : sum(n_right[: i + 1])] for i in range(parts)]
    mine_ref, other_ref, turned = rest[-3:]
    rows = turned.shape[0] // (2 * chips)

    def deal(chip, at, number, one, two):
        core = rank_ref[chips]
        mine_ref[rank_ref[chip], at : at + number] = jnp.where(core == 0, one, two)
        other_ref[rank_ref[chip], at : at + number] = jnp.where(core == 0, two, one)

    for i in range(parts):

        @pl.when(pl.program_id(0) == i)
        def _():
            if i == 0 or names[i] != names[i - 1]:
                turned[...] = jnp.transpose(joined(lefts[names[i]]))
            total = low(mm(turned[...], joined(rights[i])))
            for chip in range(chips):
                one = total[2 * chip * rows : (2 * chip + 1) * rows]
                two = total[(2 * chip + 1) * rows : (2 * chip + 2) * rows]
                deal(chip, i * rows if extra else 0, rows, one, two)
            if extra and i == 0:
                terms = extra[0][...] + extra[1][...] + extra[2][...]
                empty = jnp.zeros((8, 512 - rows), jnp.float32)
                for chip in range(chips):
                    one, two = (
                        low(jnp.concatenate([jnp.concatenate([terms[:, s * rows : (s + 1) * rows], empty], axis=1), jnp.zeros((24, 512), jnp.float32)], axis=0))
                        for s in (2 * chip, 2 * chip + 1)
                    )
                    deal(chip, parts * rows, 32, one, two)


def term_sets(rank, lefts, parts, count, after=(), extra=()):
    total, depth = sum(x.shape[1] for x in lefts[0]), lefts[0][0].shape[0]
    flat = [x for left in lefts for x in left]
    rows = total // count
    chips = count // 2
    number = len(parts)
    all_rows = number * rows + (32 if extra else 0)
    rights, specs = [], []
    for _, given in parts:
        for x, c in given:
            rights.append(x)
            specs.append(pl.BlockSpec((depth, 512 // len(given)), lambda n, _, c=c: (0, c)))
    return pl.pallas_call(
        functools.partial(term_kernel, [p[0] for p in parts], chips, [len(left) for left in lefts], [len(p[1]) for p in parts], len(extra)),
        grid_spec=pltpu.PrefetchScalarGridSpec(
            num_scalar_prefetch=1,
            grid=(number,),
            in_specs=[pl.BlockSpec(x.shape, lambda n, _: (0, 0)) for x in [*extra, *flat]]
            + specs
            + [pl.BlockSpec(memory_space=pl.ANY)] * len(after),
            out_specs=[pl.BlockSpec((chips, all_rows, 512), lambda n, _: (0, 0, 0)) if extra else pl.BlockSpec((chips, rows, 512), lambda n, _: (0, n, 0))] * 2,
            scratch_shapes=[pltpu.VMEM((total, depth), jnp.bfloat16)],
        ),
        out_shape=[jax.ShapeDtypeStruct((chips, all_rows, 512), jnp.bfloat16)] * 2,
        compiler_params=pltpu.CompilerParams(vmem_limit_bytes=58 << 20),
        cost_estimate=estimate(
            flops=2 * number * total * 512 * depth, bytes_accessed=6 * number * total * 512, transcendentals=0
        ),
    )(rank, *extra, *flat, *rights, *after)


def ffn_term_kernel(left_ref, right_ref, *rest):
    total = lax.dot_general(left_ref[...], right_ref[...], TN, preferred_element_type=jnp.float32)
    rest[-1][...] = low(total).reshape(rest[-1].shape)


def ffn_terms(a, du, h, df, count):
    depth, width = a.shape
    parts = du.shape[1] // width
    rows_in, rows_out = width // count, parts * width // count
    out_shape = jax.ShapeDtypeStruct((count, parts * rows_in + rows_out, width), jnp.bfloat16)
    whole = pl.BlockSpec((depth, width), lambda n: (0, 0))
    part = pl.BlockSpec((depth, width), lambda n: (0, n))
    params = pltpu.CompilerParams(vmem_limit_bytes=58 << 20)
    cost = estimate(flops=2 * parts * depth * width * width, bytes_accessed=6 * parts * width * width, transcendentals=0)
    terms = pl.pallas_call(
        ffn_term_kernel,
        grid=(parts,),
        in_specs=[whole, part],
        out_specs=pl.BlockSpec((count, rows_in, width), lambda n: (0, n, 0)),
        out_shape=out_shape,
        compiler_params=params,
        cost_estimate=cost,
    )(a, du)
    return pl.pallas_call(
        ffn_term_kernel,
        grid=(parts,),
        in_specs=[part, whole, pl.BlockSpec(memory_space=pl.ANY)],
        out_specs=pl.BlockSpec((width // rows_out, rows_out, width), lambda n: (n, 1, 0)),
        out_shape=out_shape,
        input_output_aliases={2: 0},
        compiler_params=params,
        cost_estimate=cost,
    )(h, df, terms)


def halve_kernel(rep_ref, mine_ref, came_ref, *rest):
    keep_ref, send_ref = rest[-2:]
    total = low(mine_ref[...].astype(jnp.float32) + came_ref[...].astype(jnp.float32))
    half = total.shape[1] // 2
    one, two = total[:, :half], total[:, half:]
    keep_ref[...] = jnp.where(rep_ref[0] == 0, one, two)
    send_ref[...] = jnp.where(rep_ref[0] == 0, two, one)


def halve(rep, mine, came, after=()):
    chips, rows, width = mine.shape
    spec = pl.BlockSpec((2, rows, width), lambda i, _: (i, 0, 0))
    out = pl.BlockSpec((2, rows // 2, width), lambda i, _: (i, 0, 0))
    return pl.pallas_call(
        halve_kernel,
        grid_spec=pltpu.PrefetchScalarGridSpec(
            num_scalar_prefetch=1,
            grid=(chips // 2,),
            in_specs=[spec, spec] + [pl.BlockSpec(memory_space=pl.ANY)] * len(after),
            out_specs=[out, out],
        ),
        out_shape=[jax.ShapeDtypeStruct((chips, rows // 2, width), jnp.bfloat16)] * 2,
        compiler_params=pltpu.CompilerParams(vmem_limit_bytes=32 << 20),
        cost_estimate=estimate(flops=2 * mine.size, bytes_accessed=6 * mine.size, transcendentals=0),
    )(rep, mine, came, *after)


def hop_kernel(first, second, carried, *rest):
    rest = rest[: len(rest) - carried]
    if first:
        mine_up, came_up, mine_down, came_down = rest[:4]
        up = mine_up[0].astype(jnp.float32) + came_up[0].astype(jnp.float32)
        down = mine_down[0].astype(jnp.float32) + came_down[0].astype(jnp.float32)
        rest[-2][...] = low(up)
        rest[-1][...] = low(down)
        return
    up_ref, mine_up, came_up = rest[:3]
    up = up_ref[...].astype(jnp.float32) + mine_up[0].astype(jnp.float32) + came_up[0].astype(jnp.float32)
    if not second:
        rest[-1][...] = low(up)
        return
    down_ref, mine_down, came_down = rest[3:6]
    down = down_ref[...].astype(jnp.float32) + mine_down[0].astype(jnp.float32) + came_down[0].astype(jnp.float32)
    rest[-2][...] = low(up)
    rest[-1][...] = low(down)


def hop(mine, came, up, down, up_at, down_at, after=(), carry=()):
    rows, width = mine.shape[1:]
    blocks = 2 if rows % 32 == 0 else 1
    part = rows // blocks

    def pick(at):
        return pl.BlockSpec((1, part, width), lambda i: (at, i, 0))

    flat = pl.BlockSpec((part, width), lambda i: (i, 0))
    args, specs = [], []
    if up is not None:
        args.append(up)
        specs.append(flat)
    args += [mine, came]
    specs += [pick(up_at)] * 2
    if down_at is not None:
        if down is not None:
            args.append(down)
            specs.append(flat)
        args += [mine, came]
        specs += [pick(down_at)] * 2
    number = 1 if down_at is None else 2
    return pl.pallas_call(
        functools.partial(hop_kernel, up is None, down_at is not None, len(carry)),
        grid=(blocks,),
        in_specs=specs + [pl.BlockSpec(memory_space=pl.ANY)] * (len(after) + len(carry)),
        out_specs=[flat] * number + [pl.BlockSpec(memory_space=pl.ANY)] * len(carry),
        out_shape=[jax.ShapeDtypeStruct((rows, width), jnp.bfloat16)] * number
        + [jax.ShapeDtypeStruct(x.shape, x.dtype) for x in carry],
        input_output_aliases={len(args) + len(after) + i: number + i for i in range(len(carry))},
        cost_estimate=estimate(flops=4 * rows * width, bytes_accessed=16 * rows * width, transcendentals=0),
    )(*args, *after, *carry)


def ring_walk(chips):
    half = chips // 2
    return [2 * i for i in range(half)] + [2 * i + 1 for i in reversed(range(half))]


def ring_moves(count):
    walk = ring_walk(count // 2)
    chips = len(walk)
    up = [(2 * walk[i] + c, 2 * walk[(i + 1) % chips] + c) for i in range(chips) for c in range(2)]
    down = [(b, a) for a, b in up]
    swap = [(i, i ^ 1) for i in range(count)]
    return up, down, swap


def ring_tables(count):
    chips = count // 2
    walk = ring_walk(chips)
    place = [0] * chips
    for at, chip in enumerate(walk):
        place[chip] = at
    order, rank = [], []
    for shard in range(count):
        at, core = place[shard // 2], shard % 2
        near = [walk[(at + k) % chips] for k in range(chips)]
        order.append([2 * c + core for c in near] + [2 * c + 1 - core for c in near])
        rank.append([(place[c] - at) % chips for c in range(chips)] + [core])
    me = lax.axis_index("shard")
    return jnp.array(order, jnp.int32)[me], jnp.array(rank, jnp.int32)[me]


def gather_pieces(piece, count):
    up, down, swap = ring_moves(count)
    chips = count // 2
    pieces = [piece] + [None] * (chips - 1)
    upward = downward = piece
    for step in range(1, chips // 2 + 1):
        upward = lax.ppermute(upward, "shard", up)
        pieces[chips - step] = upward
        if step < chips // 2:
            downward = lax.ppermute(downward, "shard", down)
            pieces[step] = downward
    return pieces + [lax.ppermute(p, "shard", swap) for p in pieces]


class RingGather:
    def __init__(self, piece, count):
        self.up, self.down, self.swap = ring_moves(count)
        self.chips = count // 2
        self.pieces = [piece] + [None] * (self.chips - 1)
        self.step = 0

    def hop(self, *after):
        last, half = self.step, self.chips // 2
        upward, downward = self.pieces[-last % self.chips], self.pieces[last]
        held = sum(low(a[:1, :1]) for a in after) * 0
        self.step += 1
        self.pieces[self.chips - self.step] = lax.ppermute(upward + held, "shard", self.up)
        if self.step < half:
            self.pieces[self.step] = lax.ppermute(downward + held, "shard", self.down)

    def finish(self):
        return self.pieces + [lax.ppermute(p, "shard", self.swap) for p in self.pieces]


def add_low(*values_in):
    return low(sum(v.astype(jnp.float32) for v in values_in))


def over_rep(owned):
    partner = lax.ppermute(owned, "rep", [(0, 1), (1, 0)])
    return owned.astype(jnp.float32) + partner.astype(jnp.float32)


class RingSum:
    def __init__(self, mine, came, count, flip=False):
        self.up, self.down, _ = ring_moves(count)
        self.chips = count // 2
        self.sign = 1
        if flip:
            self.up, self.down, self.sign = self.down, self.up, -1
        self.mine, self.came = mine, came
        self.step = self.chips // 2
        self.upward = self.downward = None

    def at(self, distance):
        return (self.sign * distance) % self.chips

    def hop(self, after=(), carry=()):
        half = self.chips // 2
        down_at = 1 - self.step if self.step > 1 else None
        sums = hop(
            self.mine, self.came, self.upward, self.downward if down_at is not None else None,
            self.at(self.step), None if down_at is None else self.at(down_at), after, carry,
        )
        self.carried = sums[len(sums) - len(carry) :]
        self.upward = lax.ppermute(sums[0], "shard", self.up)
        if down_at is not None:
            self.downward = lax.ppermute(sums[1], "shard", self.down)
        self.step -= 1
        return [sums[0]]

    def finish(self):
        return add_low(self.mine[0], self.came[0], self.upward, self.downward)


def over_cores(other, count):
    return lax.ppermute(other, "shard", ring_moves(count)[2])


def swap_reps(part):
    return lax.ppermute(part, "rep", [(0, 1), (1, 0)])


def both_halves(rep, owned):
    partner = swap_reps(owned)
    first = rep[0] == 0
    return jnp.concatenate([jnp.where(first, owned, partner), jnp.where(first, partner, owned)], axis=0).astype(jnp.float32)


def scatter_sum(term):
    return over_rep(lax.psum_scatter(low(term), "shard", scatter_dimension=0, tiled=True))


def weight_term(left, right):
    return jnp.einsum("ra,rb->ab", left, right, preferred_element_type=jnp.float32)


def body(
    tokens,
    enc_states,
    unit_ids,
    enc_ids,
    self_q,
    self_k,
    self_v,
    self_o,
    cross_q,
    cross_k,
    cross_v,
    cross_o,
    ffn_in,
    ffn_out,
    norm_gains,
    norm_biases,
    cotangent,
):
    count = lax.axis_size("shard")
    ring = count == 16
    own, width = self_q.shape
    own_out = ffn_out.shape[0]
    parts = ffn_in.shape[1] // width
    hidden = parts * width
    own_width = norm_gains.shape[1]
    x = tokens.reshape(-1, width)
    enc = enc_states.reshape(-1, width)
    cot = cotangent.reshape(-1, width)
    row_count = x.shape[0]
    bf16, f32 = jnp.bfloat16, jnp.float32

    norm_piece = jnp.concatenate([norm_gains, norm_biases], axis=0)
    in_parts = [ffn_in[:, i * width : (i + 1) * width] for i in range(parts)]
    unit_extra, enc_extra = key_extras(unit_ids[0]), key_extras(enc_ids[0])
    query_extra = query_extras(unit_ids[0])
    self_windows = windows(unit_ids[0], unit_ids[0], 256, 256, True)
    cross_windows = windows(unit_ids[0], enc_ids[0], 256, 256, False)
    if ring:
        order, rank = ring_tables(count)
        norm_row = jnp.pad(norm_piece.reshape(1, -1), ((0, 15), (0, width - 8 * own_width)))
        rep = lax.axis_index("rep").astype(jnp.int32).reshape(1)
        piece_b = jnp.concatenate([self_o, cross_q, cross_k, cross_v, cross_o], axis=0)
        half_c = jnp.where(rep[0] == 0, jnp.concatenate(in_parts, axis=0), ffn_out)
        set_a = gather_pieces(jnp.concatenate([self_q, self_k, self_v, norm_row], axis=0), count)
        ring_b = RingGather(piece_b, count)
        ring_b.hop(set_a[count // 4])
        set_c = [lax.all_gather(half_c, ("rep", "shard"), axis=0, tiled=True)]
        norm_rows = jnp.concatenate([p[3 * own : 3 * own + 1, : 8 * own_width] for p in set_a], axis=0)
        place = (jnp.arange(count, dtype=jnp.int32)[:, None] == order[None, :]).astype(bf16)
        norms = mm(place, norm_rows)
        norms = jnp.transpose(norms.reshape(count, 8, own_width), (1, 0, 2)).reshape(8, width)
        kinds = ("ring", "ring", "tiled")
    else:
        order = jnp.zeros((1,), jnp.int32)

        def whole(part):
            return lax.all_gather(part, "shard", axis=0, tiled=True)

        set_a = [jnp.concatenate([whole(w) for w in (self_q, self_k, self_v)], axis=0)]
        set_b = [jnp.concatenate([whole(w) for w in (self_o, cross_q, cross_k, cross_v, cross_o)], axis=0)]
        set_c = [jnp.concatenate([whole(w) for w in in_parts + [ffn_out]], axis=0)]
        norms = lax.all_gather(norm_piece, "shard", axis=1, tiled=True).astype(f32)
        kinds = ("flat", "flat", "flat")
    plan_a = [(kinds[0], i * own, own, i * width, 0, count) for i in range(3)]
    plan_b = [(kinds[1], i * own, own, i * width, 0, count) for i in range(5)]
    plan_c = [(kinds[2], i * own, own, i * width, parts * own, count) for i in range(parts)]
    plan_c.append(("flat", 0, own_out, parts * width, 0, count))
    sems = pltpu.SemaphoreType.DMA
    square = 2 * row_count * width * width

    a1, q1, k1, v1 = by_rows(
        functools.partial(first_kernel, plan_a, len(set_a)), order, [x], norms, set_a,
        [(width, bf16)] * 4, False,
        [pltpu.VMEM((3, width, width), bf16), sems((3,))], 3 * square,
    )
    pairs = width // 128
    self_args = (q1, k1, v1, query_extra, unit_extra, self_windows, True)
    if ring:
        o1_low, log1_low = attend_forward(*self_args, (0, pairs // 2))
        ring_b.hop(o1_low)
        o1_high, log1_high = attend_forward(*self_args, (pairs // 2, pairs), [o1_low])
        ring_b.hop(o1_high)
        ring_b.hop()
        set_b = ring_b.finish()
    else:
        o1_low, log1_low = attend_forward(*self_args, (0, pairs // 2))
        o1_high, log1_high = attend_forward(*self_args, (pairs // 2, pairs))
    o1 = [o1_low, o1_high]
    r1, a2, q2, k2, v2 = by_rows(
        functools.partial(second_kernel, plan_b[:4], len(set_b), 2), order, o1 + [x, enc], norms, set_b,
        [(width, f32)] + [(width, bf16)] * 4, False,
        [pltpu.VMEM((4, width, width), bf16), sems((4,))], 4 * square,
    )
    o2, log2 = attend_forward(q2, k2, v2, query_extra, enc_extra, cross_windows, False, (0, pairs))
    out, a3, h, df, du, dr2, dc2, do2, terms_three = by_rows(
        functools.partial(third_kernel, plan_b[4:] + plan_c, len(set_b), len(set_c), 1), order, [o2, r1, cot], norms, set_b + set_c,
        [(width, bf16), (width, bf16), (hidden, bf16), (width, bf16), (hidden, bf16), (width, f32), (width, bf16), (width, bf16)], True,
        [
            pltpu.VMEM((width, width), bf16),
            pltpu.VMEM((parts, width, width), bf16),
            pltpu.VMEM((hidden, width), bf16),
            pltpu.VMEM((256, hidden), f32),
            sems((parts + 2,)),
        ],
        (2 + 4 * parts) * square,
    )

    cross_args = (q2, k2, v2, o2, do2, log2, enc_extra, cross_windows, False)
    if ring:
        ffn_set = ffn_terms(a3, du, h, df, count)
        ffn_set = lax.psum_scatter(ffn_set.reshape(-1, width), "shard", scatter_dimension=0, tiled=True)
    else:
        grad_in, grad_out = scatter_sum(weight_term(a3, du)), scatter_sum(weight_term(h, df))
    dq2, dk2, dv2 = attend_backward(*cross_args, (0, pairs))
    dr1, dc1, do1, terms_two = by_rows(
        functools.partial(fourth_kernel, plan_b[:2], len(set_b)), order, [dq2, r1, dr2], norms, set_b,
        [(width, f32), (width, bf16), (width, bf16)], True,
        [pltpu.VMEM((2, width, width), bf16), sems((2,))], 2 * square,
    )

    def enc_backward(after):
        return by_rows(
            functools.partial(enc_kernel, plan_b[2:4], len(set_b)), order, [dk2, dv2], norms, set_b,
            [(width, f32)], False,
            [pltpu.VMEM((2, width, width), bf16), sems((2,))], 2 * square, after,
        )[0]

    half = pairs // 2

    def self_backward(i, after):
        return attend_backward(
            q1, k1, v1, o1[i], do1, (log1_low, log1_high)[i], unit_extra, self_windows, True,
            (i * half, (i + 1) * half), i * half, after,
        )

    def fifth(groups, after, part=(0, 1), into=None):
        dq1, dk1, dv1 = ([g[i] for g in groups] for i in range(3))
        return by_rows(
            functools.partial(fifth_kernel, plan_a, len(set_a), len(groups)), order, dq1 + dk1 + dv1 + [x, dr1], norms, set_a,
            [(width, f32)], True,
            [pltpu.VMEM((3, width, width), bf16), sems((3,))], 3 * square // part[1], after, part=part, into=into,
        )

    if ring:
        groups = [self_backward(0, [])]
        groups.append(self_backward(1, [groups[0][0]]))
        mine, other = term_sets(
            rank, [tuple(o1), (a1,)],
            [(0, [(dc1, c)]) for c in range(2)] + [(1, [(g[i], 0)]) for i in range(3) for g in groups], count,
        )
        sums_a = RingSum(mine, over_cores(other, count), count, True)
        grad_x, terms_one = fifth(groups, [mine])
        last = sums_a.hop([grad_x])
        mine, other = term_sets(
            rank, [(o2,), (a2,), (enc,)],
            [(i, [(g, c)]) for i, g in ((0, dc2), (1, dq2), (2, dk2), (2, dv2)) for c in range(2)], count, last,
            [terms_one, terms_two, terms_three],
        )
        last = sums_a.hop([mine], [other])
        came = over_cores(sums_a.carried[0], count)
        grad_enc = enc_backward(last)
        keep, send = halve(rep, mine, came, [grad_enc])
        sums_b = RingSum(keep, swap_reps(send), count)
        last = sums_a.hop(sums_a.hop([keep]))
        ffn_set = over_rep(ffn_set + last[0][:1, :1] * 0)
        last = sums_b.hop(sums_b.hop(sums_b.hop(last)))
        sums_b.hop(last + [ffn_set])
        grad_a, grad_b = over_rep(sums_a.finish()), both_halves(rep, sums_b.finish())
        grad_in = jnp.concatenate([ffn_set[i * own : (i + 1) * own] for i in range(parts)], axis=1)
        grad_out = ffn_set[parts * own :]

        norm_sum = grad_b[8 * own : 8 * own + 8, :own_width]

        def columns(array, places):
            return jnp.concatenate([array[i * own : (i + 1) * own] for i in places], axis=1)

        grad_co, grad_cq, grad_ck, grad_cv = (columns(grad_b, (2 * w, 2 * w + 1)) for w in range(4))
        grad_so, grad_sq, grad_sk, grad_sv = (columns(grad_a, (2 * w, 2 * w + 1)) for w in range(4))
    else:
        grad_enc = enc_backward(())
        groups = [self_backward(i, ()) for i in range(2)]
        dq1, dk1, dv1 = (jnp.concatenate([g[i] for g in groups], axis=1) for i in range(3))
        grad_x, terms_one = fifth(groups, ())
        norm_sum = lax.psum(terms_one + terms_two + terms_three, ("rep", "shard"))
        norm_sum = lax.dynamic_slice_in_dim(norm_sum, lax.axis_index("shard") * own_width, own_width, 1)
        grad_co, grad_cq, grad_ck, grad_cv, grad_so, grad_sq, grad_sk, grad_sv = (
            scatter_sum(weight_term(a, b))
            for a, b in (
                (o2, dc2), (a2, dq2), (enc, dk2), (enc, dv2), (jnp.concatenate(o1, axis=1), dc1), (a1, dq1), (a1, dk1), (a1, dv1)
            )
        )
    return (
        out.reshape(tokens.shape),
        grad_x.reshape(tokens.shape),
        grad_enc.reshape(enc_states.shape),
        grad_sq,
        grad_sk,
        grad_sv,
        grad_so,
        grad_cq,
        grad_ck,
        grad_cv,
        grad_co,
        grad_in,
        grad_out,
        norm_sum[:4],
        norm_sum[4:],
    )


def solution(mesh):
    return jax.shard_map(
        body,
        mesh=mesh,
        in_specs=(
            P(("rep", "shard"), None, None),
            P(("rep", "shard"), None, None),
            P(("rep", "shard"), None),
            P(("rep", "shard"), None),
            P("shard", None),
            P("shard", None),
            P("shard", None),
            P("shard", None),
            P("shard", None),
            P("shard", None),
            P("shard", None),
            P("shard", None),
            P("shard", None),
            P("shard", None),
            P(None, "shard"),
            P(None, "shard"),
            P(("rep", "shard"), None, None),
        ),
        out_specs=(
            P(("rep", "shard"), None, None),
            P(("rep", "shard"), None, None),
            P(("rep", "shard"), None, None),
            P("shard", None),
            P("shard", None),
            P("shard", None),
            P("shard", None),
            P("shard", None),
            P("shard", None),
            P("shard", None),
            P("shard", None),
            P("shard", None),
            P("shard", None),
            P(None, "shard"),
            P(None, "shard"),
        ),
        check_vma=False,
    )
```

```python
import functools
import math

import jax
import jax.numpy as jnp
from jax import lax
from jax.experimental import pallas as pl
from jax.experimental.pallas import tpu as pltpu
from jax.sharding import PartitionSpec as P

HEADS = 16
HEAD = 64


eps_norm = 1e-05


COST = 4


def estimate(flops, bytes_accessed, transcendentals):
    return pl.CostEstimate(flops=flops // 8, bytes_accessed=bytes_accessed // 8, transcendentals=0)
BIG = 1e30
NT = (((1,), (1,)), ((), ()))
TN = (((0,), (0,)), ((), ()))


def key_extras(ids):
    lane = jnp.arange(128)[None, :] % 64
    return jnp.where(lane < 8, (ids[:, None] != lane).astype(jnp.bfloat16), ((lane >= 8) & (lane < 11)).astype(jnp.bfloat16))


def query_extras(ids):
    lane = jnp.arange(128)[None, :] % 64
    return jnp.where((lane < 8) & (ids[:, None] == lane), -BIG, 0.0).astype(jnp.bfloat16)


def windows(unit_ids, key_ids, bq, bk, causal):
    n = key_ids.shape[0]
    nq = unit_ids.shape[0] // bq
    blocks = unit_ids.reshape(nq, bq)
    low = jnp.sum((key_ids[None, :] < blocks[:, :1]).astype(jnp.int32), axis=1)
    if causal:
        end = (jnp.arange(nq, dtype=jnp.int32) + 1) * bq
        count = (end - low + bk - 1) // bk
        start = end - count * bk
    else:
        end = jnp.sum((key_ids[None, :] <= blocks[:, -1:]).astype(jnp.int32), axis=1)
        low = low // 16 * 16
        count = (end - low + bk - 1) // bk
        start = jnp.minimum(low, n - count * bk)
    return jnp.concatenate([start, count])


def attend_forward_kernel(bq, bk, causal, hp, norm, win_ref, q_ref, k_ref, v_ref, qx_ref, kx_ref, *rest):
    o_ref, qe_ref, ka = rest[-3:]
    L, N = q_ref.shape[0], k_ref.shape[0]
    nq = L // bq
    lane = lax.broadcasted_iota(jnp.int32, (1, 128), 1)
    first = lane < 64
    part = lane % 64
    for g in range(hp):
        kp = k_ref[:, g*128:(g+1)*128]
        ka[2*g] = jnp.where(first, kp, kx_ref[...])
        ka[2*g+1] = jnp.where(first, kx_ref[...], kp)
    row = lax.broadcasted_iota(jnp.int32, (128, 1), 0)
    rpart = row % 64
    zero = jnp.zeros((1, 128), jnp.bfloat16)

    def one(i, W):
        rows = pl.ds(pl.multiple_of(i * bq, bq), bq)
        win = pl.ds(pl.multiple_of(win_ref[i], 16), W)
        xb = qx_ref[rows, :]
        ss = []
        for h in range(2*hp):
            g = h // 2
            qb = q_ref[rows, g*128:(g+1)*128]
            qa = jnp.where(first, qb, xb) if h % 2 == 0 else jnp.where(first, xb, qb)
            s = lax.dot_general(ka[h, win, :], qa, NT, preferred_element_type=jnp.float32)
            if causal:
                tri = lax.broadcasted_iota(jnp.int32, (bq, bq), 0) <= lax.broadcasted_iota(jnp.int32, (bq, bq), 1)
                d = jnp.where(tri, s[W - bq:, :], -BIG)
                s = d if W == bq else jnp.concatenate([s[: W - bq, :], d], axis=0)
            ss.append(s)
        outs, invs, lses = [], [], []
        for h in range(2*hp):
            g = h // 2
            s = ss[h]
            m = jnp.max(s, axis=0, keepdims=True)
            p = jnp.exp(s - m)
            l = jnp.sum(p, axis=0, keepdims=True)
            inv = 1.0 / l
            if norm: p = p * inv
            vw = v_ref[win, g*128:(g+1)*128]
            vw = jnp.where(first, vw, zero) if h % 2 == 0 else jnp.where(first, zero, vw)
            outs.append(lax.dot_general(vw, p.astype(jnp.bfloat16), TN, preferred_element_type=jnp.float32)); invs.append(inv)
            neg = -(m + jnp.log(l))
            hi = neg.astype(jnp.bfloat16).astype(jnp.float32)
            mid = (neg - hi).astype(jnp.bfloat16).astype(jnp.float32)
            lo = neg - hi - mid
            lses.append((hi, mid, lo))
        for g in range(hp):
            o = outs[2*g] + outs[2*g+1]
            if not norm:
                o = o * jnp.where(row < 64, invs[2*g], invs[2*g+1])
            o = jnp.transpose(o)
            o_ref[rows, g*128:(g+1)*128] = o.astype(jnp.bfloat16)
            a, b = lses[2*g], lses[2*g+1]
            e = jnp.where(row < 64, jnp.where(rpart == 8, b[0], jnp.where(rpart == 9, b[1], b[2])), jnp.where(rpart == 8, a[0], jnp.where(rpart == 9, a[1], a[2])))
            e = jnp.transpose(jnp.where((rpart >= 8) & (rpart < 11), e, 0.0))
            qe_ref[rows, g*128:(g+1)*128] = jnp.where(part < 8, xb.astype(jnp.float32), e).astype(jnp.bfloat16)

    def step(i, c):
        for j in range(bq // bk if causal else 1, N // bk + 1):
            @pl.when(win_ref[nq + i] == j)
            def _():
                one(i, j * bk)
        return c

    lax.fori_loop(0, nq, step, 0)

def attend_forward(q, k, v, qx, kx, win, causal, pairs, after=(), bq=256, bk=128, hp=4):
    L, N = q.shape[0], k.shape[0]
    w = 128 * hp
    start, number = pairs[0] // hp, (pairs[1] - pairs[0]) // hp
    col = lambda n: pl.BlockSpec((n, w), lambda p, _: (0, start + p))
    own = lambda n: pl.BlockSpec((n, w), lambda p, _: (0, p))
    fix = lambda n: pl.BlockSpec((n, 128), lambda p, _: (0, 0))
    return pl.pallas_call(
        functools.partial(attend_forward_kernel, bq, bk, causal, hp, True),
        grid_spec=pltpu.PrefetchScalarGridSpec(
            num_scalar_prefetch=1,
            grid=(number,),
            in_specs=[col(L), col(N), col(N), fix(L), fix(N)] + [pl.BlockSpec(memory_space=pl.ANY)] * len(after),
            out_specs=[own(L), own(L)],
            scratch_shapes=[pltpu.VMEM((2 * hp, N, 128), jnp.bfloat16)],
        ),
        out_shape=[jax.ShapeDtypeStruct((L, number * w), jnp.bfloat16)] * 2,
        compiler_params=pltpu.CompilerParams(vmem_limit_bytes=56 << 20),
        cost_estimate=estimate(
            flops=COST * 2 * 2 * L * N * number * w, bytes_accessed=10 * L * number * w, transcendentals=0
        ),
    )(win, q, k, v, qx, kx, *after)


def attend_backward_kernel(bq, bk, causal, hp, win_ref, q_ref, k_ref, v_ref, o_ref, do_ref, qe_ref, kx_ref, *rest):
    dq_ref, dk_ref, dv_ref, ka, va, dka, dva = rest[-7:]
    L, N = q_ref.shape[0], k_ref.shape[0]
    nq = L // bq
    lane = lax.broadcasted_iota(jnp.int32, (1, 128), 1)
    first = lane < 64
    part = lane % 64
    ones = jnp.broadcast_to(jnp.where(part < 3, 1.0, 0.0).astype(jnp.bfloat16), (N, 128))
    for g in range(hp):
        c = slice(g*128,(g+1)*128)
        ka[2*g] = jnp.where(first, k_ref[:, c], kx_ref[...])
        ka[2*g+1] = jnp.where(first, kx_ref[...], k_ref[:, c])
        va[2*g] = jnp.where(first, v_ref[:, c], ones)
        va[2*g+1] = jnp.where(first, ones, v_ref[:, c])
    dka[...] = jnp.zeros_like(dka)
    dva[...] = jnp.zeros_like(dva)
    zero = jnp.zeros((1, 128), jnp.bfloat16)

    def one(i, W):
        rows = pl.ds(pl.multiple_of(i * bq, bq), bq)
        win = pl.ds(pl.multiple_of(win_ref[i], 16), W)
        S = []
        for g in range(hp):
            c = slice(g*128,(g+1)*128)
            qb, xb, dob = q_ref[rows, c], qe_ref[rows, c], do_ref[rows, c]
            prod = dob.astype(jnp.float32) * o_ref[rows, c].astype(jnp.float32)
            for h in range(2):
                mine = first if h == 0 else jnp.logical_not(first)
                neg = -jnp.sum(jnp.where(mine, prod, 0.0), axis=1, keepdims=True)
                hi = neg.astype(jnp.bfloat16).astype(jnp.float32)
                mid = (neg - hi).astype(jnp.bfloat16).astype(jnp.float32)
                lo = neg - hi - mid
                de = jnp.where(part == 0, hi, jnp.where(part == 1, mid, jnp.where(part == 2, lo, 0.0))).astype(jnp.bfloat16)
                qa = jnp.where(mine, qb, xb)
                da = jnp.where(mine, dob, de)
                s = lax.dot_general(ka[2*g+h, win, :], qa, NT, preferred_element_type=jnp.float32)
                dp = lax.dot_general(va[2*g+h, win, :], da, NT, preferred_element_type=jnp.float32)
                S.append((s, dp))
        for g in range(hp):
            c = slice(g*128,(g+1)*128)
            qb, dob = q_ref[rows, c], do_ref[rows, c]
            ps, dss = [], []
            for h in range(2):
                s, dp = S[2*g+h]
                if causal:
                    tri = lax.broadcasted_iota(jnp.int32, (bq, bq), 0) <= lax.broadcasted_iota(jnp.int32, (bq, bq), 1)
                    d = jnp.where(tri, s[W - bq:, :], -BIG)
                    s = d if W == bq else jnp.concatenate([s[: W - bq, :], d], axis=0)
                p = jnp.exp(s)
                dss.append((p * dp).astype(jnp.bfloat16))
                ps.append(p.astype(jnp.bfloat16))
            docat = jnp.concatenate([jnp.where(first, dob, zero), jnp.where(first, zero, dob)], axis=0)
            qcat = jnp.concatenate([jnp.where(first, qb, zero), jnp.where(first, zero, qb)], axis=0)
            dva[win, c] += jnp.dot(jnp.concatenate(ps, axis=1), docat, preferred_element_type=jnp.float32)
            dka[win, c] += jnp.dot(jnp.concatenate(dss, axis=1), qcat, preferred_element_type=jnp.float32)
            kw = k_ref[win, c]
            k0, k1 = jnp.where(first, kw, zero), jnp.where(first, zero, kw)
            turned = lax.dot_general(k0, dss[0], TN, preferred_element_type=jnp.float32)
            turned = turned + lax.dot_general(k1, dss[1], TN, preferred_element_type=jnp.float32)
            dq = jnp.transpose(turned)
            dq_ref[rows, c] = (dq * 0.125).astype(jnp.bfloat16)

    def step(i, c):
        for j in range(bq // bk if causal else 1, N // bk + 1):
            @pl.when(win_ref[nq + i] == j)
            def _():
                one(i, j * bk)
        return c

    lax.fori_loop(0, nq, step, 0)
    dk_ref[...] = dka[...].astype(jnp.bfloat16)
    dv_ref[...] = dva[...].astype(jnp.bfloat16)

def attend_backward(q, k, v, o, do, qe, kx, win, causal, pairs, base=0, after=(), bq=256, bk=128, hp=2):
    L, N = q.shape[0], k.shape[0]
    w = 128 * hp
    start, number, base = pairs[0] // hp, (pairs[1] - pairs[0]) // hp, base // hp
    col = lambda n: pl.BlockSpec((n, w), lambda p, _: (0, start + p))
    own = lambda n: pl.BlockSpec((n, w), lambda p, _: (0, p))
    held = pl.BlockSpec((L, w), lambda p, _: (0, start - base + p))
    fix = lambda n: pl.BlockSpec((n, 128), lambda p, _: (0, 0))
    return pl.pallas_call(
        functools.partial(attend_backward_kernel, bq, bk, causal, hp),
        grid_spec=pltpu.PrefetchScalarGridSpec(
            num_scalar_prefetch=1,
            grid=(number,),
            in_specs=[col(L), col(N), col(N), held, col(L), held, fix(N)]
            + [pl.BlockSpec(memory_space=pl.ANY)] * len(after),
            out_specs=[own(L), own(N), own(N)],
            scratch_shapes=[pltpu.VMEM((2 * hp, N, 128), jnp.bfloat16)] * 2 + [pltpu.VMEM((N, w), jnp.float32)] * 2,
        ),
        out_shape=[jax.ShapeDtypeStruct((L, number * w), jnp.bfloat16)]
        + [jax.ShapeDtypeStruct((N, number * w), jnp.bfloat16)] * 2,
        compiler_params=pltpu.CompilerParams(vmem_limit_bytes=58 << 20),
        cost_estimate=estimate(
            flops=COST * 5 * 2 * L * N * number * w, bytes_accessed=16 * L * number * w, transcendentals=0
        ),
    )(win, q, k, v, o, do, qe, kx, *after)


def fetch(plan, refs, order_ref, dst, sem):
    kind, offset, rows, flat, piece_rows, count = plan
    if kind == "flat":
        part = rows * count // 16
        for j in range(16):
            pltpu.make_async_copy(refs[0].at[pl.ds(flat + j * part, part)], dst.at[pl.ds(j * part, part)], sem).start()
        return
    for j in range(count):
        if kind == "ring":
            src = refs[j].at[pl.ds(offset, rows)]
            at = pl.multiple_of(order_ref[j] * rows, 16)
        else:
            src = refs[0].at[pl.ds(j * piece_rows + offset, rows)]
            at = j * rows
        pltpu.make_async_copy(src, dst.at[pl.ds(at, rows)], sem).start()


def arrived(dst, sem):
    pltpu.make_async_copy(dst, dst, sem).wait()


def normed(values_in):
    centre = values_in - jnp.mean(values_in, axis=-1, keepdims=True)
    spread = jnp.mean(centre * centre, axis=-1, keepdims=True)
    scale = lax.rsqrt(spread + eps_norm)
    return centre * scale, scale


def normed_back(unit, scale, gain, grad_out):
    grad_unit = grad_out * gain
    inner = jnp.mean(grad_unit * unit, axis=-1, keepdims=True)
    return (grad_unit - jnp.mean(grad_unit, axis=-1, keepdims=True) - unit * inner) * scale


def mm(left, right):
    return jnp.dot(left, right, preferred_element_type=jnp.float32)


def mm_back(left, right):
    return lax.dot_general(left, right, NT, preferred_element_type=jnp.float32)


def low(values_in):
    return values_in.astype(jnp.bfloat16)


def term_rows(refs, at, values_in):
    refs[at : at + 1, :] += jnp.sum(values_in, axis=0, keepdims=True)


def first_kernel(plans, n_refs, order_ref, x_ref, norm_ref, *rest):
    refs, (a_ref, q_ref, k_ref, v_ref, w, sem) = rest[:n_refs], rest[-6:]

    @pl.when(pl.program_id(0) == 0)
    def _():
        for i in range(3):
            fetch(plans[i], refs, order_ref, w.at[i], sem.at[i])
        for i in range(3):
            arrived(w.at[i], sem.at[i])

    unit, _ = normed(x_ref[...].astype(jnp.float32))
    a = low(unit * norm_ref[0:1, :] + norm_ref[4:5, :])
    a_ref[...] = a
    q_ref[...] = low(mm(a, w[0]) * 0.125)
    k_ref[...] = low(mm(a, w[1]))
    v_ref[...] = low(mm(a, w[2]))


def joined(refs):
    return refs[0][...] if len(refs) == 1 else jnp.concatenate([r[...] for r in refs], axis=1)


def second_kernel(plans, n_refs, n_o, order_ref, *rest):
    o_refs, (x_ref, e_ref, norm_ref), rest = rest[:n_o], rest[n_o : n_o + 3], rest[n_o + 3 :]
    refs, (r_ref, a_ref, q_ref, k_ref, v_ref, w, sem) = rest[:n_refs], rest[-7:]

    @pl.when(pl.program_id(0) == 0)
    def _():
        for i in range(4):
            fetch(plans[i], refs, order_ref, w.at[i], sem.at[i])
        for i in range(4):
            arrived(w.at[i], sem.at[i])

    r = x_ref[...].astype(jnp.float32) + mm(joined(o_refs), w[0])
    r_ref[...] = r
    k_ref[...] = low(mm(e_ref[...], w[2]))
    v_ref[...] = low(mm(e_ref[...], w[3]))
    unit, _ = normed(r)
    a = low(unit * norm_ref[1:2, :] + norm_ref[5:6, :])
    a_ref[...] = a
    q_ref[...] = low(mm(a, w[1]) * 0.125)


def third_kernel(plans, n_b, n_c, n_o, order_ref, *rest):
    o_refs, (r_ref, cot_ref, norm_ref), rest = rest[:n_o], rest[n_o : n_o + 3], rest[n_o + 3 :]
    refs_b, refs_c = rest[:n_b], rest[n_b : n_b + n_c]
    (out_ref, a_ref, h_ref, df_ref, du_ref, dr_ref, dc_ref, do_ref, term_ref, wc, wi, wo, slope, sem) = rest[-14:]
    parts = wi.shape[0]
    first = pl.program_id(0) == 0

    @pl.when(first)
    def _():
        fetch(plans[0], refs_b, order_ref, wc, sem.at[0])
        for i in range(parts):
            fetch(plans[1 + i], refs_c, order_ref, wi.at[i], sem.at[1 + i])
        fetch(plans[1 + parts], refs_c, order_ref, wo, sem.at[1 + parts])
        term_ref[...] = jnp.zeros_like(term_ref)
        arrived(wc, sem.at[0])

    r2 = r_ref[...] + mm(joined(o_refs), wc[...])
    unit2, scale2 = normed(r2)
    a3 = low(unit2 * norm_ref[2:3, :] + norm_ref[6:7, :])
    a_ref[...] = a3

    @pl.when(first)
    def _():
        for i in range(parts):
            arrived(wi.at[i], sem.at[1 + i])
        arrived(wo, sem.at[1 + parts])

    width = wi.shape[2]
    r3 = r2
    for i in range(parts):
        cols = slice(i * width, (i + 1) * width)
        u = mm(a3, wi[i])
        half = 0.5 * (1.0 + lax.erf(u * (1.0 / math.sqrt(2.0))))
        h = low(u * half)
        h_ref[:, cols] = h
        slope[:, cols] = half + u * jnp.exp(-0.5 * u * u) * (1.0 / math.sqrt(2.0 * math.pi))
        r3 = r3 + mm(h, wo[cols, :])
    unit3, scale3 = normed(r3)
    out_ref[...] = low(unit3 * norm_ref[3:4, :] + norm_ref[7:8, :])
    cot = cot_ref[...].astype(jnp.float32)
    term_rows(term_ref, 3, cot * unit3)
    term_rows(term_ref, 7, cot)
    dr3 = normed_back(unit3, scale3, norm_ref[3:4, :], cot)
    df = low(dr3)
    df_ref[...] = df
    da3 = jnp.zeros_like(dr3)
    for i in range(parts):
        cols = slice(i * width, (i + 1) * width)
        du = low(mm_back(df, wo[cols, :]) * slope[:, cols])
        du_ref[:, cols] = du
        da3 = da3 + mm_back(du, wi[i])
    term_rows(term_ref, 2, da3 * unit2)
    term_rows(term_ref, 6, da3)
    dr2 = dr3 + normed_back(unit2, scale2, norm_ref[2:3, :], da3)
    dr_ref[...] = dr2
    dc = low(dr2)
    dc_ref[...] = dc
    do_ref[...] = low(mm_back(dc, wc[...]))


def fourth_kernel(plans, n_refs, order_ref, dq_ref, r_ref, dr_ref, norm_ref, *rest):
    refs, (dx_ref, dc_ref, do_ref, term_ref, w, sem) = rest[:n_refs], rest[-6:]

    @pl.when(pl.program_id(0) == 0)
    def _():
        for i in range(2):
            fetch(plans[i], refs, order_ref, w.at[i], sem.at[i])
        for i in range(2):
            arrived(w.at[i], sem.at[i])
        term_ref[...] = jnp.zeros_like(term_ref)

    da = mm_back(dq_ref[...], w[1])
    unit, scale = normed(r_ref[...])
    term_rows(term_ref, 1, da * unit)
    term_rows(term_ref, 5, da)
    dx = dr_ref[...] + normed_back(unit, scale, norm_ref[1:2, :], da)
    dx_ref[...] = dx
    dc = low(dx)
    dc_ref[...] = dc
    do_ref[...] = low(mm_back(dc, w[0]))


def enc_kernel(plans, n_refs, order_ref, dk_ref, dv_ref, norm_ref, *rest):
    refs, (de_ref, w, sem) = rest[:n_refs], rest[-3:]

    @pl.when(pl.program_id(0) == 0)
    def _():
        for i in range(2):
            fetch(plans[i], refs, order_ref, w.at[i], sem.at[i])
        for i in range(2):
            arrived(w.at[i], sem.at[i])

    de_ref[...] = mm_back(dk_ref[...], w[0]) + mm_back(dv_ref[...], w[1])


def fifth_kernel(plans, n_refs, n_g, order_ref, *rest):
    dq_refs, dk_refs, dv_refs = (rest[i * n_g : (i + 1) * n_g] for i in range(3))
    (x_ref, dr_ref, norm_ref), rest = rest[3 * n_g : 3 * n_g + 3], rest[3 * n_g + 3 :]
    refs, (dx_ref, term_ref, w, sem) = rest[:n_refs], rest[-4:]

    @pl.when(pl.program_id(0) == 0)
    def _():
        for i in range(3):
            fetch(plans[i], refs, order_ref, w.at[i], sem.at[i])
        for i in range(3):
            arrived(w.at[i], sem.at[i])
        term_ref[...] = jnp.zeros_like(term_ref)

    da = mm_back(joined(dq_refs), w[0]) + mm_back(joined(dk_refs), w[1]) + mm_back(joined(dv_refs), w[2])
    unit, scale = normed(x_ref[...].astype(jnp.float32))
    term_rows(term_ref, 0, da * unit)
    term_rows(term_ref, 4, da)
    dx_ref[...] = dr_ref[...] + normed_back(unit, scale, norm_ref[0:1, :], da)


def by_rows(kernel, order, row_inputs, norms, piece_refs, row_outputs, terms, scratch, flops, after=(), block=256, part=(0, 1), into=None):
    rows = row_inputs[0].shape[0]
    steps = rows // block // part[1]
    first = part[0] * steps
    piece_refs = list(piece_refs) + list(after) + ([] if into is None else [into])
    aliases = {} if into is None else {1 + len(row_inputs) + len(piece_refs): 0}

    def spec(width):
        return pl.BlockSpec((block, width), lambda i, _: (first + i, 0))

    def fixed(shape):
        return pl.BlockSpec(shape, lambda i, _: (0, 0))

    out_shape = [jax.ShapeDtypeStruct((rows, w), t) for w, t in row_outputs]
    out_specs = [spec(w) for w, _ in row_outputs]
    if terms:
        out_shape.append(jax.ShapeDtypeStruct(norms.shape, jnp.float32))
        out_specs.append(fixed(norms.shape))
    moved = sum(x.size * x.dtype.itemsize for x in row_inputs) + sum(rows * w * t.dtype.itemsize if hasattr(t, "dtype") else rows * w * jnp.dtype(t).itemsize for w, t in row_outputs)
    return pl.pallas_call(
        kernel,
        grid_spec=pltpu.PrefetchScalarGridSpec(
            num_scalar_prefetch=1,
            grid=(steps,),
            in_specs=[spec(x.shape[1]) for x in row_inputs]
            + [fixed(norms.shape)]
            + [pl.BlockSpec(memory_space=pl.ANY)] * len(piece_refs),
            out_specs=out_specs,
            scratch_shapes=scratch,
        ),
        out_shape=out_shape,
        input_output_aliases=aliases,
        compiler_params=pltpu.CompilerParams(vmem_limit_bytes=58 << 20),
        cost_estimate=estimate(flops=flops, bytes_accessed=moved, transcendentals=0),
    )(order, *row_inputs, norms, *piece_refs)


def term_kernel(names, chips, n_left, n_right, n_extra, rank_ref, *rest):
    parts = len(names)
    extra, rest = rest[:n_extra], rest[n_extra:]
    flat, rest = rest[: sum(n_left)], rest[sum(n_left) :]
    lefts = [flat[sum(n_left[:i]) : sum(n_left[: i + 1])] for i in range(len(n_left))]
    rights = [rest[sum(n_right[:i]) : sum(n_right[: i + 1])] for i in range(parts)]
    mine_ref, other_ref, turned = rest[-3:]
    rows = turned.shape[0] // (2 * chips)

    def deal(chip, at, number, one, two):
        core = rank_ref[chips]
        mine_ref[rank_ref[chip], at : at + number] = jnp.where(core == 0, one, two)
        other_ref[rank_ref[chip], at : at + number] = jnp.where(core == 0, two, one)

    for i in range(parts):

        @pl.when(pl.program_id(0) == i)
        def _():
            if i == 0 or names[i] != names[i - 1]:
                turned[...] = jnp.transpose(joined(lefts[names[i]]))
            total = low(mm(turned[...], joined(rights[i])))
            for chip in range(chips):
                one = total[2 * chip * rows : (2 * chip + 1) * rows]
                two = total[(2 * chip + 1) * rows : (2 * chip + 2) * rows]
                deal(chip, i * rows if extra else 0, rows, one, two)
            if extra and i == 0:
                terms = extra[0][...] + extra[1][...] + extra[2][...]
                empty = jnp.zeros((8, 512 - rows), jnp.float32)
                for chip in range(chips):
                    one, two = (
                        low(jnp.concatenate([jnp.concatenate([terms[:, s * rows : (s + 1) * rows], empty], axis=1), jnp.zeros((24, 512), jnp.float32)], axis=0))
                        for s in (2 * chip, 2 * chip + 1)
                    )
                    deal(chip, parts * rows, 32, one, two)


def term_sets(rank, lefts, parts, count, after=(), extra=()):
    total, depth = sum(x.shape[1] for x in lefts[0]), lefts[0][0].shape[0]
    flat = [x for left in lefts for x in left]
    rows = total // count
    chips = count // 2
    number = len(parts)
    all_rows = number * rows + (32 if extra else 0)
    rights, specs = [], []
    for _, given in parts:
        for x, c in given:
            rights.append(x)
            specs.append(pl.BlockSpec((depth, 512 // len(given)), lambda n, _, c=c: (0, c)))
    return pl.pallas_call(
        functools.partial(term_kernel, [p[0] for p in parts], chips, [len(left) for left in lefts], [len(p[1]) for p in parts], len(extra)),
        grid_spec=pltpu.PrefetchScalarGridSpec(
            num_scalar_prefetch=1,
            grid=(number,),
            in_specs=[pl.BlockSpec(x.shape, lambda n, _: (0, 0)) for x in [*extra, *flat]]
            + specs
            + [pl.BlockSpec(memory_space=pl.ANY)] * len(after),
            out_specs=[pl.BlockSpec((chips, all_rows, 512), lambda n, _: (0, 0, 0)) if extra else pl.BlockSpec((chips, rows, 512), lambda n, _: (0, n, 0))] * 2,
            scratch_shapes=[pltpu.VMEM((total, depth), jnp.bfloat16)],
        ),
        out_shape=[jax.ShapeDtypeStruct((chips, all_rows, 512), jnp.bfloat16)] * 2,
        compiler_params=pltpu.CompilerParams(vmem_limit_bytes=58 << 20),
        cost_estimate=estimate(
            flops=2 * number * total * 512 * depth, bytes_accessed=6 * number * total * 512, transcendentals=0
        ),
    )(rank, *extra, *flat, *rights, *after)


def ffn_term_kernel(left_ref, right_ref, *rest):
    total = lax.dot_general(left_ref[...], right_ref[...], TN, preferred_element_type=jnp.float32)
    rest[-1][...] = low(total).reshape(rest[-1].shape)


def ffn_terms(a, du, h, df, count):
    depth, width = a.shape
    parts = du.shape[1] // width
    rows_in, rows_out = width // count, parts * width // count
    out_shape = jax.ShapeDtypeStruct((count, parts * rows_in + rows_out, width), jnp.bfloat16)
    whole = pl.BlockSpec((depth, width), lambda n: (0, 0))
    part = pl.BlockSpec((depth, width), lambda n: (0, n))
    params = pltpu.CompilerParams(vmem_limit_bytes=58 << 20)
    cost = estimate(flops=2 * parts * depth * width * width, bytes_accessed=6 * parts * width * width, transcendentals=0)
    terms = pl.pallas_call(
        ffn_term_kernel,
        grid=(parts,),
        in_specs=[whole, part],
        out_specs=pl.BlockSpec((count, rows_in, width), lambda n: (0, n, 0)),
        out_shape=out_shape,
        compiler_params=params,
        cost_estimate=cost,
    )(a, du)
    return pl.pallas_call(
        ffn_term_kernel,
        grid=(parts,),
        in_specs=[part, whole, pl.BlockSpec(memory_space=pl.ANY)],
        out_specs=pl.BlockSpec((width // rows_out, rows_out, width), lambda n: (n, 1, 0)),
        out_shape=out_shape,
        input_output_aliases={2: 0},
        compiler_params=params,
        cost_estimate=cost,
    )(h, df, terms)


def halve_kernel(rep_ref, mine_ref, came_ref, *rest):
    keep_ref, send_ref = rest[-2:]
    total = low(mine_ref[...].astype(jnp.float32) + came_ref[...].astype(jnp.float32))
    half = total.shape[1] // 2
    one, two = total[:, :half], total[:, half:]
    keep_ref[...] = jnp.where(rep_ref[0] == 0, one, two)
    send_ref[...] = jnp.where(rep_ref[0] == 0, two, one)


def halve(rep, mine, came, after=()):
    chips, rows, width = mine.shape
    spec = pl.BlockSpec((2, rows, width), lambda i, _: (i, 0, 0))
    out = pl.BlockSpec((2, rows // 2, width), lambda i, _: (i, 0, 0))
    return pl.pallas_call(
        halve_kernel,
        grid_spec=pltpu.PrefetchScalarGridSpec(
            num_scalar_prefetch=1,
            grid=(chips // 2,),
            in_specs=[spec, spec] + [pl.BlockSpec(memory_space=pl.ANY)] * len(after),
            out_specs=[out, out],
        ),
        out_shape=[jax.ShapeDtypeStruct((chips, rows // 2, width), jnp.bfloat16)] * 2,
        compiler_params=pltpu.CompilerParams(vmem_limit_bytes=32 << 20),
        cost_estimate=estimate(flops=2 * mine.size, bytes_accessed=6 * mine.size, transcendentals=0),
    )(rep, mine, came, *after)


def hop_kernel(first, second, carried, *rest):
    rest = rest[: len(rest) - carried]
    if first:
        mine_up, came_up, mine_down, came_down = rest[:4]
        up = mine_up[0].astype(jnp.float32) + came_up[0].astype(jnp.float32)
        down = mine_down[0].astype(jnp.float32) + came_down[0].astype(jnp.float32)
        rest[-2][...] = low(up)
        rest[-1][...] = low(down)
        return
    up_ref, mine_up, came_up = rest[:3]
    up = up_ref[...].astype(jnp.float32) + mine_up[0].astype(jnp.float32) + came_up[0].astype(jnp.float32)
    if not second:
        rest[-1][...] = low(up)
        return
    down_ref, mine_down, came_down = rest[3:6]
    down = down_ref[...].astype(jnp.float32) + mine_down[0].astype(jnp.float32) + came_down[0].astype(jnp.float32)
    rest[-2][...] = low(up)
    rest[-1][...] = low(down)


def hop(mine, came, up, down, up_at, down_at, after=(), carry=()):
    rows, width = mine.shape[1:]
    blocks = 2 if rows % 32 == 0 else 1
    part = rows // blocks

    def pick(at):
        return pl.BlockSpec((1, part, width), lambda i: (at, i, 0))

    flat = pl.BlockSpec((part, width), lambda i: (i, 0))
    args, specs = [], []
    if up is not None:
        args.append(up)
        specs.append(flat)
    args += [mine, came]
    specs += [pick(up_at)] * 2
    if down_at is not None:
        if down is not None:
            args.append(down)
            specs.append(flat)
        args += [mine, came]
        specs += [pick(down_at)] * 2
    number = 1 if down_at is None else 2
    return pl.pallas_call(
        functools.partial(hop_kernel, up is None, down_at is not None, len(carry)),
        grid=(blocks,),
        in_specs=specs + [pl.BlockSpec(memory_space=pl.ANY)] * (len(after) + len(carry)),
        out_specs=[flat] * number + [pl.BlockSpec(memory_space=pl.ANY)] * len(carry),
        out_shape=[jax.ShapeDtypeStruct((rows, width), jnp.bfloat16)] * number
        + [jax.ShapeDtypeStruct(x.shape, x.dtype) for x in carry],
        input_output_aliases={len(args) + len(after) + i: number + i for i in range(len(carry))},
        cost_estimate=estimate(flops=4 * rows * width, bytes_accessed=16 * rows * width, transcendentals=0),
    )(*args, *after, *carry)


def ring_walk(chips):
    half = chips // 2
    return [2 * i for i in range(half)] + [2 * i + 1 for i in reversed(range(half))]


def ring_moves(count):
    walk = ring_walk(count // 2)
    chips = len(walk)
    up = [(2 * walk[i] + c, 2 * walk[(i + 1) % chips] + c) for i in range(chips) for c in range(2)]
    down = [(b, a) for a, b in up]
    swap = [(i, i ^ 1) for i in range(count)]
    return up, down, swap


def ring_tables(count):
    chips = count // 2
    walk = ring_walk(chips)
    place = [0] * chips
    for at, chip in enumerate(walk):
        place[chip] = at
    order, rank = [], []
    for shard in range(count):
        at, core = place[shard // 2], shard % 2
        near = [walk[(at + k) % chips] for k in range(chips)]
        order.append([2 * c + core for c in near] + [2 * c + 1 - core for c in near])
        rank.append([(place[c] - at) % chips for c in range(chips)] + [core])
    me = lax.axis_index("shard")
    return jnp.array(order, jnp.int32)[me], jnp.array(rank, jnp.int32)[me]


def gather_pieces(piece, count):
    up, down, swap = ring_moves(count)
    chips = count // 2
    pieces = [piece] + [None] * (chips - 1)
    upward = downward = piece
    for step in range(1, chips // 2 + 1):
        upward = lax.ppermute(upward, "shard", up)
        pieces[chips - step] = upward
        if step < chips // 2:
            downward = lax.ppermute(downward, "shard", down)
            pieces[step] = downward
    return pieces + [lax.ppermute(p, "shard", swap) for p in pieces]


class RingGather:
    def __init__(self, piece, count):
        self.up, self.down, self.swap = ring_moves(count)
        self.chips = count // 2
        self.pieces = [piece] + [None] * (self.chips - 1)
        self.step = 0

    def hop(self, *after):
        last, half = self.step, self.chips // 2
        upward, downward = self.pieces[-last % self.chips], self.pieces[last]
        held = sum(low(a[:1, :1]) for a in after) * 0
        self.step += 1
        self.pieces[self.chips - self.step] = lax.ppermute(upward + held, "shard", self.up)
        if self.step < half:
            self.pieces[self.step] = lax.ppermute(downward + held, "shard", self.down)

    def finish(self):
        return self.pieces + [lax.ppermute(p, "shard", self.swap) for p in self.pieces]


def add_low(*values_in):
    return low(sum(v.astype(jnp.float32) for v in values_in))


def over_rep(owned):
    partner = lax.ppermute(owned, "rep", [(0, 1), (1, 0)])
    return owned.astype(jnp.float32) + partner.astype(jnp.float32)


class RingSum:
    def __init__(self, mine, came, count, flip=False):
        self.up, self.down, _ = ring_moves(count)
        self.chips = count // 2
        self.sign = 1
        if flip:
            self.up, self.down, self.sign = self.down, self.up, -1
        self.mine, self.came = mine, came
        self.step = self.chips // 2
        self.upward = self.downward = None

    def at(self, distance):
        return (self.sign * distance) % self.chips

    def hop(self, after=(), carry=()):
        half = self.chips // 2
        down_at = 1 - self.step if self.step > 1 else None
        sums = hop(
            self.mine, self.came, self.upward, self.downward if down_at is not None else None,
            self.at(self.step), None if down_at is None else self.at(down_at), after, carry,
        )
        self.carried = sums[len(sums) - len(carry) :]
        self.upward = lax.ppermute(sums[0], "shard", self.up)
        if down_at is not None:
            self.downward = lax.ppermute(sums[1], "shard", self.down)
        self.step -= 1
        return [sums[0]]

    def finish(self):
        return add_low(self.mine[0], self.came[0], self.upward, self.downward)


def over_cores(other, count):
    return lax.ppermute(other, "shard", ring_moves(count)[2])


def swap_reps(part):
    return lax.ppermute(part, "rep", [(0, 1), (1, 0)])


def both_halves(rep, owned):
    partner = swap_reps(owned)
    first = rep[0] == 0
    return jnp.concatenate([jnp.where(first, owned, partner), jnp.where(first, partner, owned)], axis=0).astype(jnp.float32)


def scatter_sum(term):
    return over_rep(lax.psum_scatter(low(term), "shard", scatter_dimension=0, tiled=True))


def weight_term(left, right):
    return jnp.einsum("ra,rb->ab", left, right, preferred_element_type=jnp.float32)


def body(
    tokens,
    enc_states,
    unit_ids,
    enc_ids,
    self_q,
    self_k,
    self_v,
    self_o,
    cross_q,
    cross_k,
    cross_v,
    cross_o,
    ffn_in,
    ffn_out,
    norm_gains,
    norm_biases,
    cotangent,
):
    count = lax.axis_size("shard")
    ring = count == 16
    own, width = self_q.shape
    own_out = ffn_out.shape[0]
    parts = ffn_in.shape[1] // width
    hidden = parts * width
    own_width = norm_gains.shape[1]
    x = tokens.reshape(-1, width)
    enc = enc_states.reshape(-1, width)
    cot = cotangent.reshape(-1, width)
    row_count = x.shape[0]
    bf16, f32 = jnp.bfloat16, jnp.float32

    norm_piece = jnp.concatenate([norm_gains, norm_biases], axis=0)
    in_parts = [ffn_in[:, i * width : (i + 1) * width] for i in range(parts)]
    unit_extra, enc_extra = key_extras(unit_ids[0]), key_extras(enc_ids[0])
    query_extra = query_extras(unit_ids[0])
    self_windows = windows(unit_ids[0], unit_ids[0], 256, 128, True)
    cross_windows = windows(unit_ids[0], enc_ids[0], 256, 128, False)
    if ring:
        order, rank = ring_tables(count)
        norm_row = jnp.pad(norm_piece.reshape(1, -1), ((0, 15), (0, width - 8 * own_width)))
        rep = lax.axis_index("rep").astype(jnp.int32).reshape(1)
        piece_b = jnp.concatenate([self_o, cross_q, cross_k, cross_v, cross_o], axis=0)
        half_c = jnp.where(rep[0] == 0, jnp.concatenate(in_parts, axis=0), ffn_out)
        set_a = gather_pieces(jnp.concatenate([self_q, self_k, self_v, norm_row], axis=0), count)
        ring_b = RingGather(piece_b, count)
        ring_b.hop(set_a[count // 4])
        set_c = [lax.all_gather(half_c, ("rep", "shard"), axis=0, tiled=True)]
        norm_rows = jnp.concatenate([p[3 * own : 3 * own + 1, : 8 * own_width] for p in set_a], axis=0)
        place = (jnp.arange(count, dtype=jnp.int32)[:, None] == order[None, :]).astype(bf16)
        norms = mm(place, norm_rows)
        norms = jnp.transpose(norms.reshape(count, 8, own_width), (1, 0, 2)).reshape(8, width)
        kinds = ("ring", "ring", "tiled")
    else:
        order = jnp.zeros((1,), jnp.int32)

        def whole(part):
            return lax.all_gather(part, "shard", axis=0, tiled=True)

        set_a = [jnp.concatenate([whole(w) for w in (self_q, self_k, self_v)], axis=0)]
        set_b = [jnp.concatenate([whole(w) for w in (self_o, cross_q, cross_k, cross_v, cross_o)], axis=0)]
        set_c = [jnp.concatenate([whole(w) for w in in_parts + [ffn_out]], axis=0)]
        norms = lax.all_gather(norm_piece, "shard", axis=1, tiled=True).astype(f32)
        kinds = ("flat", "flat", "flat")
    plan_a = [(kinds[0], i * own, own, i * width, 0, count) for i in range(3)]
    plan_b = [(kinds[1], i * own, own, i * width, 0, count) for i in range(5)]
    plan_c = [(kinds[2], i * own, own, i * width, parts * own, count) for i in range(parts)]
    plan_c.append(("flat", 0, own_out, parts * width, 0, count))
    sems = pltpu.SemaphoreType.DMA
    square = 2 * row_count * width * width

    a1, q1, k1, v1 = by_rows(
        functools.partial(first_kernel, plan_a, len(set_a)), order, [x], norms, set_a,
        [(width, bf16)] * 4, False,
        [pltpu.VMEM((3, width, width), bf16), sems((3,))], 3 * square,
    )
    pairs = width // 128
    self_args = (q1, k1, v1, query_extra, unit_extra, self_windows, True)
    if ring:
        o1_low, log1_low = attend_forward(*self_args, (0, pairs // 2))
        ring_b.hop(o1_low)
        o1_high, log1_high = attend_forward(*self_args, (pairs // 2, pairs), [o1_low])
        ring_b.hop(o1_high)
        ring_b.hop()
        set_b = ring_b.finish()
    else:
        o1_low, log1_low = attend_forward(*self_args, (0, pairs // 2))
        o1_high, log1_high = attend_forward(*self_args, (pairs // 2, pairs))
    o1 = [o1_low, o1_high]
    r1, a2, q2, k2, v2 = by_rows(
        functools.partial(second_kernel, plan_b[:4], len(set_b), 2), order, o1 + [x, enc], norms, set_b,
        [(width, f32)] + [(width, bf16)] * 4, False,
        [pltpu.VMEM((4, width, width), bf16), sems((4,))], 4 * square,
    )
    o2, log2 = attend_forward(q2, k2, v2, query_extra, enc_extra, cross_windows, False, (0, pairs))
    out, a3, h, df, du, dr2, dc2, do2, terms_three = by_rows(
        functools.partial(third_kernel, plan_b[4:] + plan_c, len(set_b), len(set_c), 1), order, [o2, r1, cot], norms, set_b + set_c,
        [(width, bf16), (width, bf16), (hidden, bf16), (width, bf16), (hidden, bf16), (width, f32), (width, bf16), (width, bf16)], True,
        [
            pltpu.VMEM((width, width), bf16),
            pltpu.VMEM((parts, width, width), bf16),
            pltpu.VMEM((hidden, width), bf16),
            pltpu.VMEM((256, hidden), f32),
            sems((parts + 2,)),
        ],
        (2 + 4 * parts) * square,
    )

    cross_args = (q2, k2, v2, o2, do2, log2, enc_extra, cross_windows, False)
    if ring:
        ffn_set = ffn_terms(a3, du, h, df, count)
        ffn_set = lax.psum_scatter(ffn_set.reshape(-1, width), "shard", scatter_dimension=0, tiled=True)
    else:
        grad_in, grad_out = scatter_sum(weight_term(a3, du)), scatter_sum(weight_term(h, df))
    dq2, dk2, dv2 = attend_backward(*cross_args, (0, pairs))
    dr1, dc1, do1, terms_two = by_rows(
        functools.partial(fourth_kernel, plan_b[:2], len(set_b)), order, [dq2, r1, dr2], norms, set_b,
        [(width, f32), (width, bf16), (width, bf16)], True,
        [pltpu.VMEM((2, width, width), bf16), sems((2,))], 2 * square,
    )

    def enc_backward(after):
        return by_rows(
            functools.partial(enc_kernel, plan_b[2:4], len(set_b)), order, [dk2, dv2], norms, set_b,
            [(width, f32)], False,
            [pltpu.VMEM((2, width, width), bf16), sems((2,))], 2 * square, after,
        )[0]

    half = pairs // 2

    def self_backward(i, after):
        return attend_backward(
            q1, k1, v1, o1[i], do1, (log1_low, log1_high)[i], unit_extra, self_windows, True,
            (i * half, (i + 1) * half), i * half, after,
        )

    def fifth(groups, after, part=(0, 1), into=None):
        dq1, dk1, dv1 = ([g[i] for g in groups] for i in range(3))
        return by_rows(
            functools.partial(fifth_kernel, plan_a, len(set_a), len(groups)), order, dq1 + dk1 + dv1 + [x, dr1], norms, set_a,
            [(width, f32)], True,
            [pltpu.VMEM((3, width, width), bf16), sems((3,))], 3 * square // part[1], after, part=part, into=into,
        )

    if ring:
        groups = [self_backward(0, [])]
        groups.append(self_backward(1, [groups[0][0]]))
        mine, other = term_sets(
            rank, [tuple(o1), (a1,)],
            [(0, [(dc1, c)]) for c in range(2)] + [(1, [(g[i], 0)]) for i in range(3) for g in groups], count,
        )
        sums_a = RingSum(mine, over_cores(other, count), count, True)
        grad_x, terms_one = fifth(groups, [mine])
        last = sums_a.hop([grad_x])
        mine, other = term_sets(
            rank, [(o2,), (a2,), (enc,)],
            [(i, [(g, c)]) for i, g in ((0, dc2), (1, dq2), (2, dk2), (2, dv2)) for c in range(2)], count, last,
            [terms_one, terms_two, terms_three],
        )
        last = sums_a.hop([mine], [other])
        came = over_cores(sums_a.carried[0], count)
        grad_enc = enc_backward(last)
        keep, send = halve(rep, mine, came, [grad_enc])
        sums_b = RingSum(keep, swap_reps(send), count)
        last = sums_a.hop(sums_a.hop([keep]))
        ffn_set = over_rep(ffn_set + last[0][:1, :1] * 0)
        last = sums_b.hop(sums_b.hop(sums_b.hop(last)))
        sums_b.hop(last + [ffn_set])
        grad_a, grad_b = over_rep(sums_a.finish()), both_halves(rep, sums_b.finish())
        grad_in = jnp.concatenate([ffn_set[i * own : (i + 1) * own] for i in range(parts)], axis=1)
        grad_out = ffn_set[parts * own :]

        norm_sum = grad_b[8 * own : 8 * own + 8, :own_width]

        def columns(array, places):
            return jnp.concatenate([array[i * own : (i + 1) * own] for i in places], axis=1)

        grad_co, grad_cq, grad_ck, grad_cv = (columns(grad_b, (2 * w, 2 * w + 1)) for w in range(4))
        grad_so, grad_sq, grad_sk, grad_sv = (columns(grad_a, (2 * w, 2 * w + 1)) for w in range(4))
    else:
        grad_enc = enc_backward(())
        groups = [self_backward(i, ()) for i in range(2)]
        dq1, dk1, dv1 = (jnp.concatenate([g[i] for g in groups], axis=1) for i in range(3))
        grad_x, terms_one = fifth(groups, ())
        norm_sum = lax.psum(terms_one + terms_two + terms_three, ("rep", "shard"))
        norm_sum = lax.dynamic_slice_in_dim(norm_sum, lax.axis_index("shard") * own_width, own_width, 1)
        grad_co, grad_cq, grad_ck, grad_cv, grad_so, grad_sq, grad_sk, grad_sv = (
            scatter_sum(weight_term(a, b))
            for a, b in (
                (o2, dc2), (a2, dq2), (enc, dk2), (enc, dv2), (jnp.concatenate(o1, axis=1), dc1), (a1, dq1), (a1, dk1), (a1, dv1)
            )
        )
    return (
        out.reshape(tokens.shape),
        grad_x.reshape(tokens.shape),
        grad_enc.reshape(enc_states.shape),
        grad_sq,
        grad_sk,
        grad_sv,
        grad_so,
        grad_cq,
        grad_ck,
        grad_cv,
        grad_co,
        grad_in,
        grad_out,
        norm_sum[:4],
        norm_sum[4:],
    )


def solution(mesh):
    return jax.shard_map(
        body,
        mesh=mesh,
        in_specs=(
            P(("rep", "shard"), None, None),
            P(("rep", "shard"), None, None),
            P(("rep", "shard"), None),
            P(("rep", "shard"), None),
            P("shard", None),
            P("shard", None),
            P("shard", None),
            P("shard", None),
            P("shard", None),
            P("shard", None),
            P("shard", None),
            P("shard", None),
            P("shard", None),
            P("shard", None),
            P(None, "shard"),
            P(None, "shard"),
            P(("rep", "shard"), None, None),
        ),
        out_specs=(
            P(("rep", "shard"), None, None),
            P(("rep", "shard"), None, None),
            P(("rep", "shard"), None, None),
            P("shard", None),
            P("shard", None),
            P("shard", None),
            P("shard", None),
            P("shard", None),
            P("shard", None),
            P("shard", None),
            P("shard", None),
            P("shard", None),
            P("shard", None),
            P(None, "shard"),
            P(None, "shard"),
        ),
        check_vma=False,
    )
```
